32 devices in a mesh: gx: 8 (over z, y), gy: 4 (over x, core).
Axes of the slice: x: 2, y: 2, z: 4, core: 2. Of those that a mesh axis runs over, the one named last changes fastest.
Arguments:
- offsets: float32 [3, 16, 8, 1024], P(None, 'gx', 'gy'), as said below
- charges: float32 [16, 8, 1024], P('gx', 'gy'), may hold values from -0.08 to 0.08
Outputs:
- potential: float32 [16, 8, 1024], P('gx', 'gy')
The draws below stay inside these ranges and needn't reach their ends.
Inputs may be any that keep to these rules, and one draw needn't show every extreme that they name: `offsets`: particle p of a leaf lies in sub-cell (p // 4^2, (p // 4) % 4, p % 4) of the leaf's grid of 4^3 equal sub-cells, inside the middle half of that sub-cell along each dimension.
All inputs are finite; a program needn't handle non-finite values. Where the reference program divides by a largest or mean magnitude, that divisor is 1e-20 or more.
Results may differ from the reference program's by a relative error of at most 0.0003.
Values sent between devices are 32-bit elements; how exact they have to be, the bound alone decides.
No kernel may reach another device: no remote copies, remote signals or barrier semaphores. Data moves between devices by JAX's collectives and lax.ppermute only.
A program may use at most 192 MiB of HBM per device.

```python
import jax
import jax.numpy as jnp
from jax import lax

LZ = 16
SUB = 4
PPL = 64
NX = 16
NY = 8


def draw_offsets(key, part):
    jitter = jax.random.uniform(key, (3, NX, NY, LZ, PPL), jnp.float32)
    counter = jnp.arange(PPL, dtype=jnp.int32)
    cells = jnp.stack([counter // (SUB * SUB), counter // SUB % SUB, counter % SUB]).astype(jnp.float32)
    placed = (cells[:, None, None, None, :] + 0.25 + 0.5 * jitter) / SUB
    return placed.reshape(3, NX, NY, LZ * PPL)


def block_levels(key, dims, pieces, least, largest):
    def one(position, blocks):
        draws = jax.random.uniform(jax.random.fold_in(jax.random.fold_in(key, 6), position), (blocks,), jnp.float32, least / len(pieces), largest / len(pieces))
        return jnp.repeat(jnp.exp(draws), dims[position] // blocks).reshape((-1,) + (1,) * (len(dims) - position - 1))

    gain = one(*pieces[0])
    for cut in pieces[1:]:
        gain = gain * one(*cut)
    return gain


def noise(rng, extent, width, bound, pieces=(), kind=jnp.bfloat16):
    entries = jax.random.normal(rng, extent, jnp.float32) * width
    if len(pieces) > 0:
        entries = block_levels(rng, extent, pieces, -0.22, 0.18) * entries
    return jnp.clip(entries, min=-bound, max=bound).astype(kind)


def setup_inputs(seed: int = 0) -> dict:
    seeds = jax.random.split(jax.random.key(seed), 3)
    return {
        "offsets": draw_offsets(jax.random.fold_in(seeds[2], 71), 0),
        "charges": noise(seeds[1], (NX, NY, LZ * PPL), 0.01, 0.08, ((0, 8), (1, 4)), jnp.float32),
    }


highest = lax.Precision.HIGHEST

def cheb_points():
    return jnp.cos((2.0 * jnp.arange(4, dtype=jnp.float32) + 1.0) * jnp.pi / 8.0)

def interpolate(coords):
    points = cheb_points()
    first = points
    second = 2.0 * points * points - 1.0
    third = 4.0 * points * points * points - 3.0 * points
    value = coords[..., None]
    return 0.25 + 0.5 * (value * first + (2.0 * value * value - 1.0) * second + (4.0 * value * value * value - 3.0 * value) * third)

def node_grid():
    points = cheb_points()
    counter = jnp.arange(64, dtype=jnp.int32)
    return jnp.stack([points[counter // 16], points[counter // 4 % 4], points[counter % 4]], -1)

def child_grid():
    counter = jnp.arange(8, dtype=jnp.int32)
    return jnp.stack([counter // 4, counter // 2 % 2, counter % 2], -1).astype(jnp.float32)

def upward_matrix():
    points = cheb_points()
    halves = jnp.array([0.0, 1.0], dtype=jnp.float32)
    shifted = (points[None, :] + 2.0 * halves[:, None] - 1.0) / 2.0
    factor = interpolate(shifted)
    return jnp.einsum('xia,yjb,zkc->xyzijkabc', factor, factor, factor, precision=highest).reshape(512, 64)

def translation(offset):
    node_points = node_grid()
    child_corner = child_grid()
    box_offsets = 2.0 * offset[None, None, :] + child_corner[:, None, :] - child_corner[None, :, :]
    spread = (node_points[None, :, :] - node_points[:, None, :]) / 2.0
    separation = spread[None, :, None, :, :] - box_offsets[:, None, :, None, :]
    adjacent = (lax.optimization_barrier(jnp.max(jnp.abs(box_offsets), -1)) <= 1.0).astype(jnp.float32)[:, None, :, None]
    distance = jnp.sqrt(lax.optimization_barrier(jnp.sum(separation * separation, -1)))
    return ((1.0 - adjacent) / (distance + adjacent)).reshape(512, 512)

def offset_of(counter):
    return (jnp.stack([counter // 9, counter // 3 % 3, counter % 3]) - 1).astype(jnp.int32)

def translation_tables():

    def one_table(counter):
        return translation(offset_of(counter).astype(jnp.float32))
    return lax.map(one_table, jnp.arange(27, dtype=jnp.int32))

def to_parent(moments):
    size_x, size_y, size_z, _ = moments.shape
    moments = moments.reshape(size_x // 2, 2, size_y // 2, 2, size_z // 2, 2, 64)
    return moments.transpose(0, 2, 4, 1, 3, 5, 6).reshape(size_x // 2, size_y // 2, size_z // 2, 512)

def from_parent(moments):
    size_x, size_y, size_z, _ = moments.shape
    moments = moments.reshape(size_x, size_y, size_z, 2, 2, 2, 64)
    return moments.transpose(0, 3, 1, 4, 2, 5, 6).reshape(2 * size_x, 2 * size_y, 2 * size_z, 64)

def matmul(left, right):
    return jnp.dot(left, right, precision=highest, preferred_element_type=jnp.float32)

def coarsen(moments, upward):
    parents = to_parent(moments)
    return matmul(parents.reshape(-1, 512), upward).reshape(parents.shape[:3] + (64,))

def refine(local, upward):
    spread_out = matmul(local.reshape(-1, 64), upward.T).reshape(local.shape[:3] + (512,))
    return from_parent(spread_out)

def pad_one(moments):
    return jnp.pad(moments, ((1, 1), (1, 1), (1, 1), (0, 0)))

def far_translate(padded, scaling, tables):
    size_x, size_y, size_z = (padded.shape[0] - 2, padded.shape[1] - 2, padded.shape[2] - 2)

    def step_fn(running, inputs):
        counter, table = inputs
        offset = offset_of(counter)
        window_piece = lax.dynamic_slice(padded, (offset[0] + 1, offset[1] + 1, offset[2] + 1, jnp.int32(0)), (size_x, size_y, size_z, 512))
        return (running + matmul(window_piece.reshape(-1, 512), table), None)
    running, _ = lax.scan(step_fn, jnp.zeros((size_x * size_y * size_z, 512), jnp.float32), (jnp.arange(27, dtype=jnp.int32), tables))
    return (scaling * running).reshape(size_x, size_y, size_z, 512)

def dense_translate(targets, sources, weights):
    node_points = node_grid()
    spread = (node_points[:, None, :] - node_points[None, :, :]) / 2.0
    box_offsets = sources[None, :, :] - targets[:, None, :]
    separation = spread[None, :, None, :, :] - box_offsets[:, None, :, None, :]
    adjacent = (lax.optimization_barrier(jnp.max(jnp.abs(box_offsets), -1)) <= 1.0).astype(jnp.float32)[:, None, :, None]
    distance = jnp.sqrt(lax.optimization_barrier(jnp.sum(separation * separation, -1)))
    kernel = ((1.0 - adjacent) / (distance + adjacent)).reshape(targets.shape[0] * 64, sources.shape[0] * 64)
    return (0.125 * matmul(kernel, weights.reshape(-1))).reshape(targets.shape[0], 64)

def particle_basis(offsets):
    coords = 2.0 * offsets - 1.0
    along_x = interpolate(coords[0])
    along_y = interpolate(coords[1])
    along_z = interpolate(coords[2])
    product = along_x[..., :, None, None] * along_y[..., None, :, None] * along_z[..., None, None, :]
    return product.reshape(along_x.shape[:-1] + (64,))

def gather_moments(charges, interp_basis):
    return jnp.einsum('...p,...pm->...m', charges, interp_basis, precision=highest, preferred_element_type=jnp.float32)

def evaluate_local(interp_basis, local):
    return jnp.einsum('...pm,...m->...p', interp_basis, local, precision=highest, preferred_element_type=jnp.float32)

def near_field(targets, sources, weights):
    size_x, size_y, depth, count = (targets.shape[1], targets.shape[2], targets.shape[3], targets.shape[4])
    self_mask = jnp.concatenate([jnp.zeros((count, count), jnp.float32), jnp.eye(count, dtype=jnp.float32), jnp.zeros((count, count), jnp.float32)], 1)
    running = jnp.zeros((size_x, size_y, depth, count), jnp.float32)
    for step_x in range(3):
        for step_y in range(3):
            window = sources[:, step_x:step_x + size_x, step_y:step_y + size_y]
            stacked = jnp.concatenate([window[..., 0:depth, :], window[..., 1:depth + 1, :], window[..., 2:depth + 2, :]], -1)
            charge_win = weights[step_x:step_x + size_x, step_y:step_y + size_y]
            charge_win = jnp.concatenate([charge_win[..., 0:depth, :], charge_win[..., 1:depth + 1, :], charge_win[..., 2:depth + 2, :]], -1)
            squared = jnp.zeros((size_x, size_y, depth, count, 3 * count), jnp.float32)
            for comp in range(3):
                differ = targets[comp][..., :, None] - stacked[comp][..., None, :]
                squared = squared + differ * differ
            if step_x == 1 and step_y == 1:
                inverse = lax.rsqrt(squared + self_mask) * (1.0 - self_mask)
            else:
                inverse = lax.rsqrt(squared)
            running = running + lax.optimization_barrier(jnp.sum(inverse * charge_win[..., None, :], -1))
    return running

def reference(offsets, charges):
    upward = upward_matrix()
    tables = translation_tables()
    offsets_five = offsets.reshape(3, NX, NY, LZ, PPL)
    charge_four = charges.reshape(NX, NY, LZ, PPL)
    by_column = offsets_five.transpose(1, 0, 2, 3, 4)

    def column_moments(inputs):
        column_offsets, column_charges = inputs
        return gather_moments(column_charges, particle_basis(column_offsets))
    leaf_moments = lax.map(column_moments, (by_column, charge_four))
    first_moments = coarsen(leaf_moments, upward)
    second_moments = coarsen(first_moments, upward)
    third_moments = coarsen(second_moments, upward)
    leaf_far = from_parent(far_translate(pad_one(to_parent(leaf_moments)), 1.0, tables))
    first_far = from_parent(far_translate(pad_one(to_parent(first_moments)), 0.5, tables))
    second_far = from_parent(far_translate(pad_one(to_parent(second_moments)), 0.25, tables))
    boxes_x, boxes_y, boxes_z = (NX // 8, NY // 8, LZ // 8)
    counter = jnp.arange(boxes_x * boxes_y * boxes_z, dtype=jnp.int32)
    sources = jnp.stack([counter // (boxes_y * boxes_z), counter // boxes_z % boxes_y, counter % boxes_z], -1).astype(jnp.float32)
    flat_third = third_moments.reshape(-1, 64)

    def top_row(column):
        inner = jnp.arange(boxes_y * boxes_z, dtype=jnp.int32)
        targets = jnp.stack([jnp.full((boxes_y * boxes_z,), column, jnp.int32), inner // boxes_z, inner % boxes_z], -1).astype(jnp.float32)
        return dense_translate(targets, sources, flat_third)
    top_far = lax.map(top_row, jnp.arange(boxes_x, dtype=jnp.int32)).reshape(boxes_x, boxes_y, boxes_z, 64)
    second_local = refine(top_far, upward) + second_far
    first_local = refine(second_local, upward) + first_far
    leaf_local = refine(first_local, upward) + leaf_far

    def column_far(inputs):
        column_offsets, column_local = inputs
        return evaluate_local(particle_basis(column_offsets), column_local)
    far_potential = lax.map(column_far, (by_column, leaf_local))
    padded = jnp.pad(offsets_five, ((0, 0), (1, 1), (1, 1), (1, 1), (0, 0)))
    grid_x = jnp.arange(-1, NX + 1, dtype=jnp.int32).astype(jnp.float32)
    grid_y = jnp.arange(-1, NY + 1, dtype=jnp.int32).astype(jnp.float32)
    grid_z = jnp.arange(-1, LZ + 1, dtype=jnp.int32).astype(jnp.float32)
    positions = jnp.stack([padded[0] + grid_x[:, None, None, None], padded[1] + grid_y[None, :, None, None], padded[2] + grid_z[None, None, :, None]])
    charge_pad = jnp.pad(charge_four, ((1, 1), (1, 1), (1, 1), (0, 0)))
    targets_all = positions[:, 1:-1, 1:-1, 1:-1]

    def near_column(column):
        target_slice = lax.dynamic_slice_in_dim(targets_all, column, 1, 1)
        source_slice = lax.dynamic_slice_in_dim(positions, column, 3, 1)
        charge_slice = lax.dynamic_slice_in_dim(charge_pad, column, 3, 0)
        return near_field(target_slice, source_slice, charge_slice)[0]
    near_potential = lax.map(near_column, jnp.arange(NX, dtype=jnp.int32))
    return (far_potential + near_potential).reshape(NX, NY, LZ * PPL)
```

```python
import itertools

import jax
import jax.numpy as jnp
import ml_dtypes
import numpy as np
from jax import lax
from jax.experimental import pallas as pl
from jax.experimental.pallas import tpu as pltpu
from jax.sharding import PartitionSpec as P

F32 = jnp.float32
BF16 = jnp.bfloat16
MIB = 1 << 20

CX = 2
CY = 2
LZ = 16
ROWS = 8
FEATURES = 32
VMEM = pl.BlockSpec(memory_space=pltpu.VMEM)
HBM = pl.BlockSpec(memory_space=pl.ANY)


def nodes_1d():
    return np.cos((2.0 * np.arange(4) + 1.0) * np.pi / 8.0)


def cheb_terms(value):
    return value, 2.0 * value * value - 1.0, 4.0 * value**3 - 3.0 * value


def node_weights():
    return [[0.5 * term for term in cheb_terms(point)] for point in nodes_1d()]


def node_grid():
    points = nodes_1d()
    counter = np.arange(64)
    return np.stack([points[counter // 16], points[counter // 4 % 4], points[counter % 4]], -1)


def split_two(table):
    high = table.astype(np.float32).astype(ml_dtypes.bfloat16)
    low = (table - high.astype(np.float64)).astype(np.float32).astype(ml_dtypes.bfloat16)
    return high, low


def upward_tensor():
    points = nodes_1d()
    shifted = (points[None, :] + 2.0 * np.arange(2)[:, None] - 1.0) / 2.0
    factor = 0.25 + 0.0 * shifted[..., None]
    for of_value, of_node in zip(cheb_terms(shifted), cheb_terms(points)):
        factor = factor + 0.5 * of_value[..., None] * of_node
    full = np.einsum("xia,yjb,zkc->xyzijkabc", factor, factor, factor)
    return full.reshape(2, 2, 2, 64, 64)


def inverse_distance(offset):
    grid = node_grid()
    spread = (grid[None, :, :] - grid[:, None, :]) / 2.0 - np.asarray(offset, np.float64)
    return 1.0 / np.sqrt(np.sum(spread * spread, -1))


def adjacent(offset):
    return max(abs(int(step)) for step in offset) <= 1


def canonical_tiles():
    return [
        (cx, cy, cz)
        for cx in range(2)
        for cy in range(2)
        for cz in range(4)
        if not (cx == 0 and cy == 0 and cz <= 1)
    ]


def translation_tiles():
    tiles = []
    for cx, cy, cz in canonical_tiles():
        tile = np.zeros((4, 64, 4, 64))
        for source in range(4):
            for target in range(4):
                offset = (
                    2 * cx + source // 2 - target // 2,
                    2 * cy + source % 2 - target % 2,
                    cz,
                )
                if not adjacent(offset):
                    tile[source, :, target, :] = inverse_distance(offset)
        tiles.append(tile.reshape(256, 256))
    return np.stack(split_two(np.stack(tiles)), 1)


def reflection_matrix(flip_x, flip_y, flip_z):
    index = np.arange(256)
    hx, hy, a, b, c = index // 128, index // 64 % 2, index // 16 % 4, index // 4 % 4, index % 4
    if flip_x:
        hx, a = 1 - hx, 3 - a
    if flip_y:
        hy, b = 1 - hy, 3 - b
    if flip_z:
        c = 3 - c
    matrix = np.zeros((256, 256), np.float32)
    matrix[hx * 128 + hy * 64 + a * 16 + b * 4 + c, index] = 1.0
    return matrix


def reflection_tables():
    pairs = [
        np.concatenate([reflection_matrix(fx, fy, 0), reflection_matrix(fx, fy, 1)], 1)
        for fx in range(2)
        for fy in range(2)
    ]
    return np.stack(pairs).astype(ml_dtypes.bfloat16)


def up_tables():
    upward = upward_tensor()
    table = upward.transpose(0, 1, 3, 2, 4).reshape(256, 128)
    return np.stack(split_two(table))


def down_table():
    upward = upward_tensor()
    table = upward.transpose(4, 2, 0, 1, 3).reshape(64, 512)
    high, low = split_two(table)
    return np.concatenate([high, high, low, np.zeros_like(low)], 0)


def top_tables(boxes_x, boxes_y):
    offsets = range(-(boxes_x - 1), boxes_x), range(-(boxes_y - 1), boxes_y)
    table = np.zeros((len(offsets[0]), len(offsets[1]), 2, 64, 2, 64))
    for (ix, dx), (iy, dy) in itertools.product(enumerate(offsets[0]), enumerate(offsets[1])):
        for source, target in itertools.product(range(2), range(2)):
            offset = (dx, dy, source - target)
            if not adjacent(offset):
                table[ix, iy, source, :, target, :] = 0.125 * inverse_distance(offset)
    return np.stack(split_two(table.reshape(len(offsets[0]), len(offsets[1]), 128, 128)), 2)


def leaf_segments():
    table = np.zeros((LZ, LZ * 64), np.float32)
    for leaf in range(LZ):
        table[leaf, leaf * 64 : leaf * 64 + 64] = 1.0
    return table.astype(ml_dtypes.bfloat16)


def halves(value):
    high = value.astype(BF16)
    return high, (value - high.astype(F32)).astype(BF16)


def dot(left, right):
    return jnp.dot(left, right, preferred_element_type=F32)


def dot_three(value, high_table, low_table):
    rows = value.shape[0]
    high, low = halves(value)
    both = dot(jnp.concatenate([high, low], 0), high_table)
    return both[:rows] + both[rows:] + dot(high, low_table)


def lanes(shape):
    return lax.broadcasted_iota(jnp.int32, shape, len(shape) - 1)


def sublanes(shape):
    return lax.broadcasted_iota(jnp.int32, shape, len(shape) - 2)


def lane_flip(value):
    return pltpu.roll(value, 64, 1)


def weight_rows(pattern):
    weights = node_weights()
    index = sublanes((8, 128))
    rows = []
    for term in range(3):
        row = jnp.full((8, 128), weights[pattern(0)][term], F32)
        for sub in range(1, 8):
            row = jnp.where(index == sub, weights[pattern(sub)][term], row)
        rows.append(row)
    return rows


def basis_rows():
    return (
        weight_rows(lambda sub: sub // 4),
        weight_rows(lambda sub: 2 + sub // 4),
        weight_rows(lambda sub: sub % 4),
    )


def basis_tile(row_x, row_y, row_z, scale, tables):
    y_low, y_high, z_all = tables
    wide = [jnp.broadcast_to(2.0 * row - 1.0, (8, 128)) for row in (row_x, row_y, row_z)]
    terms = [cheb_terms(value) for value in wide]

    def mix(weights, term):
        return 0.25 + (weights[0] * term[0] + weights[1] * term[1] + weights[2] * term[2])

    along_z = mix(z_all, terms[2])
    pair = mix(y_low, terms[1]) * along_z, mix(y_high, terms[1]) * along_z
    tiles = []
    for weights in node_weights():
        along_x = mix(weights, terms[0])
        if scale is not None:
            along_x = along_x * scale
        tiles += [along_x * pair[0], along_x * pair[1]]
    return tiles


def three_pieces(value):
    first = value.astype(BF16).astype(F32)
    rest = value - first
    second = rest.astype(BF16).astype(F32)
    return first, second, rest - second


def source_features(coords):
    rows = []
    total = None
    for coord in coords:
        one, two, three = three_pieces(coord)
        rows += [one, two, one, two, three, one]
        total = coord * coord if total is None else total + coord * coord
    unit = jnp.ones_like(coords[0])
    return rows + [unit] * 3 + list(three_pieces(total)) + [jnp.zeros_like(unit)] * 8


def target_features(coords):
    rows = []
    total = None
    for coord in coords:
        one, two, three = three_pieces(-2.0 * coord)
        rows += [one, one, two, two, one, three]
        total = coord * coord if total is None else total + coord * coord
    unit = jnp.ones_like(coords[0])
    return rows + list(three_pieces(total)) + [unit] * 3 + [jnp.zeros_like(unit)] * 8


def store_features(rows, wide_ref, group):
    for row, value in enumerate(rows):
        wide_ref[group, pl.ds(row, ROWS, stride=FEATURES), :] = value


class Near:
    def __init__(self, raw, wide_ref, source_ref, charge_ref, target_ref):
        self.raw = raw
        self.wide_ref = wide_ref
        self.source_ref = source_ref
        self.charge_ref = charge_ref
        self.target_ref = target_ref
        self.groups = 0
        self.charges = 0
        self.upper = lanes((ROWS, 128)) >= 64
        self.row = sublanes((ROWS, 128))

    def place(self, x, y):
        return self.raw(0, x, y) + (x - 2.0), self.raw(1, x, y) + (y - 2.0)

    def targets(self):
        for ab in range(4):
            x, y = ab // 2 + 1, ab % 2 + 1
            coords = self.place(x, y)
            along_z = self.raw(2, x, y) + jnp.where(self.upper, 0.0, -1.0)
            store_features(target_features(coords + (along_z,)), self.wide_ref, ab)
        for ab in range(4):
            for j in range(ROWS):
                block = self.wide_ref[ab, FEATURES * j : FEATURES * (j + 1), :]
                self.target_ref[ab, j] = block.T.astype(BF16)

    def add_group(self, coords):
        store_features(source_features(coords), self.wide_ref, self.groups)
        self.groups += 1
        return self.groups - 1

    def add_charge(self, charge):
        self.charge_ref[self.charges] = charge
        self.charges += 1
        return self.charges - 1

    def main(self, x, y):
        along_z = self.raw(2, x, y) + jnp.where(self.upper, 0.0, -1.0)
        group = self.add_group(self.place(x, y) + (along_z,))
        return group, self.add_charge(self.raw(3, x, y))

    def outer(self, first, second, side, keep=None):
        place = [self.place(*first), self.place(*second)]

        def merge(one, two):
            if side == 0:
                value = jnp.where(self.upper, two, lane_flip(one))
                return pltpu.roll(value, 1, 0)
            value = jnp.where(self.upper, lane_flip(two), one)
            return pltpu.roll(value, ROWS - 1, 0)

        along_z = merge(self.raw(2, *first), self.raw(2, *second)) + (-2.0 if side == 0 else 1.0)
        coords = (merge(place[0][0], place[1][0]), merge(place[0][1], place[1][1]), along_z)
        charge = merge(self.raw(3, *first), self.raw(3, *second))
        charge = jnp.where(self.row == (0 if side == 0 else ROWS - 1), 0.0, charge)
        group = self.add_group(coords)
        if keep is None:
            return group, self.add_charge(charge)
        low = self.add_charge(jnp.where(self.upper, 0.0, charge))
        high = self.add_charge(jnp.where(self.upper, charge, 0.0))
        return (group, low), (group, high)

    def convert(self):
        for group in range(self.groups):
            for j in range(ROWS):
                block = self.wide_ref[group, FEATURES * j : FEATURES * (j + 1), :]
                self.source_ref[group, j] = block.astype(BF16)

    def run(self, plan, emit):
        eye = sublanes((128, 128)) == lanes((128, 128))

        def pairs(targets, tiles, j, own, total):
            if not tiles:
                return total
            block = jnp.concatenate([self.source_ref[group, j] for group, _ in tiles], 1)
            squared = dot(targets, block)
            for position, (group, charge) in enumerate(tiles):
                inverse = lax.rsqrt(squared[:, 128 * position : 128 * position + 128])
                if group == own:
                    inverse = jnp.where(eye, 0.0, inverse)
                total = total + inverse * self.charge_ref[charge, pl.ds(j, 1), :]
            return total

        def step(j, carry):
            for ab in range(4):
                mains, below, above, own = plan[ab]
                targets = self.target_ref[ab, j]
                total = pairs(targets, mains, j, own, jnp.zeros((128, 128), F32))
                lower = pairs(targets[:64], below, j, None, total[:64])
                higher = pairs(targets[64:], above, j, None, total[64:])
                total = jnp.concatenate([lower, higher], 0)
                emit(ab, j, jnp.sum(total.T, 0, keepdims=True))
            return carry

        lax.fori_loop(0, ROWS, step, 0)


def plan_own(near):
    mains = {(x, y): near.main(x, y) for x in (1, 2) for y in (1, 2)}
    outer = [[near.outer((x, 1), (x, 2), side) for x in (1, 2)] for side in range(2)]
    plan = []
    for ab in range(4):
        own = mains[(ab // 2 + 1, ab % 2 + 1)][0]
        plan.append((list(mains.values()), outer[0], outer[1], own))
    return plan


def plan_beside_y(near):
    plan = []
    sides = []
    for y in (0, 3):
        mains = [near.main(x, y) for x in (1, 2)]
        outer = [[near.outer((1, y), (2, y), side)] for side in range(2)]
        sides.append((mains, outer[0], outer[1], None))
    for ab in range(4):
        plan.append(sides[ab % 2])
    return plan


def plan_beside_x(near):
    plan = []
    for x in (0, 3):
        mains = [near.main(x, y) for y in range(4)]
        middle = [near.outer((x, 1), (x, 2), side) for side in range(2)]
        ends = [near.outer((x, 0), (x, 3), side, keep=True) for side in range(2)]
        for b in range(2):
            plan.append(
                (mains[b : b + 3], [middle[0], ends[0][b]], [middle[1], ends[1][b]], None)
            )
    return plan


def join_plans(plans):
    joined = []
    for ab in range(4):
        parts = [plan[ab] for plan in plans]
        own = next((part[3] for part in parts if part[3] is not None), None)
        joined.append(tuple(sum((part[k] for part in parts), []) for k in range(3)) + (own,))
    return joined


def near_scratch(groups, charges):
    return [
        pltpu.VMEM((groups, ROWS * FEATURES, 128), F32),
        pltpu.VMEM((groups, ROWS, FEATURES, 128), BF16),
        pltpu.VMEM((charges, ROWS, 128), F32),
        pltpu.VMEM((4, ROWS, 128, FEATURES), BF16),
    ]


ONE_ROWS = 8
LEAF_ROWS = 32
EDGE_ROWS = 64


def moments_kernel(offsets, charges, segments, up, own_part, to_low, to_high, basis, sums):
    index_y = lax.axis_index("gy")
    tables = basis_rows()
    for x in range(CX):
        for y in range(CY):
            for j in range(ROWS):
                span = slice(128 * j, 128 * j + 128)
                rows = [offsets[c, x, y : y + 1, span] for c in range(3)]
                charge = charges[x, y : y + 1, span]
                for c, row in enumerate(rows + [charge]):
                    own_part[c, x, y, j : j + 1, :] = row
                    edge = ONE_ROWS + LEAF_ROWS + (c * CX + x) * ROWS + j
                    target = to_low if y == 0 else to_high
                    target[edge : edge + 1, :] = row
                tiles = basis_tile(*rows, charge, tables)
                for k in range(4):
                    pair = jnp.concatenate(tiles[2 * k : 2 * k + 2], 0)
                    high, low = halves(pair)
                    first = (x * CY + y) * 64 + 16 * k
                    basis[0, first : first + 16, span] = high
                    basis[1, first : first + 16, span] = low
    contract = (((1,), (1,)), ((), ()))
    leaf = lax.dot_general(segments[...], basis[0], contract, preferred_element_type=F32)
    leaf = leaf + lax.dot_general(segments[...], basis[1], contract, preferred_element_type=F32)
    sums[...] = dot_three(leaf, up[0], up[1])
    first = sums[pl.ds(0, 8, stride=2), :] + lane_flip(sums[pl.ds(1, 8, stride=2), :])
    first = jnp.where(lanes((8, 128)) < 64, first, 0.0)
    first = jnp.where(lax.rem(index_y, 2) == 1, lane_flip(first), first)
    for target in (to_low, to_high):
        target[0:8, :] = first
        target[8:24, :] = leaf[:, :128]
        target[24:40, :] = leaf[:, 128:]


def moments_call(offsets, charges, segments, up):
    payload = jax.ShapeDtypeStruct((ONE_ROWS + LEAF_ROWS + EDGE_ROWS, 128), F32)
    return pl.pallas_call(
        moments_kernel,
        out_shape=(jax.ShapeDtypeStruct((4, CX, CY, ROWS, 128), F32), payload, payload),
        in_specs=[VMEM] * 4,
        out_specs=(VMEM,) * 3,
        scratch_shapes=[pltpu.VMEM((2, 256, 1024), BF16), pltpu.VMEM((16, 128), F32)],
        compiler_params=pltpu.CompilerParams(vmem_limit_bytes=16 * MIB),
        cost_estimate=pl.CostEstimate(flops=10_000_000, bytes_accessed=300_000, transcendentals=0),
        name="moments",
    )(offsets, charges, segments, up)


PART_ROWS = 4 * 4 * ROWS


def row_kernel(count_y, own_part, to_low, from_low, from_high, *rest):
    others, (out_low, out_high) = rest[:-2], rest[-2:]
    index_y = lax.axis_index("gy")
    ones = count_y // 2 * 8
    has_low = index_y > 0
    has_high = index_y < count_y - 1

    out_low[0:ones, :] = jnp.zeros((ones, 128), F32)
    received = {0: to_low, 1: from_low, count_y - 1: from_high}
    for shift, ref in zip(range(2, count_y - 1), others):
        received[shift] = ref
    for shift, ref in received.items():
        source = lax.rem(index_y - shift + count_y, count_y)
        place = pl.ds(pl.multiple_of(source // 2 * 8, 8), 8)
        out_low[place, :] = out_low[place, :] + ref[0:8, :]
    for piece, (ref, keep) in enumerate(((from_low, has_low), (to_low, None), (from_high, has_high))):
        block = ref[ONE_ROWS : ONE_ROWS + LEAF_ROWS, :]
        if keep is not None:
            block = jnp.where(keep, block, 0.0)
        out_low[ones + LEAF_ROWS * piece : ones + LEAF_ROWS * (piece + 1), :] = block
    shared = ones + 3 * LEAF_ROWS
    out_high[0:shared, :] = out_low[0:shared, :]
    for x, out in enumerate((out_low, out_high)):
        for c in range(4):
            edge = ONE_ROWS + LEAF_ROWS + (c * CX + x) * ROWS
            columns = [
                from_low[edge : edge + ROWS, :],
                own_part[c, x, 0],
                own_part[c, x, 1],
                from_high[edge : edge + ROWS, :],
            ]
            if c == 3:
                columns[0] = jnp.where(has_low, columns[0], 0.0)
                columns[3] = jnp.where(has_high, columns[3], 0.0)
            for y, column in enumerate(columns):
                row = shared + (c * 4 + y) * ROWS
                out[row : row + ROWS, :] = column


def row_call(count_y, own_part, to_low, from_low, from_high, others):
    rows = count_y // 2 * 8 + 3 * LEAF_ROWS + PART_ROWS
    payload = jax.ShapeDtypeStruct((rows, 128), F32)
    operands = (own_part, to_low, from_low, from_high, *others)
    return pl.pallas_call(
        lambda *refs: row_kernel(count_y, *refs),
        out_shape=(payload, payload),
        in_specs=[VMEM] * len(operands),
        out_specs=(VMEM,) * 2,
        compiler_params=pltpu.CompilerParams(vmem_limit_bytes=16 * MIB),
        cost_estimate=pl.CostEstimate(flops=100_000, bytes_accessed=500_000, transcendentals=0),
        name="row",
    )(*operands)


def finish_kernel(count_x, count_y, refs):
    (own_low, own_high, from_low, from_high), refs = refs[:4], refs[4:]
    others, refs = refs[: count_x - 3], refs[count_x - 3 :]
    segments, up, down, flips, top, tiles_hbm, refs = *refs[:6], refs[6:]
    out, refs = refs[0], refs[1:]
    wide_ref, source_ref, charge_ref, target_ref, refs = *refs[:4], refs[4:]
    near_rows, far_rows, tiles, level_one, level_two, boxes, flipped, sums, local, semaphore = refs

    index_x, index_y = lax.axis_index("gx"), lax.axis_index("gy")
    pairs_y = count_y // 2
    ones = pairs_y * 8
    shared = ones + 3 * LEAF_ROWS
    has_low = index_x > 0
    has_high = index_x < count_x - 1
    fetch = pltpu.make_async_copy(tiles_hbm, tiles, semaphore)
    fetch.start()

    columns = (from_low, own_low, own_high, from_high)

    def raw(c, x, y):
        row = shared + (c * 4 + y) * ROWS
        value = columns[x][row : row + ROWS, :]
        if c == 3 and x in (0, 3):
            value = jnp.where(has_low if x == 0 else has_high, value, 0.0)
        return value

    near = Near(raw, wide_ref, source_ref, charge_ref, target_ref)
    near.targets()
    plan = join_plans([plan_own(near), plan_beside_y(near), plan_beside_x(near)])
    near.convert()

    def emit(ab, j, row):
        near_rows[ab, pl.ds(j, 1), :] = row

    near.run(plan, emit)

    level_one[...] = jnp.zeros_like(level_one)
    level_two[...] = jnp.zeros_like(level_two)
    received = {0: own_low, 1: from_low, count_x - 1: from_high}
    for shift, ref in zip(range(2, count_x - 1), others):
        received[shift] = ref
    for shift, ref in received.items():
        source = lax.rem(index_x - shift + count_x, count_x)
        for pair in range(pairs_y):
            level_one[source + 2, pair + 1] = ref[8 * pair : 8 * pair + 8, :]
    half_x = count_x // 2
    children = jnp.concatenate(
        [
            jnp.concatenate([level_one[2 * x + 2, y + 1], level_one[2 * x + 3, y + 1]], 1)
            for x in range(half_x)
            for y in range(pairs_y)
        ],
        0,
    )
    below = half_x * pairs_y * 8
    low_lanes = lanes((4, 128)) < 64
    sums[0:below, :] = dot_three(children, up[0], up[1])
    for x in range(half_x):
        for y in range(pairs_y):
            row = (x * pairs_y + y) * 8
            even = sums[pl.ds(row, 4, stride=2), :]
            odd = sums[pl.ds(row + 1, 4, stride=2), :]
            level_two[x + 2, y + 2, 0:4] = jnp.where(low_lanes, even + lane_flip(odd), 0.0)

    def second_group(group_x, group_y):
        return jnp.concatenate(
            [
                level_two[2 * group_x + h + 2, 2 * group_y + 2]
                + lane_flip(level_two[2 * group_x + h + 2, 2 * group_y + 3])
                for h in range(2)
            ],
            1,
        )

    quarter_x, quarter_y = index_x // 4, index_y // 4
    tops = [(x, y) for x in range(count_x // 4) for y in range(count_y // 4)]
    stacked = jnp.concatenate([second_group(x, y) for x, y in tops], 0)
    if stacked.shape[0] % 16 != 0:
        stacked = jnp.concatenate([stacked, jnp.zeros((8, 256), F32)], 0)
    sums[0 : stacked.shape[0], :] = dot_three(stacked, up[0], up[1])
    top_far = jnp.zeros((16, 128), F32)
    for position, (x, y) in enumerate(tops):
        even = sums[pl.ds(8 * position, 2, stride=2), :]
        odd = sums[pl.ds(8 * position + 1, 2, stride=2), :]
        third = jnp.where(lanes((2, 128)) < 64, even + lane_flip(odd), 0.0)
        third = third[0:1] + lane_flip(third)[1:2]
        table = top.at[x - quarter_x + count_x // 4 - 1, y - quarter_y + count_y // 4 - 1]
        top_far = top_far + dot_three(jnp.broadcast_to(third, (16, 128)), table[0], table[1])

    boxes[...] = jnp.zeros_like(boxes)
    leaf_refs = {-1: from_low, 0: own_low, 1: from_high}
    for gx in (-1, 0, 1):
        for gy in (-1, 0, 1):
            start = ones + LEAF_ROWS * (gy + 1)
            for h in range(2):
                block = leaf_refs[gx][start + 16 * h : start + 16 * h + 16, :]
                if gx != 0:
                    block = jnp.where(has_low if gx < 0 else has_high, block, 0.0)
                span = slice(128 * h, 128 * h + 128)
                boxes[8:24, span] = block
                boxes[32:40, span] = level_one[
                    2 * (index_x // 2 + gx) + h + 2, index_y // 2 + gy + 1
                ]
            boxes[48:56, :] = second_group(quarter_x + gx, quarter_y + gy)
            high, low = halves(boxes[...])
            table = flips[2 * (gx < 0) + (gy < 0)]
            mixed = dot(jnp.concatenate([high, low], 0), table)
            group = 3 * (gx + 1) + gy + 1
            for z in range(2):
                flipped[group, z, 0] = mixed[:64, 256 * z : 256 * z + 256]
                flipped[group, z, 1] = mixed[64:, 256 * z : 256 * z + 256]

    fetch.wait()
    odd_row = lax.rem(sublanes((32, 256)), 2) == 1
    totals = {}
    for position, (cx, cy, cz) in enumerate(canonical_tiles()):
        entries = [
            (gx, gy, dz)
            for gx in sorted({cx, -cx})
            for gy in sorted({cy, -cy})
            for dz in sorted({cz, -cz})
        ]
        pieces = [[], []]
        for gx, gy, dz in entries:
            group = 3 * (gx + 1) + gy + 1
            for part in range(2):
                view = flipped.at[group, int(dz < 0), part]
                block = jnp.concatenate(
                    [view[8 + dz : 24 + dz, :], view[32 + dz : 40 + dz, :], view[48 + dz : 56 + dz, :]],
                    0,
                )
                if abs(dz) == 3:
                    block = jnp.where(odd_row if dz < 0 else ~odd_row, block, 0.0)
                pieces[part].append(block.astype(BF16))
        rows = 32 * len(entries)
        both = dot(jnp.concatenate(pieces[0] + pieces[1], 0), tiles[position, 0])
        result = both[:rows] + both[rows:] + dot(jnp.concatenate(pieces[0], 0), tiles[position, 1])
        for order, (gx, gy, dz) in enumerate(entries):
            key = (int(gx < 0), int(gy < 0), int(dz < 0))
            piece = result[32 * order : 32 * order + 32]
            totals[key] = totals[key] + piece if key in totals else piece
    far = None
    for (fx, fy, fz), total in totals.items():
        if (fx, fy, fz) != (0, 0, 0):
            high, low = halves(total)
            table = flips[2 * fx + fy, :, 256 * fz : 256 * fz + 256]
            both = dot(jnp.concatenate([high, low], 0), table)
            total = both[:32] + both[32:]
        far = total if far is None else far + total

    def select(block, hx, hy):
        tile = jnp.where(hx == 1, block[:, 128:256], block[:, 0:128])
        return jnp.where(hy == 1, lane_flip(tile), tile)

    def refine(parent):
        keep = lanes((16, 128)) < 64
        parent = jnp.where(keep, parent, 0.0)
        high = parent.astype(BF16).astype(F32)
        low = parent - high
        left = jnp.concatenate([high + lane_flip(low), high], 1).astype(BF16)
        spread = dot(left, down[...])
        for half in range(2):
            for h in range(2):
                span = slice(256 * half + 128 * h, 256 * half + 128 * h + 128)
                local[h, pl.ds(half, 16, stride=2), :] = spread[:, span]
        return jnp.concatenate([local[0], local[1]], 1)

    top_local = jnp.where(
        sublanes((16, 128)) == 0, top_far, jnp.where(sublanes((16, 128)) == 1, lane_flip(top_far), 0.0)
    )
    children_far = refine(top_local)
    half_index_x, half_index_y = index_x // 2, index_y // 2
    second = select(children_far[0:8], lax.rem(half_index_x, 2), lax.rem(half_index_y, 2))
    second = second + 0.25 * select(far[24:32], lax.rem(half_index_x, 2), lax.rem(half_index_y, 2))
    zeros = jnp.zeros((8, 128), F32)
    children_far = refine(jnp.concatenate([second, zeros], 0))
    first = select(children_far[0:8], lax.rem(index_x, 2), lax.rem(index_y, 2))
    first = first + 0.5 * select(far[16:24], lax.rem(index_x, 2), lax.rem(index_y, 2))
    leaf = refine(jnp.concatenate([first, zeros], 0))[0:16] + far[0:16]

    one, two = halves(leaf)
    turned = jnp.concatenate([one.astype(F32), two.astype(F32)], 0).T.astype(BF16)
    table = jnp.concatenate([segments[...], segments[...]], 0)
    tables = basis_rows()
    for x in range(CX):
        for y in range(CY):
            column = x * CY + y
            spread = dot(turned[64 * column : 64 * column + 64], table)
            for j in range(ROWS):
                span = slice(128 * j, 128 * j + 128)
                rows = [raw(c, x + 1, y + 1)[j : j + 1] for c in range(3)]
                basis = basis_tile(*rows, None, tables)
                total = None
                for k in range(8):
                    term = basis[k] * spread[8 * k : 8 * k + 8, span]
                    total = term if total is None else total + term
                value = jnp.sum(total, 0, keepdims=True) + near_rows[column, j : j + 1, :]
                out[x, y : y + 1, span] = value


def finish_call(count_x, count_y, payloads, others, constants):
    segments, up, down, flips, top, tiles = constants
    operands = (*payloads, *others, segments, up, down, flips, top, tiles)
    half_x, half_y = count_x // 2, count_y // 2
    scratch = near_scratch(32, 36) + [
        pltpu.VMEM((4, ROWS, 128), F32),
        pltpu.VMEM((4, ROWS, 128), F32),
        pltpu.VMEM(tiles.shape, BF16),
        pltpu.VMEM((count_x + 4, half_y + 2, 8, 128), F32),
        pltpu.VMEM((half_x + 4, half_y + 4, 8, 128), F32),
        pltpu.VMEM((64, 256), F32),
        pltpu.VMEM((9, 2, 2, 64, 256), F32),
        pltpu.VMEM((max(16, half_x * half_y * 8), 128), F32),
        pltpu.VMEM((2, 32, 128), F32),
        pltpu.SemaphoreType.DMA,
    ]
    return pl.pallas_call(
        lambda *refs: finish_kernel(count_x, count_y, refs),
        out_shape=jax.ShapeDtypeStruct((CX, CY, LZ * 64), F32),
        in_specs=[VMEM] * (len(operands) - 1) + [HBM],
        out_specs=VMEM,
        scratch_shapes=scratch,
        compiler_params=pltpu.CompilerParams(vmem_limit_bytes=56 * MIB),
        name="finish",
    )(*operands)


def shift_ring(value, axis, shift):
    count = lax.axis_size(axis)
    return lax.ppermute(value, axis, [(i, (i + shift) % count) for i in range(count)])


def solution(mesh):
    count_x, count_y = mesh.shape["gx"], mesh.shape["gy"]
    segments, up, down, flips = leaf_segments(), up_tables(), down_table(), reflection_tables()
    top, tiles = top_tables(count_x // 4, count_y // 4), translation_tiles()

    def body(offsets, charges):
        constants = [jnp.asarray(table) for table in (segments, up, down, flips, top, tiles)]
        own_part, to_low, to_high = moments_call(offsets, charges, constants[0], constants[1])
        from_low = shift_ring(to_high, "gy", 1)
        from_high = shift_ring(to_low, "gy", count_y - 1)
        own_one = to_low[:ONE_ROWS]
        others = [shift_ring(own_one, "gy", shift) for shift in range(2, count_y - 1)]
        row_low, row_high = row_call(count_y, own_part, to_low, from_low, from_high, others)
        next_low = shift_ring(row_high, "gx", 1)
        next_high = shift_ring(row_low, "gx", count_x - 1)
        row_one = row_low[: count_y // 2 * 8]
        others = [shift_ring(row_one, "gx", shift) for shift in range(2, count_x - 1)]
        payloads = (row_low, row_high, next_low, next_high)
        return finish_call(count_x, count_y, payloads, others, constants)

    in_specs = (P(None, "gx", "gy", None), P("gx", "gy", None))
    out_specs = P("gx", "gy", None)
    return jax.shard_map(body, mesh=mesh, in_specs=in_specs, out_specs=out_specs, check_vma=False)
```

```python
import itertools

import jax
import jax.numpy as jnp
import ml_dtypes
import numpy as np
from jax import lax
from jax.experimental import pallas as pl
from jax.experimental.pallas import tpu as pltpu
from jax.sharding import PartitionSpec as P

F32 = jnp.float32
BF16 = jnp.bfloat16
MIB = 1 << 20

CX = 2
CY = 2
LZ = 16
ROWS = 8
FEATURES = 32
VMEM = pl.BlockSpec(memory_space=pltpu.VMEM)
HBM = pl.BlockSpec(memory_space=pltpu.HBM)


def nodes_1d():
    return np.cos((2.0 * np.arange(4) + 1.0) * np.pi / 8.0)


def cheb_terms(value):
    return value, 2.0 * value * value - 1.0, 4.0 * value**3 - 3.0 * value


def node_weights():
    return [[0.5 * term for term in cheb_terms(point)] for point in nodes_1d()]


def node_grid():
    points = nodes_1d()
    counter = np.arange(64)
    return np.stack([points[counter // 16], points[counter // 4 % 4], points[counter % 4]], -1)


def split_two(table):
    high = table.astype(np.float32).astype(ml_dtypes.bfloat16)
    low = (table - high.astype(np.float64)).astype(np.float32).astype(ml_dtypes.bfloat16)
    return high, low


def upward_tensor():
    points = nodes_1d()
    shifted = (points[None, :] + 2.0 * np.arange(2)[:, None] - 1.0) / 2.0
    factor = 0.25 + 0.0 * shifted[..., None]
    for of_value, of_node in zip(cheb_terms(shifted), cheb_terms(points)):
        factor = factor + 0.5 * of_value[..., None] * of_node
    full = np.einsum("xia,yjb,zkc->xyzijkabc", factor, factor, factor)
    return full.reshape(2, 2, 2, 64, 64)


def inverse_distance(offset):
    grid = node_grid()
    spread = (grid[None, :, :] - grid[:, None, :]) / 2.0 - np.asarray(offset, np.float64)
    return 1.0 / np.sqrt(np.sum(spread * spread, -1))


def adjacent(offset):
    return max(abs(int(step)) for step in offset) <= 1


def canonical_tiles():
    return [
        (cx, cy, cz)
        for cx in range(2)
        for cy in range(2)
        for cz in range(4)
        if not (cx == 0 and cy == 0 and cz <= 1)
    ]


def translation_tiles():
    tiles = []
    for cx, cy, cz in canonical_tiles():
        tile = np.zeros((4, 64, 4, 64))
        for source in range(4):
            for target in range(4):
                offset = (
                    2 * cx + source // 2 - target // 2,
                    2 * cy + source % 2 - target % 2,
                    cz,
                )
                if not adjacent(offset):
                    tile[source, :, target, :] = inverse_distance(offset)
        tiles.append(tile.reshape(256, 256))
    return np.stack(split_two(np.stack(tiles)), 1)


def reflection_matrix(flip_x, flip_y, flip_z):
    index = np.arange(256)
    hx, hy, a, b, c = index // 128, index // 64 % 2, index // 16 % 4, index // 4 % 4, index % 4
    if flip_x:
        hx, a = 1 - hx, 3 - a
    if flip_y:
        hy, b = 1 - hy, 3 - b
    if flip_z:
        c = 3 - c
    matrix = np.zeros((256, 256), np.float32)
    matrix[hx * 128 + hy * 64 + a * 16 + b * 4 + c, index] = 1.0
    return matrix


def reflection_tables():
    pairs = [
        np.concatenate([reflection_matrix(fx, fy, 0), reflection_matrix(fx, fy, 1)], 1)
        for fx in range(2)
        for fy in range(2)
    ]
    return np.stack(pairs).astype(ml_dtypes.bfloat16)


def up_tables():
    upward = upward_tensor()
    table = upward.transpose(0, 1, 3, 2, 4).reshape(256, 128)
    return np.stack(split_two(table))


def down_table():
    upward = upward_tensor()
    table = upward.transpose(4, 2, 0, 1, 3).reshape(64, 512)
    high, low = split_two(table)
    return np.concatenate([high, high, low, np.zeros_like(low)], 0)


def top_tables(boxes_x, boxes_y):
    offsets = range(-(boxes_x - 1), boxes_x), range(-(boxes_y - 1), boxes_y)
    table = np.zeros((len(offsets[0]), len(offsets[1]), 2, 64, 2, 64))
    for (ix, dx), (iy, dy) in itertools.product(enumerate(offsets[0]), enumerate(offsets[1])):
        for source, target in itertools.product(range(2), range(2)):
            offset = (dx, dy, source - target)
            if not adjacent(offset):
                table[ix, iy, source, :, target, :] = 0.125 * inverse_distance(offset)
    return np.stack(split_two(table.reshape(len(offsets[0]), len(offsets[1]), 128, 128)), 2)


def small_tables(boxes_x, boxes_y):
    down = down_table().reshape(256, 4, 128).transpose(1, 0, 2)
    parts = [up_tables(), down, top_tables(boxes_x, boxes_y)]
    return np.concatenate([part.reshape(-1, 128) for part in parts], 0)


def halves(value):
    high = value.astype(BF16)
    return high, (value - high.astype(F32)).astype(BF16)


def dot(left, right):
    return jnp.dot(left, right, preferred_element_type=F32)


def dot_three(value, high_table, low_table):
    rows = value.shape[0]
    high, low = halves(value)
    both = dot(jnp.concatenate([high, low], 0), high_table)
    return both[:rows] + both[rows:] + dot(high, low_table)


def lanes(shape):
    return lax.broadcasted_iota(jnp.int32, shape, len(shape) - 1)


def sublanes(shape):
    return lax.broadcasted_iota(jnp.int32, shape, len(shape) - 2)


def leaf_segments(leaves):
    shape = (leaves, LZ * 64)
    return jnp.where(lanes(shape) // 64 == lax.rem(sublanes(shape), LZ), 1.0, 0.0).astype(BF16)


def lane_flip(value):
    return pltpu.roll(value, 64, 1)


def weight_rows(pattern):
    weights = node_weights()
    index = sublanes((8, 128))
    rows = []
    for term in range(3):
        row = jnp.full((8, 128), weights[pattern(0)][term], F32)
        for sub in range(1, 8):
            row = jnp.where(index == sub, weights[pattern(sub)][term], row)
        rows.append(row)
    return rows


def basis_rows():
    return (
        weight_rows(lambda sub: sub // 4),
        weight_rows(lambda sub: 2 + sub // 4),
        weight_rows(lambda sub: sub % 4),
    )


def basis_tile(row_x, row_y, row_z, scale, tables):
    y_low, y_high, z_all = tables
    wide = [jnp.broadcast_to(2.0 * row - 1.0, (8, 128)) for row in (row_x, row_y, row_z)]
    terms = [cheb_terms(value) for value in wide]

    def mix(weights, term):
        return 0.25 + (weights[0] * term[0] + weights[1] * term[1] + weights[2] * term[2])

    along_z = mix(z_all, terms[2])
    pair = mix(y_low, terms[1]) * along_z, mix(y_high, terms[1]) * along_z
    tiles = []
    for weights in node_weights():
        along_x = mix(weights, terms[0])
        if scale is not None:
            along_x = along_x * scale
        tiles += [along_x * pair[0], along_x * pair[1]]
    return tiles


def three_pieces(value):
    first = value.astype(BF16).astype(F32)
    rest = value - first
    second = rest.astype(BF16).astype(F32)
    return first, second, rest - second


def source_features(coords):
    rows = []
    total = None
    for coord in coords:
        one, two, three = three_pieces(coord)
        rows += [one, two, one, two, three, one]
        total = coord * coord if total is None else total + coord * coord
    unit = jnp.ones_like(coords[0])
    return rows + [unit] * 3 + list(three_pieces(total)) + [jnp.zeros_like(unit)] * 8


def target_features(coords):
    rows = []
    total = None
    for coord in coords:
        one, two, three = three_pieces(-2.0 * coord)
        rows += [one, one, two, two, one, three]
        total = coord * coord if total is None else total + coord * coord
    unit = jnp.ones_like(coords[0])
    return rows + list(three_pieces(total)) + [unit] * 3 + [jnp.zeros_like(unit)] * 8


def store_features(rows, wide_ref, group):
    for row, value in enumerate(rows):
        wide_ref[group, pl.ds(row, ROWS, stride=FEATURES), :] = value


class Near:
    def __init__(self, raw, wide_ref, charge_ref, target_ref):
        self.raw = raw
        self.wide_ref = wide_ref
        self.charge_ref = charge_ref
        self.target_ref = target_ref
        self.groups = 0
        self.charges = 0
        self.upper = lanes((ROWS, 128)) >= 64
        self.row = sublanes((ROWS, 128))

    def place(self, x, y):
        return self.raw(0, x, y) + (x - 2.0), self.raw(1, x, y) + (y - 2.0)

    def targets(self):
        for ab in range(4):
            x, y = ab // 2 + 1, ab % 2 + 1
            coords = self.place(x, y)
            along_z = self.raw(2, x, y) + jnp.where(self.upper, 0.0, -1.0)
            store_features(target_features(coords + (along_z,)), self.wide_ref, ab)
        for ab in range(4):
            for j in range(ROWS):
                block = self.wide_ref[ab, FEATURES * j : FEATURES * (j + 1), :]
                self.target_ref[ab, j] = block.T.astype(BF16)

    def add_group(self, coords):
        store_features(source_features(coords), self.wide_ref, self.groups)
        self.groups += 1
        return self.groups - 1

    def add_charge(self, charge):
        self.charge_ref[self.charges] = charge
        self.charges += 1
        return self.charges - 1

    def main(self, x, y):
        along_z = self.raw(2, x, y) + jnp.where(self.upper, 0.0, -1.0)
        group = self.add_group(self.place(x, y) + (along_z,))
        return group, self.add_charge(self.raw(3, x, y))

    def outer(self, first, second, side, keep=None):
        place = [self.place(*first), self.place(*second)]

        def merge(one, two):
            if side == 0:
                value = jnp.where(self.upper, two, lane_flip(one))
                return pltpu.roll(value, 1, 0)
            value = jnp.where(self.upper, lane_flip(two), one)
            return pltpu.roll(value, ROWS - 1, 0)

        along_z = merge(self.raw(2, *first), self.raw(2, *second)) + (-2.0 if side == 0 else 1.0)
        coords = (merge(place[0][0], place[1][0]), merge(place[0][1], place[1][1]), along_z)
        charge = merge(self.raw(3, *first), self.raw(3, *second))
        charge = jnp.where(self.row == (0 if side == 0 else ROWS - 1), 0.0, charge)
        group = self.add_group(coords)
        if keep is None:
            return group, self.add_charge(charge)
        low = self.add_charge(jnp.where(self.upper, 0.0, charge))
        high = self.add_charge(jnp.where(self.upper, charge, 0.0))
        return (group, low), (group, high)

    def run(self, plan, emit):
        eye = sublanes((128, 128)) == lanes((128, 128))

        def pairs(targets, tiles, j, own, total):
            if not tiles:
                return total
            span = pl.ds(pl.multiple_of(j * FEATURES, FEATURES), FEATURES)
            block = jnp.concatenate([self.wide_ref[group, span, :] for group, _ in tiles], 1)
            squared = dot(targets, block.astype(BF16))
            for position, (group, charge) in enumerate(tiles):
                inverse = lax.rsqrt(squared[:, 128 * position : 128 * position + 128])
                if group == own:
                    inverse = jnp.where(eye, 0.0, inverse)
                total = total + inverse * self.charge_ref[charge, pl.ds(j, 1), :]
            return total

        def step(j, carry):
            for ab in range(4):
                mains, below, above, own = plan[ab]
                targets = self.target_ref[ab, j]
                total = pairs(targets, mains, j, own, jnp.zeros((128, 128), F32))
                lower = pairs(targets[:64], below, j, None, total[:64])
                higher = pairs(targets[64:], above, j, None, total[64:])
                total = jnp.concatenate([lower, higher], 0)
                emit(ab, j, jnp.sum(total.T, 0, keepdims=True))
            return carry

        lax.fori_loop(0, ROWS, step, 0)


def plan_own(near):
    mains = {(x, y): near.main(x, y) for x in (1, 2) for y in (1, 2)}
    outer = [[near.outer((x, 1), (x, 2), side) for x in (1, 2)] for side in range(2)]
    plan = []
    for ab in range(4):
        own = mains[(ab // 2 + 1, ab % 2 + 1)][0]
        plan.append((list(mains.values()), outer[0], outer[1], own))
    return plan


def plan_beside_y(near):
    plan = []
    sides = []
    for y in (0, 3):
        mains = [near.main(x, y) for x in (1, 2)]
        outer = [[near.outer((1, y), (2, y), side)] for side in range(2)]
        sides.append((mains, outer[0], outer[1], None))
    for ab in range(4):
        plan.append(sides[ab % 2])
    return plan


def plan_beside_x(near):
    plan = []
    for x in (0, 3):
        mains = [near.main(x, y) for y in range(4)]
        middle = [near.outer((x, 1), (x, 2), side) for side in range(2)]
        ends = [near.outer((x, 0), (x, 3), side, keep=True) for side in range(2)]
        for b in range(2):
            plan.append(
                (mains[b : b + 3], [middle[0], ends[0][b]], [middle[1], ends[1][b]], None)
            )
    return plan


def join_plans(plans):
    joined = []
    for ab in range(4):
        parts = [plan[ab] for plan in plans]
        own = next((part[3] for part in parts if part[3] is not None), None)
        joined.append(tuple(sum((part[k] for part in parts), []) for k in range(3)) + (own,))
    return joined


def near_scratch(groups, charges):
    return [
        pltpu.VMEM((groups, ROWS * FEATURES, 128), F32),
        pltpu.VMEM((charges, ROWS, 128), F32),
        pltpu.VMEM((4, ROWS, 128, FEATURES), BF16),
    ]


ONE_ROWS = 8
LEAF_ROWS = 32
EDGE_ROWS = 64


def moments_kernel(
    offsets_hbm, charges_hbm, small_hbm, own_part, to_low, to_high, offsets, charges, up, basis, sums, semaphores
):
    index_y = lax.axis_index("gy")
    copies = [
        pltpu.make_async_copy(offsets_hbm, offsets, semaphores.at[0]),
        pltpu.make_async_copy(charges_hbm, charges, semaphores.at[1]),
        pltpu.make_async_copy(small_hbm.at[0:512], up, semaphores.at[2]),
    ]
    for copy in copies:
        copy.start()
    tables = basis_rows()
    segments = leaf_segments(LZ)
    copies[0].wait()
    copies[1].wait()
    for x in range(CX):
        for y in range(CY):
            for j in range(ROWS):
                span = slice(128 * j, 128 * j + 128)
                rows = [offsets[c, x, y : y + 1, span] for c in range(3)]
                charge = charges[x, y : y + 1, span]
                for c, row in enumerate(rows + [charge]):
                    own_part[c, x, y, j : j + 1, :] = row
                    edge = ONE_ROWS + LEAF_ROWS + (c * CX + x) * ROWS + j
                    target = to_low if y == 0 else to_high
                    target[edge : edge + 1, :] = row
                tiles = basis_tile(*rows, charge, tables)
                for k in range(4):
                    pair = jnp.concatenate(tiles[2 * k : 2 * k + 2], 0)
                    high, low = halves(pair)
                    first = (x * CY + y) * 64 + 16 * k
                    basis[0, first : first + 16, span] = high
                    basis[1, first : first + 16, span] = low
    contract = (((1,), (1,)), ((), ()))
    leaf = lax.dot_general(segments, basis[0], contract, preferred_element_type=F32)
    leaf = leaf + lax.dot_general(segments, basis[1], contract, preferred_element_type=F32)
    copies[2].wait()
    sums[...] = dot_three(leaf, up[0:256], up[256:512])
    first = sums[pl.ds(0, 8, stride=2), :] + lane_flip(sums[pl.ds(1, 8, stride=2), :])
    first = jnp.where(lanes((8, 128)) < 64, first, 0.0)
    first = jnp.where(lax.rem(index_y, 2) == 1, lane_flip(first), first)
    for target in (to_low, to_high):
        target[0:8, :] = first
        target[8:24, :] = leaf[:, :128]
        target[24:40, :] = leaf[:, 128:]


def moments_call(offsets, charges, small):
    payload = jax.ShapeDtypeStruct((ONE_ROWS + LEAF_ROWS + EDGE_ROWS, 128), F32)
    return pl.pallas_call(
        moments_kernel,
        out_shape=(jax.ShapeDtypeStruct((4, CX, CY, ROWS, 128), F32), payload, payload),
        in_specs=[HBM] * 3,
        out_specs=(VMEM,) * 3,
        scratch_shapes=[
            pltpu.VMEM(offsets.shape, F32),
            pltpu.VMEM(charges.shape, F32),
            pltpu.VMEM((512, 128), BF16),
            pltpu.VMEM((2, 256, 1024), BF16),
            pltpu.VMEM((16, 128), F32),
            pltpu.SemaphoreType.DMA((3,)),
        ],
        compiler_params=pltpu.CompilerParams(vmem_limit_bytes=8 * MIB),
        cost_estimate=pl.CostEstimate(flops=10_000_000, bytes_accessed=300_000, transcendentals=0),
        name="moments",
    )(offsets, charges, small)


PART_ROWS = 4 * 4 * ROWS


def row_kernel(count_y, own_part, to_low, from_low, from_high, *rest):
    others, (out_low, out_high) = rest[:-2], rest[-2:]
    index_y = lax.axis_index("gy")
    ones = count_y // 2 * 8
    has_low = index_y > 0
    has_high = index_y < count_y - 1

    out_low[0:ones, :] = jnp.zeros((ones, 128), F32)
    received = {0: to_low, 1: from_low, count_y - 1: from_high}
    for shift, ref in zip(range(2, count_y - 1), others):
        received[shift] = ref
    for shift, ref in received.items():
        source = lax.rem(index_y - shift + count_y, count_y)
        place = pl.ds(pl.multiple_of(source // 2 * 8, 8), 8)
        out_low[place, :] = out_low[place, :] + ref[0:8, :]
    for piece, (ref, keep) in enumerate(((from_low, has_low), (to_low, None), (from_high, has_high))):
        block = ref[ONE_ROWS : ONE_ROWS + LEAF_ROWS, :]
        if keep is not None:
            block = jnp.where(keep, block, 0.0)
        out_low[ones + LEAF_ROWS * piece : ones + LEAF_ROWS * (piece + 1), :] = block
    shared = ones + 3 * LEAF_ROWS
    out_high[0:shared, :] = out_low[0:shared, :]
    for x, out in enumerate((out_low, out_high)):
        for c in range(4):
            edge = ONE_ROWS + LEAF_ROWS + (c * CX + x) * ROWS
            columns = [
                from_low[edge : edge + ROWS, :],
                own_part[c, x, 0],
                own_part[c, x, 1],
                from_high[edge : edge + ROWS, :],
            ]
            if c == 3:
                columns[0] = jnp.where(has_low, columns[0], 0.0)
                columns[3] = jnp.where(has_high, columns[3], 0.0)
            for y, column in enumerate(columns):
                row = shared + (c * 4 + y) * ROWS
                out[row : row + ROWS, :] = column


def row_call(count_y, own_part, to_low, from_low, from_high, others):
    rows = count_y // 2 * 8 + 3 * LEAF_ROWS + PART_ROWS
    payload = jax.ShapeDtypeStruct((rows, 128), F32)
    operands = (own_part, to_low, from_low, from_high, *others)
    return pl.pallas_call(
        lambda *refs: row_kernel(count_y, *refs),
        out_shape=(payload, payload),
        in_specs=[VMEM] * len(operands),
        out_specs=(VMEM,) * 2,
        compiler_params=pltpu.CompilerParams(vmem_limit_bytes=8 * MIB),
        cost_estimate=pl.CostEstimate(flops=100_000, bytes_accessed=500_000, transcendentals=0),
        name="row",
    )(*operands)


def finish_kernel(count_x, count_y, refs):
    (own_low, own_high, from_low, from_high), refs = refs[:4], refs[4:]
    others, refs = refs[: count_x - 3], refs[count_x - 3 :]
    constants, refs = refs[:3], refs[3:]
    out, refs = refs[0], refs[1:]
    wide_ref, charge_ref, target_ref, refs = *refs[:3], refs[3:]
    near_rows, small, flips, tiles, level_one, level_two, boxes, flipped, sums, local, semaphores = refs

    index_x, index_y = lax.axis_index("gx"), lax.axis_index("gy")
    pairs_y = count_y // 2
    ones = pairs_y * 8
    shared = ones + 3 * LEAF_ROWS
    has_low = index_x > 0
    has_high = index_x < count_x - 1
    fetches = [
        pltpu.make_async_copy(constant, place, semaphores.at[k])
        for k, (constant, place) in enumerate(zip(constants, (small, flips, tiles)))
    ]
    for fetch in fetches:
        fetch.start()

    columns = (from_low, own_low, own_high, from_high)

    def raw(c, x, y):
        row = shared + (c * 4 + y) * ROWS
        value = columns[x][row : row + ROWS, :]
        if c == 3 and x in (0, 3):
            value = jnp.where(has_low if x == 0 else has_high, value, 0.0)
        return value

    near = Near(raw, wide_ref, charge_ref, target_ref)
    near.targets()
    plan = join_plans([plan_own(near), plan_beside_y(near), plan_beside_x(near)])

    def emit(ab, j, row):
        near_rows[ab, pl.ds(j, 1), :] = row

    near.run(plan, emit)

    fetches[0].wait()
    level_one[...] = jnp.zeros_like(level_one)
    level_two[...] = jnp.zeros_like(level_two)
    received = {0: own_low, 1: from_low, count_x - 1: from_high}
    for shift, ref in zip(range(2, count_x - 1), others):
        received[shift] = ref
    for shift, ref in received.items():
        source = lax.rem(index_x - shift + count_x, count_x)
        for pair in range(pairs_y):
            level_one[source + 2, pair + 1] = ref[8 * pair : 8 * pair + 8, :]
    half_x = count_x // 2
    children = jnp.concatenate(
        [
            jnp.concatenate([level_one[2 * x + 2, y + 1], level_one[2 * x + 3, y + 1]], 1)
            for x in range(half_x)
            for y in range(pairs_y)
        ],
        0,
    )
    below = half_x * pairs_y * 8
    low_lanes = lanes((4, 128)) < 64
    sums[0:below, :] = dot_three(children, small[0:256], small[256:512])
    for x in range(half_x):
        for y in range(pairs_y):
            row = (x * pairs_y + y) * 8
            even = sums[pl.ds(row, 4, stride=2), :]
            odd = sums[pl.ds(row + 1, 4, stride=2), :]
            level_two[x + 2, y + 2, 0:4] = jnp.where(low_lanes, even + lane_flip(odd), 0.0)

    def second_group(group_x, group_y):
        return jnp.concatenate(
            [
                level_two[2 * group_x + h + 2, 2 * group_y + 2]
                + lane_flip(level_two[2 * group_x + h + 2, 2 * group_y + 3])
                for h in range(2)
            ],
            1,
        )

    quarter_x, quarter_y = index_x // 4, index_y // 4
    tops = [(x, y) for x in range(count_x // 4) for y in range(count_y // 4)]
    stacked = jnp.concatenate([second_group(x, y) for x, y in tops], 0)
    if stacked.shape[0] % 16 != 0:
        stacked = jnp.concatenate([stacked, jnp.zeros((8, 256), F32)], 0)
    sums[0 : stacked.shape[0], :] = dot_three(stacked, small[0:256], small[256:512])
    top_far = jnp.zeros((16, 128), F32)
    for position, (x, y) in enumerate(tops):
        even = sums[pl.ds(8 * position, 2, stride=2), :]
        odd = sums[pl.ds(8 * position + 1, 2, stride=2), :]
        third = jnp.where(lanes((2, 128)) < 64, even + lane_flip(odd), 0.0)
        third = third[0:1] + lane_flip(third)[1:2]
        step_x, step_y = x - quarter_x + count_x // 4 - 1, y - quarter_y + count_y // 4 - 1
        row = 1536 + 256 * (step_x * (count_y // 4 * 2 - 1) + step_y)
        table = [small[pl.ds(pl.multiple_of(row + 128 * k, 128), 128), :] for k in range(2)]
        top_far = top_far + dot_three(jnp.broadcast_to(third, (16, 128)), table[0], table[1])

    fetches[1].wait()
    boxes[...] = jnp.zeros_like(boxes)
    leaf_refs = {-1: from_low, 0: own_low, 1: from_high}
    for gx in (-1, 0, 1):
        for gy in (-1, 0, 1):
            start = ones + LEAF_ROWS * (gy + 1)
            for h in range(2):
                block = leaf_refs[gx][start + 16 * h : start + 16 * h + 16, :]
                if gx != 0:
                    block = jnp.where(has_low if gx < 0 else has_high, block, 0.0)
                span = slice(128 * h, 128 * h + 128)
                boxes[8:24, span] = block
                boxes[32:40, span] = level_one[
                    2 * (index_x // 2 + gx) + h + 2, index_y // 2 + gy + 1
                ]
            boxes[48:56, :] = second_group(quarter_x + gx, quarter_y + gy)
            high, low = halves(boxes[...])
            table = flips[2 * (gx < 0) + (gy < 0)]
            mixed = dot(jnp.concatenate([high, low], 0), table)
            group = 3 * (gx + 1) + gy + 1
            for z in range(2):
                flipped[group, z, 0] = mixed[:64, 256 * z : 256 * z + 256]
                flipped[group, z, 1] = mixed[64:, 256 * z : 256 * z + 256]

    fetches[2].wait()
    odd_row = lax.rem(sublanes((32, 256)), 2) == 1
    totals = {}
    for position, (cx, cy, cz) in enumerate(canonical_tiles()):
        entries = [
            (gx, gy, dz)
            for gx in sorted({cx, -cx})
            for gy in sorted({cy, -cy})
            for dz in sorted({cz, -cz})
        ]
        pieces = [[], []]
        for gx, gy, dz in entries:
            group = 3 * (gx + 1) + gy + 1
            for part in range(2):
                view = flipped.at[group, int(dz < 0), part]
                block = jnp.concatenate(
                    [view[8 + dz : 24 + dz, :], view[32 + dz : 40 + dz, :], view[48 + dz : 56 + dz, :]],
                    0,
                )
                if abs(dz) == 3:
                    block = jnp.where(odd_row if dz < 0 else ~odd_row, block, 0.0)
                pieces[part].append(block.astype(BF16))
        rows = 32 * len(entries)
        both = dot(jnp.concatenate(pieces[0] + pieces[1], 0), tiles[position, 0])
        result = both[:rows] + both[rows:] + dot(jnp.concatenate(pieces[0], 0), tiles[position, 1])
        for order, (gx, gy, dz) in enumerate(entries):
            key = (int(gx < 0), int(gy < 0), int(dz < 0))
            piece = result[32 * order : 32 * order + 32]
            totals[key] = totals[key] + piece if key in totals else piece
    far = None
    for (fx, fy, fz), total in totals.items():
        if (fx, fy, fz) != (0, 0, 0):
            high, low = halves(total)
            table = flips[2 * fx + fy, :, 256 * fz : 256 * fz + 256]
            both = dot(jnp.concatenate([high, low], 0), table)
            total = both[:32] + both[32:]
        far = total if far is None else far + total

    def select(block, hx, hy):
        tile = jnp.where(hx == 1, block[:, 128:256], block[:, 0:128])
        return jnp.where(hy == 1, lane_flip(tile), tile)

    def refine(parent):
        keep = lanes((16, 128)) < 64
        parent = jnp.where(keep, parent, 0.0)
        high = parent.astype(BF16).astype(F32)
        low = parent - high
        left = jnp.concatenate([high + lane_flip(low), high], 1).astype(BF16)
        down = jnp.concatenate([small[512 + 256 * k : 768 + 256 * k, :] for k in range(4)], 1)
        spread = dot(left, down)
        for half in range(2):
            for h in range(2):
                span = slice(256 * half + 128 * h, 256 * half + 128 * h + 128)
                local[h, pl.ds(half, 16, stride=2), :] = spread[:, span]
        return jnp.concatenate([local[0], local[1]], 1)

    top_local = jnp.where(
        sublanes((16, 128)) == 0, top_far, jnp.where(sublanes((16, 128)) == 1, lane_flip(top_far), 0.0)
    )
    children_far = refine(top_local)
    half_index_x, half_index_y = index_x // 2, index_y // 2
    second = select(children_far[0:8], lax.rem(half_index_x, 2), lax.rem(half_index_y, 2))
    second = second + 0.25 * select(far[24:32], lax.rem(half_index_x, 2), lax.rem(half_index_y, 2))
    zeros = jnp.zeros((8, 128), F32)
    children_far = refine(jnp.concatenate([second, zeros], 0))
    first = select(children_far[0:8], lax.rem(index_x, 2), lax.rem(index_y, 2))
    first = first + 0.5 * select(far[16:24], lax.rem(index_x, 2), lax.rem(index_y, 2))
    leaf = refine(jnp.concatenate([first, zeros], 0))[0:16] + far[0:16]

    one, two = halves(leaf)
    turned = jnp.concatenate([one.astype(F32), two.astype(F32)], 0).T.astype(BF16)
    table = leaf_segments(2 * LZ)
    tables = basis_rows()
    for x in range(CX):
        for y in range(CY):
            column = x * CY + y
            spread = dot(turned[64 * column : 64 * column + 64], table)
            for j in range(ROWS):
                span = slice(128 * j, 128 * j + 128)
                rows = [raw(c, x + 1, y + 1)[j : j + 1] for c in range(3)]
                basis = basis_tile(*rows, None, tables)
                total = None
                for k in range(8):
                    term = basis[k] * spread[8 * k : 8 * k + 8, span]
                    total = term if total is None else total + term
                value = jnp.sum(total, 0, keepdims=True) + near_rows[column, j : j + 1, :]
                out[x, y : y + 1, span] = value


def finish_call(count_x, count_y, payloads, others, constants):
    operands = (*payloads, *others, *constants)
    half_x, half_y = count_x // 2, count_y // 2
    scratch = near_scratch(32, 36) + [
        pltpu.VMEM((4, ROWS, 128), F32),
        *[pltpu.VMEM(constant.shape, BF16) for constant in constants],
        pltpu.VMEM((count_x + 4, half_y + 2, 8, 128), F32),
        pltpu.VMEM((half_x + 4, half_y + 4, 8, 128), F32),
        pltpu.VMEM((64, 256), F32),
        pltpu.VMEM((9, 2, 2, 64, 256), F32),
        pltpu.VMEM((max(16, half_x * half_y * 8), 128), F32),
        pltpu.VMEM((2, 32, 128), F32),
        pltpu.SemaphoreType.DMA((3,)),
    ]
    return pl.pallas_call(
        lambda *refs: finish_kernel(count_x, count_y, refs),
        out_shape=jax.ShapeDtypeStruct((CX, CY, LZ * 64), F32),
        in_specs=[VMEM] * (len(operands) - 3) + [HBM] * 3,
        out_specs=VMEM,
        scratch_shapes=scratch,
        compiler_params=pltpu.CompilerParams(vmem_limit_bytes=24 * MIB),
        name="finish",
    )(*operands)


def in_hbm(value):
    return pltpu.with_memory_space_constraint(value, pltpu.HBM)


def shift_ring(value, axis, shift):
    count = lax.axis_size(axis)
    return lax.ppermute(value, axis, [(i, (i + shift) % count) for i in range(count)])


def solution(mesh):
    count_x, count_y = mesh.shape["gx"], mesh.shape["gy"]
    tables = small_tables(count_x // 4, count_y // 4), reflection_tables(), translation_tiles()

    def body(offsets, charges):
        constants = [in_hbm(jnp.asarray(table)) for table in tables]
        offsets, charges = in_hbm(offsets), in_hbm(charges)
        own_part, to_low, to_high = moments_call(offsets, charges, constants[0])
        from_low = shift_ring(to_high, "gy", 1)
        from_high = shift_ring(to_low, "gy", count_y - 1)
        own_one = to_low[:ONE_ROWS]
        others = [shift_ring(own_one, "gy", shift) for shift in range(2, count_y - 1)]
        row_low, row_high = row_call(count_y, own_part, to_low, from_low, from_high, others)
        next_low = shift_ring(row_high, "gx", 1)
        next_high = shift_ring(row_low, "gx", count_x - 1)
        row_one = row_low[: count_y // 2 * 8]
        others = [shift_ring(row_one, "gx", shift) for shift in range(2, count_x - 1)]
        payloads = (row_low, row_high, next_low, next_high)
        return finish_call(count_x, count_y, payloads, others, constants)

    in_specs = (P(None, "gx", "gy", None), P("gx", "gy", None))
    out_specs = P("gx", "gy", None)
    return jax.shard_map(body, mesh=mesh, in_specs=in_specs, out_specs=out_specs, check_vma=False)
```

```python
import functools
import itertools

import jax
import jax.numpy as jnp
import ml_dtypes
import numpy as np
from jax import lax
from jax.experimental import pallas as pl
from jax.experimental.pallas import tpu as pltpu
from jax.sharding import PartitionSpec as P

F32 = jnp.float32
BF16 = jnp.bfloat16
MIB = 1 << 20

CX = 2
CY = 2
LZ = 16
ROWS = 8
FEATURES = 32
VMEM = pl.BlockSpec(memory_space=pltpu.VMEM)
HBM = pl.BlockSpec(memory_space=pltpu.HBM)


def nodes_1d():
    return np.cos((2.0 * np.arange(4) + 1.0) * np.pi / 8.0)


def cheb_terms(value):
    return value, 2.0 * value * value - 1.0, 4.0 * value**3 - 3.0 * value


def node_weights():
    return [[0.5 * term for term in cheb_terms(point)] for point in nodes_1d()]


def node_grid():
    points = nodes_1d()
    counter = np.arange(64)
    return np.stack([points[counter // 16], points[counter // 4 % 4], points[counter % 4]], -1)


def split_two(table):
    high = table.astype(np.float32).astype(ml_dtypes.bfloat16)
    low = (table - high.astype(np.float64)).astype(np.float32).astype(ml_dtypes.bfloat16)
    return high, low


def upward_tensor():
    points = nodes_1d()
    shifted = (points[None, :] + 2.0 * np.arange(2)[:, None] - 1.0) / 2.0
    factor = 0.25 + 0.0 * shifted[..., None]
    for of_value, of_node in zip(cheb_terms(shifted), cheb_terms(points)):
        factor = factor + 0.5 * of_value[..., None] * of_node
    full = np.einsum("xia,yjb,zkc->xyzijkabc", factor, factor, factor)
    return full.reshape(2, 2, 2, 64, 64)


def inverse_distance(offset):
    grid = node_grid()
    spread = (grid[None, :, :] - grid[:, None, :]) / 2.0 - np.asarray(offset, np.float64)
    return 1.0 / np.sqrt(np.sum(spread * spread, -1))


def adjacent(offset):
    return max(abs(int(step)) for step in offset) <= 1


def canonical_tiles():
    return [
        (cx, cy, cz)
        for cx in range(2)
        for cy in range(2)
        for cz in range(4)
        if not (cx == 0 and cy == 0 and cz <= 1)
    ]


def translation_tiles():
    tiles = []
    for cx, cy, cz in canonical_tiles():
        tile = np.zeros((4, 64, 4, 64))
        for source in range(4):
            for target in range(4):
                offset = (
                    2 * cx + source // 2 - target // 2,
                    2 * cy + source % 2 - target % 2,
                    cz,
                )
                if not adjacent(offset):
                    tile[source, :, target, :] = inverse_distance(offset)
        tiles.append(tile.reshape(256, 256))
    return np.stack(split_two(np.stack(tiles)), 1)


def reflection_matrix(flip_x, flip_y, flip_z):
    index = np.arange(256)
    hx, hy, a, b, c = index // 128, index // 64 % 2, index // 16 % 4, index // 4 % 4, index % 4
    if flip_x:
        hx, a = 1 - hx, 3 - a
    if flip_y:
        hy, b = 1 - hy, 3 - b
    if flip_z:
        c = 3 - c
    matrix = np.zeros((256, 256), np.float32)
    matrix[hx * 128 + hy * 64 + a * 16 + b * 4 + c, index] = 1.0
    return matrix


def reflection_tables():
    pairs = [
        np.concatenate([reflection_matrix(fx, fy, 0), reflection_matrix(fx, fy, 1)], 1)
        for fx in range(2)
        for fy in range(2)
    ]
    return np.stack(pairs).astype(ml_dtypes.bfloat16)


def up_tables():
    upward = upward_tensor()
    table = upward.transpose(0, 1, 3, 2, 4).reshape(256, 128)
    return np.stack(split_two(table))


def down_table():
    upward = upward_tensor()
    table = upward.transpose(4, 2, 0, 1, 3).reshape(64, 512)
    high, low = split_two(table)
    return np.concatenate([high, high, low, np.zeros_like(low)], 0)


def top_tables(boxes_x, boxes_y):
    offsets = range(-(boxes_x - 1), boxes_x), range(-(boxes_y - 1), boxes_y)
    table = np.zeros((len(offsets[0]), len(offsets[1]), 2, 64, 2, 64))
    for (ix, dx), (iy, dy) in itertools.product(enumerate(offsets[0]), enumerate(offsets[1])):
        for source, target in itertools.product(range(2), range(2)):
            offset = (dx, dy, source - target)
            if not adjacent(offset):
                table[ix, iy, source, :, target, :] = 0.125 * inverse_distance(offset)
    return np.stack(split_two(table.reshape(len(offsets[0]), len(offsets[1]), 128, 128)), 2)


def small_tables(boxes_x, boxes_y):
    down = down_table().reshape(256, 4, 128).transpose(1, 0, 2)
    parts = [up_tables(), down, top_tables(boxes_x, boxes_y)]
    return np.concatenate([part.reshape(-1, 128) for part in parts], 0)


def halves(value):
    high = value.astype(BF16)
    return high, (value - high.astype(F32)).astype(BF16)


def dot(left, right):
    return jnp.dot(left, right, preferred_element_type=F32)


def dot_three(value, high_table, low_table):
    rows = value.shape[0]
    high, low = halves(value)
    both = dot(jnp.concatenate([high, low], 0), high_table)
    return both[:rows] + both[rows:] + dot(high, low_table)


def lanes(shape):
    return lax.broadcasted_iota(jnp.int32, shape, len(shape) - 1)


def sublanes(shape):
    return lax.broadcasted_iota(jnp.int32, shape, len(shape) - 2)


def leaf_segments(leaves):
    shape = (leaves, LZ * 64)
    return jnp.where(lanes(shape) // 64 == lax.rem(sublanes(shape), LZ), 1.0, 0.0).astype(BF16)


def lane_flip(value):
    return pltpu.roll(value, 64, 1)


def weight_rows(pattern):
    weights = node_weights()
    index = sublanes((8, 128))
    rows = []
    for term in range(3):
        row = jnp.full((8, 128), weights[pattern(0)][term], F32)
        for sub in range(1, 8):
            row = jnp.where(index == sub, weights[pattern(sub)][term], row)
        rows.append(row)
    return rows


def basis_rows():
    return (
        weight_rows(lambda sub: sub // 4),
        weight_rows(lambda sub: 2 + sub // 4),
        weight_rows(lambda sub: sub % 4),
    )


def basis_tile(row_x, row_y, row_z, scale, tables):
    y_low, y_high, z_all = tables
    wide = [jnp.broadcast_to(2.0 * row - 1.0, (8, 128)) for row in (row_x, row_y, row_z)]
    terms = [cheb_terms(value) for value in wide]

    def mix(weights, term):
        return 0.25 + (weights[0] * term[0] + weights[1] * term[1] + weights[2] * term[2])

    along_z = mix(z_all, terms[2])
    pair = mix(y_low, terms[1]) * along_z, mix(y_high, terms[1]) * along_z
    tiles = []
    for weights in node_weights():
        along_x = mix(weights, terms[0])
        if scale is not None:
            along_x = along_x * scale
        tiles += [along_x * pair[0], along_x * pair[1]]
    return tiles


def three_pieces(value):
    first = value.astype(BF16).astype(F32)
    rest = value - first
    second = rest.astype(BF16).astype(F32)
    return first, second, rest - second


def source_features(coords):
    rows = []
    total = None
    for coord in coords:
        one, two, three = three_pieces(coord)
        rows += [one, two, one, two, three, one]
        total = coord * coord if total is None else total + coord * coord
    unit = jnp.ones_like(coords[0])
    return rows + [unit] * 3 + list(three_pieces(total)) + [jnp.zeros_like(unit)] * 8


def target_features(coords):
    rows = []
    total = None
    for coord in coords:
        one, two, three = three_pieces(-2.0 * coord)
        rows += [one, one, two, two, one, three]
        total = coord * coord if total is None else total + coord * coord
    unit = jnp.ones_like(coords[0])
    return rows + list(three_pieces(total)) + [unit] * 3 + [jnp.zeros_like(unit)] * 8


def store_features(rows, wide_ref, group):
    for row, value in enumerate(rows):
        wide_ref[group, pl.ds(row, ROWS, stride=FEATURES), :] = value


def column(raw, x, y):
    return raw(0) + (x - 2.0), raw(1) + (y - 2.0), raw(2), raw(3)


class Near:
    def __init__(self, wide_ref, charge_ref, target_ref):
        self.wide_ref = wide_ref
        self.charge_ref = charge_ref
        self.target_ref = target_ref
        self.groups = 0
        self.charges = 0
        self.upper = lanes((ROWS, 128)) >= 64
        self.row = sublanes((ROWS, 128))

    def in_pair(self, along_z):
        return along_z + jnp.where(self.upper, 0.0, -1.0)

    def targets(self, columns):
        for ab, (x, y, z, _) in enumerate(columns):
            store_features(target_features((x, y, self.in_pair(z))), self.wide_ref, ab)
        for ab in range(4):
            for j in range(ROWS):
                block = self.wide_ref[ab, FEATURES * j : FEATURES * (j + 1), :]
                self.target_ref[ab, j] = block.T.astype(BF16)

    def add_group(self, coords):
        store_features(source_features(coords), self.wide_ref, self.groups)
        self.groups += 1
        return self.groups - 1

    def add_charge(self, charge):
        self.charge_ref[self.charges] = charge
        self.charges += 1
        return self.charges - 1

    def main(self, source):
        x, y, z, charge = source
        return self.add_group((x, y, self.in_pair(z))), self.add_charge(charge)

    def outer(self, first, second, side, keep=False):
        def merge(one, two):
            if side == 0:
                value = jnp.where(self.upper, two, lane_flip(one))
                return pltpu.roll(value, 1, 0)
            value = jnp.where(self.upper, lane_flip(two), one)
            return pltpu.roll(value, ROWS - 1, 0)

        x, y, z, charge = [merge(one, two) for one, two in zip(first, second)]
        charge = jnp.where(self.row == (0 if side == 0 else ROWS - 1), 0.0, charge)
        group = self.add_group((x, y, z + (-2.0 if side == 0 else 1.0)))
        if not keep:
            return group, self.add_charge(charge)
        low = self.add_charge(jnp.where(self.upper, 0.0, charge))
        high = self.add_charge(jnp.where(self.upper, charge, 0.0))
        return (group, low), (group, high)

    def run(self, plan, emit):
        eye = sublanes((128, 128)) == lanes((128, 128))

        def pairs(targets, tiles, j, own, total):
            span = pl.ds(pl.multiple_of(j * FEATURES, FEATURES), FEATURES)
            block = jnp.concatenate([self.wide_ref[group, span, :] for group, _ in tiles], 1)
            squared = dot(targets, block.astype(BF16))
            for position, (group, charge) in enumerate(tiles):
                inverse = lax.rsqrt(squared[:, 128 * position : 128 * position + 128])
                if group == own:
                    inverse = jnp.where(eye, 0.0, inverse)
                total = total + inverse * self.charge_ref[charge, pl.ds(j, 1), :]
            return total

        def step(j, carry):
            for ab, mains, below, above, own in plan:
                targets = self.target_ref[ab, j]
                total = pairs(targets, mains, j, own, jnp.zeros((128, 128), F32))
                lower = pairs(targets[:64], below, j, None, total[:64])
                higher = pairs(targets[64:], above, j, None, total[64:])
                total = jnp.concatenate([lower, higher], 0)
                emit(ab, j, jnp.sum(total.T, 0, keepdims=True))
            return carry

        lax.fori_loop(0, ROWS, step, 0, unroll=True)


def plan_own(near, columns):
    mains = [near.main(source) for source in columns]
    outer = [
        [near.outer(columns[2 * x], columns[2 * x + 1], side) for x in range(2)]
        for side in range(2)
    ]
    return [(ab, mains, outer[0], outer[1], mains[ab][0]) for ab in range(4)]


def plan_beside_y(near, columns):
    plan = []
    for b in range(2):
        mains = [near.main(source) for source in columns[b]]
        outer = [[near.outer(*columns[b], side)] for side in range(2)]
        plan += [(2 * a + b, mains, outer[0], outer[1], None) for a in range(2)]
    return plan


def plan_beside_x(near, columns, side_x):
    mains = [near.main(source) for source in columns]
    middle = [near.outer(columns[1], columns[2], side) for side in range(2)]
    ends = [near.outer(columns[0], columns[3], side, keep=True) for side in range(2)]
    return [
        (2 * side_x + b, mains[b : b + 3], [middle[0], ends[0][b]], [middle[1], ends[1][b]], None)
        for b in range(2)
    ]


def near_scratch(groups, charges):
    return [
        pltpu.VMEM((groups, ROWS * FEATURES, 128), F32),
        pltpu.VMEM((charges, ROWS, 128), F32),
    ]


NEAR_SHAPE = (4, ROWS, 128)


def near_cost(pairs):
    return pl.CostEstimate(flops=40 * pairs, bytes_accessed=600_000, transcendentals=pairs)


ONE_ROWS = 8
LEAF_ROWS = 32
PART_ROWS = 4 * CX * CY * ROWS
OWN_ROWS = ONE_ROWS + LEAF_ROWS + PART_ROWS


def part_row(c, x, y):
    return ONE_ROWS + LEAF_ROWS + ((c * CX + x) * CY + y) * ROWS


def moments_kernel(
    offsets_hbm, charges_hbm, small_hbm, block, offsets, charges, up, basis, sums, semaphores
):
    index_y = lax.axis_index("gy")
    copies = [
        pltpu.make_async_copy(offsets_hbm, offsets, semaphores.at[0]),
        pltpu.make_async_copy(charges_hbm, charges, semaphores.at[1]),
        pltpu.make_async_copy(small_hbm.at[0:512], up, semaphores.at[2]),
    ]
    for copy in copies:
        copy.start()
    tables = basis_rows()
    segments = leaf_segments(LZ)
    copies[0].wait()
    copies[1].wait()
    for x in range(CX):
        for y in range(CY):
            for j in range(ROWS):
                span = slice(128 * j, 128 * j + 128)
                rows = [offsets[c, x, y : y + 1, span] for c in range(3)]
                charge = charges[x, y : y + 1, span]
                for c, row in enumerate(rows + [charge]):
                    place = part_row(c, x, y) + j
                    block[place : place + 1, :] = row
                tiles = basis_tile(*rows, charge, tables)
                for k in range(4):
                    pair = jnp.concatenate(tiles[2 * k : 2 * k + 2], 0)
                    high, low = halves(pair)
                    first = (x * CY + y) * 64 + 16 * k
                    basis[0, first : first + 16, span] = high
                    basis[1, first : first + 16, span] = low
    contract = (((1,), (1,)), ((), ()))
    leaf = lax.dot_general(segments, basis[0], contract, preferred_element_type=F32)
    leaf = leaf + lax.dot_general(segments, basis[1], contract, preferred_element_type=F32)
    copies[2].wait()
    sums[...] = dot_three(leaf, up[0:256], up[256:512])
    first = sums[pl.ds(0, 8, stride=2), :] + lane_flip(sums[pl.ds(1, 8, stride=2), :])
    first = jnp.where(lanes((8, 128)) < 64, first, 0.0)
    first = jnp.where(lax.rem(index_y, 2) == 1, lane_flip(first), first)
    block[0:8, :] = first
    block[8:24, :] = leaf[:, :128]
    block[24:40, :] = leaf[:, 128:]


def moments_call(offsets, charges, small):
    return pl.pallas_call(
        moments_kernel,
        out_shape=jax.ShapeDtypeStruct((OWN_ROWS, 128), F32),
        in_specs=[HBM] * 3,
        out_specs=VMEM,
        scratch_shapes=[
            pltpu.VMEM(offsets.shape, F32),
            pltpu.VMEM(charges.shape, F32),
            pltpu.VMEM((512, 128), BF16),
            pltpu.VMEM((2, 256, 1024), BF16),
            pltpu.VMEM((16, 128), F32),
            pltpu.SemaphoreType.DMA((3,)),
        ],
        compiler_params=pltpu.CompilerParams(vmem_limit_bytes=8 * MIB),
        cost_estimate=pl.CostEstimate(flops=10_000_000, bytes_accessed=300_000, transcendentals=0),
        name="moments",
    )(offsets, charges, small)


EDGE_ROWS = LEAF_ROWS + 4 * CX * ROWS


def bits_below(index, bit):
    return lax.rem(index, 1 << bit)


def bit_of(index, bit):
    return lax.rem(index // (1 << bit), 2)


def in_order(is_first, own, other):
    return jnp.concatenate([jnp.where(is_first, own, other), jnp.where(is_first, other, own)], 0)


def edge_block(block, y):
    rows = [block[ONE_ROWS : ONE_ROWS + LEAF_ROWS, :]]
    for c in range(4):
        for x in range(CX):
            rows.append(block[part_row(c, x, y) : part_row(c, x, y) + ROWS, :])
    return jnp.concatenate(rows, 0)


def group_kernel(level, last_level, own_ref, other_ref, out):
    index = lax.axis_index("gy")
    ones = ONE_ROWS << (level - 1)
    is_first = bit_of(index, level - 1) == 0
    if level == 1:
        out[0:ones, :] = own_ref[0:ones, :] + other_ref[0:ones, :]
        first = jnp.where(is_first, edge_block(own_ref, 0), edge_block(other_ref, 0))
        last = jnp.where(is_first, edge_block(other_ref, 1), edge_block(own_ref, 1))
    else:
        half = ones // 2
        out[0:ones, :] = in_order(is_first, own_ref[0:half, :], other_ref[0:half, :])
        own_far = own_ref[half + EDGE_ROWS : half + 2 * EDGE_ROWS, :]
        other_far = other_ref[half + EDGE_ROWS : half + 2 * EDGE_ROWS, :]
        first = jnp.where(is_first, own_far, other_far)
        last = jnp.where(is_first, other_far, own_far)
    lower = bit_of(index, level) == 0
    out[ones : ones + EDGE_ROWS, :] = jnp.where(lower, last, first)
    if not last_level:
        out[ones + EDGE_ROWS : ones + 2 * EDGE_ROWS, :] = jnp.where(lower, first, last)


def pack_call(kernel, rows, operands, name):
    return pl.pallas_call(
        kernel,
        out_shape=jax.ShapeDtypeStruct((rows, 128), F32),
        in_specs=[VMEM] * len(operands),
        out_specs=VMEM,
        compiler_params=pltpu.CompilerParams(vmem_limit_bytes=8 * MIB),
        cost_estimate=pl.CostEstimate(flops=100_000, bytes_accessed=300_000, transcendentals=0),
        name=name,
    )(*operands)


ROW_LEAF = 3 * LEAF_ROWS
ROW_PART = 4 * 4 * ROWS


def row_part(c, y):
    return ROW_LEAF + (c * 4 + y) * ROWS


def row_kernel(levels, block, other, *refs):
    exchanged, (ones_out, even_out, odd_out) = refs[: 2 * (levels - 1)], refs[-3:]
    index = lax.axis_index("gy")
    even = lax.rem(lax.axis_index("gx"), 2) == 0
    is_first = bit_of(index, 0) == 0
    low = jnp.where(is_first, 0.0, edge_block(other, 1))
    high = jnp.where(is_first, edge_block(other, 0), 0.0)
    ones = ONE_ROWS
    for level in range(1, levels):
        own, received = exchanged[2 * level - 2 : 2 * level]
        ones = ONE_ROWS << (level - 1)
        facing = received[ones : ones + EDGE_ROWS, :]
        below = bits_below(index, level)
        upper = bit_of(index, level) == 1
        low = jnp.where(upper & (below == 0), facing, low)
        high = jnp.where(~upper & (below == (1 << level) - 1), facing, high)
        if level == levels - 1:
            ones_out[...] = in_order(~upper, own[0:ones, :], received[0:ones, :])
    leaf = block[ONE_ROWS : ONE_ROWS + LEAF_ROWS, :]
    for piece, rows in enumerate((low[0:LEAF_ROWS], leaf, high[0:LEAF_ROWS])):
        for out in (even_out, odd_out):
            out[LEAF_ROWS * piece : LEAF_ROWS * (piece + 1), :] = rows
    for c in range(4):
        columns = []
        for x in range(CX):
            row = LEAF_ROWS + (c * CX + x) * ROWS
            own = [block[part_row(c, x, y) : part_row(c, x, y) + ROWS, :] for y in range(CY)]
            columns.append([low[row : row + ROWS], *own, high[row : row + ROWS]])
        for y in range(4):
            span = slice(row_part(c, y), row_part(c, y) + ROWS)
            even_out[span, :] = jnp.where(even, columns[1][y], columns[0][y])
            odd_out[span, :] = jnp.where(even, columns[0][y], columns[1][y])


def row_call(levels, operands):
    ones = jax.ShapeDtypeStruct((ONE_ROWS << (levels - 1), 128), F32)
    payload = jax.ShapeDtypeStruct((ROW_LEAF + ROW_PART, 128), F32)
    return pl.pallas_call(
        lambda *refs: row_kernel(levels, *refs[: 2 * levels], *refs[-3:]),
        out_shape=(ones, payload, payload),
        in_specs=[VMEM] * len(operands),
        out_specs=(VMEM,) * 3,
        compiler_params=pltpu.CompilerParams(vmem_limit_bytes=8 * MIB),
        cost_estimate=pl.CostEstimate(flops=100_000, bytes_accessed=600_000, transcendentals=0),
        name="row",
    )(*operands)


def merge_call(bit, own, other, after):
    def kernel(own_ref, other_ref, after_ref, out):
        is_first = bit_of(lax.axis_index("gx"), bit) == 0
        out[...] = in_order(is_first, own_ref[...], other_ref[...])

    return pack_call(kernel, 2 * own.shape[0], (own, other, after), "merge")


def own_kernel(block, after, out, targets, wide_ref, charge_ref):
    near = Near(wide_ref, charge_ref, targets)

    def raw(x, y):
        return lambda c: block[part_row(c, x, y) : part_row(c, x, y) + ROWS, :]

    columns = [column(raw(ab // 2, ab % 2), ab // 2 + 1, ab % 2 + 1) for ab in range(4)]
    near.targets(columns)
    plan = plan_own(near, columns)

    def emit(ab, j, row):
        out[ab, pl.ds(j, 1), :] = row

    near.run(plan, emit)


def beside_y_kernel(even_ref, odd_ref, targets, before, out, wide_ref, charge_ref):
    even = lax.rem(lax.axis_index("gx"), 2) == 0
    near = Near(wide_ref, charge_ref, targets)

    def raw(x, y):
        def read(c):
            span = slice(row_part(c, y), row_part(c, y) + ROWS)
            return jnp.where(even == (x == 1), even_ref[span, :], odd_ref[span, :])

        return read

    columns = [[column(raw(x, y), x + 1, y) for x in range(2)] for y in (0, 3)]
    plan = plan_beside_y(near, columns)
    out[...] = before[...]

    def emit(ab, j, row):
        out[ab, pl.ds(j, 1), :] = out[ab, pl.ds(j, 1), :] + row

    near.run(plan, emit)


def beside_x_kernel(parity, received, targets, before, after, out, wide_ref, charge_ref):
    index, count = lax.axis_index("gx"), lax.axis_size("gx")
    even = lax.rem(index, 2) == 0
    side = jnp.where(even == (parity == 0), 1, 0)
    alone = (index == 0) | (index == count - 1) if parity == 1 else None
    near = Near(wide_ref, charge_ref, targets)

    def raw(y):
        def read(c):
            value = received[row_part(c, y) : row_part(c, y) + ROWS, :]
            return jnp.where(alone, 0.0, value) if c == 3 and alone is not None else value

        return read

    columns = [column(raw(y), 3.0 * side.astype(F32), y) for y in range(4)]
    plan = plan_beside_x(near, columns, side)
    out[...] = before[...]

    def emit(ab, j, row):
        out[ab, pl.ds(j, 1), :] = out[ab, pl.ds(j, 1), :] + row

    near.run(plan, emit)


def near_call(kernel, operands, groups, charges, pairs, name, with_targets=False):
    out_shape = jax.ShapeDtypeStruct(NEAR_SHAPE, F32)
    if with_targets:
        out_shape = out_shape, jax.ShapeDtypeStruct((4, ROWS, 128, FEATURES), BF16)
    return pl.pallas_call(
        kernel,
        out_shape=out_shape,
        in_specs=[VMEM] * len(operands),
        out_specs=(VMEM, VMEM) if with_targets else VMEM,
        scratch_shapes=near_scratch(groups, charges),
        compiler_params=pltpu.CompilerParams(vmem_limit_bytes=12 * MIB),
        cost_estimate=near_cost(pairs),
        name=name,
    )(*operands)


def finish_kernel(count_x, count_y, refs):
    (own_block, even_ref, odd_ref, from_even, from_odd, own_ones, other_ones, near_rows), refs = refs[:8], refs[8:]
    constants, refs = refs[:3], refs[3:]
    out, refs = refs[0], refs[1:]
    small, flips, tiles, level_one, level_two, boxes, flipped, sums, local, semaphores = refs

    index_x, index_y = lax.axis_index("gx"), lax.axis_index("gy")
    is_even = lax.rem(index_x, 2) == 0
    pairs_y = count_y // 2
    has_low = index_x > 0
    has_high = index_x < count_x - 1
    fetches = [
        pltpu.make_async_copy(constant, place, semaphores.at[k])
        for k, (constant, place) in enumerate(zip(constants, (small, flips, tiles)))
    ]
    for fetch in fetches:
        fetch.start()

    fetches[0].wait()
    level_one[...] = jnp.zeros_like(level_one)
    level_two[...] = jnp.zeros_like(level_two)
    half_x = count_x // 2
    lower = index_x < half_x
    for x in range(half_x):
        for pair in range(pairs_y):
            row = 8 * (x * pairs_y + pair)
            one, two = own_ones[row : row + 8, :], other_ones[row : row + 8, :]
            level_one[x + 2, pair + 1] = jnp.where(lower, one, two)
            level_one[x + half_x + 2, pair + 1] = jnp.where(lower, two, one)
    children = jnp.concatenate(
        [
            jnp.concatenate([level_one[2 * x + 2, y + 1], level_one[2 * x + 3, y + 1]], 1)
            for x in range(half_x)
            for y in range(pairs_y)
        ],
        0,
    )
    below = half_x * pairs_y * 8
    low_lanes = lanes((4, 128)) < 64
    sums[0:below, :] = dot_three(children, small[0:256], small[256:512])
    for x in range(half_x):
        for y in range(pairs_y):
            row = (x * pairs_y + y) * 8
            even = sums[pl.ds(row, 4, stride=2), :]
            odd = sums[pl.ds(row + 1, 4, stride=2), :]
            level_two[x + 2, y + 2, 0:4] = jnp.where(low_lanes, even + lane_flip(odd), 0.0)

    def second_group(group_x, group_y):
        return jnp.concatenate(
            [
                level_two[2 * group_x + h + 2, 2 * group_y + 2]
                + lane_flip(level_two[2 * group_x + h + 2, 2 * group_y + 3])
                for h in range(2)
            ],
            1,
        )

    quarter_x, quarter_y = index_x // 4, index_y // 4
    tops = [(x, y) for x in range(count_x // 4) for y in range(count_y // 4)]
    stacked = jnp.concatenate([second_group(x, y) for x, y in tops], 0)
    if stacked.shape[0] % 16 != 0:
        stacked = jnp.concatenate([stacked, jnp.zeros((8, 256), F32)], 0)
    sums[0 : stacked.shape[0], :] = dot_three(stacked, small[0:256], small[256:512])
    top_far = jnp.zeros((16, 128), F32)
    for position, (x, y) in enumerate(tops):
        even = sums[pl.ds(8 * position, 2, stride=2), :]
        odd = sums[pl.ds(8 * position + 1, 2, stride=2), :]
        third = jnp.where(lanes((2, 128)) < 64, even + lane_flip(odd), 0.0)
        third = third[0:1] + lane_flip(third)[1:2]
        step_x, step_y = x - quarter_x + count_x // 4 - 1, y - quarter_y + count_y // 4 - 1
        row = 1536 + 256 * (step_x * (count_y // 4 * 2 - 1) + step_y)
        table = [small[pl.ds(pl.multiple_of(row + 128 * k, 128), 128), :] for k in range(2)]
        top_far = top_far + dot_three(jnp.broadcast_to(third, (16, 128)), table[0], table[1])

    fetches[1].wait()
    boxes[...] = jnp.zeros_like(boxes)
    for gx in (-1, 0, 1):
        for gy in (-1, 0, 1):
            for h in range(2):
                rows = slice(LEAF_ROWS * (gy + 1) + 16 * h, LEAF_ROWS * (gy + 1) + 16 * h + 16)
                if gx == 0:
                    moments = even_ref[rows, :]
                else:
                    moments = jnp.where(is_even == (gx == 1), from_even[rows, :], from_odd[rows, :])
                    moments = jnp.where(has_low if gx < 0 else has_high, moments, 0.0)
                span = slice(128 * h, 128 * h + 128)
                boxes[8:24, span] = moments
                boxes[32:40, span] = level_one[
                    2 * (index_x // 2 + gx) + h + 2, index_y // 2 + gy + 1
                ]
            boxes[48:56, :] = second_group(quarter_x + gx, quarter_y + gy)
            high, low = halves(boxes[...])
            table = flips[2 * (gx < 0) + (gy < 0)]
            mixed = dot(jnp.concatenate([high, low], 0), table)
            group = 3 * (gx + 1) + gy + 1
            for z in range(2):
                flipped[group, z, 0] = mixed[:64, 256 * z : 256 * z + 256]
                flipped[group, z, 1] = mixed[64:, 256 * z : 256 * z + 256]

    fetches[2].wait()
    odd_row = lax.rem(sublanes((32, 256)), 2) == 1
    totals = {}
    for position, (cx, cy, cz) in enumerate(canonical_tiles()):
        entries = [
            (gx, gy, dz)
            for gx in sorted({cx, -cx})
            for gy in sorted({cy, -cy})
            for dz in sorted({cz, -cz})
        ]
        pieces = [[], []]
        for gx, gy, dz in entries:
            group = 3 * (gx + 1) + gy + 1
            for part in range(2):
                view = flipped.at[group, int(dz < 0), part]
                block = jnp.concatenate(
                    [view[8 + dz : 24 + dz, :], view[32 + dz : 40 + dz, :], view[48 + dz : 56 + dz, :]],
                    0,
                )
                if abs(dz) == 3:
                    block = jnp.where(odd_row if dz < 0 else ~odd_row, block, 0.0)
                pieces[part].append(block.astype(BF16))
        rows = 32 * len(entries)
        both = dot(jnp.concatenate(pieces[0] + pieces[1], 0), tiles[position, 0])
        result = both[:rows] + both[rows:] + dot(jnp.concatenate(pieces[0], 0), tiles[position, 1])
        for order, (gx, gy, dz) in enumerate(entries):
            key = (int(gx < 0), int(gy < 0), int(dz < 0))
            piece = result[32 * order : 32 * order + 32]
            totals[key] = totals[key] + piece if key in totals else piece
    far = None
    for (fx, fy, fz), total in totals.items():
        if (fx, fy, fz) != (0, 0, 0):
            high, low = halves(total)
            table = flips[2 * fx + fy, :, 256 * fz : 256 * fz + 256]
            both = dot(jnp.concatenate([high, low], 0), table)
            total = both[:32] + both[32:]
        far = total if far is None else far + total

    def select(block, hx, hy):
        tile = jnp.where(hx == 1, block[:, 128:256], block[:, 0:128])
        return jnp.where(hy == 1, lane_flip(tile), tile)

    def refine(parent):
        keep = lanes((16, 128)) < 64
        parent = jnp.where(keep, parent, 0.0)
        high = parent.astype(BF16).astype(F32)
        low = parent - high
        left = jnp.concatenate([high + lane_flip(low), high], 1).astype(BF16)
        down = jnp.concatenate([small[512 + 256 * k : 768 + 256 * k, :] for k in range(4)], 1)
        spread = dot(left, down)
        for half in range(2):
            for h in range(2):
                span = slice(256 * half + 128 * h, 256 * half + 128 * h + 128)
                local[h, pl.ds(half, 16, stride=2), :] = spread[:, span]
        return jnp.concatenate([local[0], local[1]], 1)

    top_local = jnp.where(
        sublanes((16, 128)) == 0, top_far, jnp.where(sublanes((16, 128)) == 1, lane_flip(top_far), 0.0)
    )
    children_far = refine(top_local)
    half_index_x, half_index_y = index_x // 2, index_y // 2
    second = select(children_far[0:8], lax.rem(half_index_x, 2), lax.rem(half_index_y, 2))
    second = second + 0.25 * select(far[24:32], lax.rem(half_index_x, 2), lax.rem(half_index_y, 2))
    zeros = jnp.zeros((8, 128), F32)
    children_far = refine(jnp.concatenate([second, zeros], 0))
    first = select(children_far[0:8], lax.rem(index_x, 2), lax.rem(index_y, 2))
    first = first + 0.5 * select(far[16:24], lax.rem(index_x, 2), lax.rem(index_y, 2))
    leaf = refine(jnp.concatenate([first, zeros], 0))[0:16] + far[0:16]

    one, two = halves(leaf)
    turned = jnp.concatenate([one.astype(F32), two.astype(F32)], 0).T.astype(BF16)
    table = leaf_segments(2 * LZ)
    tables = basis_rows()
    for x in range(CX):
        for y in range(CY):
            column = x * CY + y
            spread = dot(turned[64 * column : 64 * column + 64], table)
            for j in range(ROWS):
                span = slice(128 * j, 128 * j + 128)
                places = [part_row(c, x, y) + j for c in range(3)]
                rows = [own_block[place : place + 1, :] for place in places]
                basis = basis_tile(*rows, None, tables)
                total = None
                for k in range(8):
                    term = basis[k] * spread[8 * k : 8 * k + 8, span]
                    total = term if total is None else total + term
                value = jnp.sum(total, 0, keepdims=True) + near_rows[column, j : j + 1, :]
                out[x, y : y + 1, span] = value


def finish_call(count_x, count_y, operands, constants):
    half_x, half_y = count_x // 2, count_y // 2
    scratch = [
        *[pltpu.VMEM(constant.shape, BF16) for constant in constants],
        pltpu.VMEM((count_x + 4, half_y + 2, 8, 128), F32),
        pltpu.VMEM((half_x + 4, half_y + 4, 8, 128), F32),
        pltpu.VMEM((64, 256), F32),
        pltpu.VMEM((9, 2, 2, 64, 256), F32),
        pltpu.VMEM((max(16, half_x * half_y * 8), 128), F32),
        pltpu.VMEM((2, 32, 128), F32),
        pltpu.SemaphoreType.DMA((3,)),
    ]
    return pl.pallas_call(
        lambda *refs: finish_kernel(count_x, count_y, refs),
        out_shape=jax.ShapeDtypeStruct((CX, CY, LZ * 64), F32),
        in_specs=[VMEM] * len(operands) + [HBM] * 3,
        out_specs=VMEM,
        scratch_shapes=scratch,
        compiler_params=pltpu.CompilerParams(vmem_limit_bytes=24 * MIB),
        name="finish",
    )(*operands, *constants)


def in_hbm(value):
    return pltpu.with_memory_space_constraint(value, pltpu.HBM)


def swap_bit(value, axis, bit):
    return lax.ppermute(value, axis, [(i, i ^ (1 << bit)) for i in range(lax.axis_size(axis))])


def swap_odd_even(value, axis):
    count = lax.axis_size(axis)
    partner = [i if i in (0, count - 1) else (i + 1 if i % 2 == 1 else i - 1) for i in range(count)]
    return lax.ppermute(value, axis, list(enumerate(partner)))


def solution(mesh):
    count_x, count_y = mesh.shape["gx"], mesh.shape["gy"]
    levels_x, levels_y = count_x.bit_length() - 1, count_y.bit_length() - 1
    tables = small_tables(count_x // 4, count_y // 4), reflection_tables(), translation_tiles()

    def body(offsets, charges):
        constants = [in_hbm(jnp.asarray(table)) for table in tables]
        block = moments_call(in_hbm(offsets), in_hbm(charges), constants[0])
        other = swap_bit(block, "gy", 0)
        pair = block, other
        exchanged = []
        for level in range(1, levels_y):
            last = level == levels_y - 1
            rows = (ONE_ROWS << (level - 1)) + EDGE_ROWS * (1 if last else 2)
            sent = pack_call(functools.partial(group_kernel, level, last), rows, pair, "group")
            pair = sent, swap_bit(sent, "gy", level)
            exchanged += pair
        near, targets = near_call(own_kernel, (block, sent), 8, 8, 4_500_000, "near_own", True)
        ones, even, odd = row_call(levels_y, (block, other, *exchanged, near))
        other_ones = swap_bit(ones, "gx", 0)
        from_even = swap_bit(even, "gx", 0)
        from_odd = swap_odd_even(odd, "gx")
        near = near_call(beside_y_kernel, (even, odd, targets, near), 8, 8, 2_200_000, "near_y")
        for bit in range(levels_x - 1):
            ones = merge_call(bit, ones, other_ones, near)
            other_ones = swap_bit(ones, "gx", bit + 1)
            if bit < 2:
                side = functools.partial(beside_x_kernel, bit)
                operands = (from_even if bit == 0 else from_odd, targets, near, ones)
                near = near_call(side, operands, 8, 10, 1_200_000, "near_x")
        operands = (block, even, odd, from_even, from_odd, ones, other_ones, near)
        return finish_call(count_x, count_y, operands, constants)

    in_specs = (P(None, "gx", "gy", None), P("gx", "gy", None))
    out_specs = P("gx", "gy", None)
    return jax.shard_map(body, mesh=mesh, in_specs=in_specs, out_specs=out_specs, check_vma=False)
```

```python
import functools
import itertools

import jax
import jax.numpy as jnp
import ml_dtypes
import numpy as np
from jax import lax
from jax.experimental import pallas as pl
from jax.experimental.pallas import tpu as pltpu
from jax.sharding import PartitionSpec as P

F32 = jnp.float32
BF16 = jnp.bfloat16
MIB = 1 << 20

CX = 2
CY = 2
LZ = 16
ROWS = 8
FEATURES = 32
VMEM = pl.BlockSpec(memory_space=pltpu.VMEM)
HBM = pl.BlockSpec(memory_space=pltpu.HBM)


def nodes_1d():
    return np.cos((2.0 * np.arange(4) + 1.0) * np.pi / 8.0)


def cheb_terms(value):
    return value, 2.0 * value * value - 1.0, 4.0 * value**3 - 3.0 * value


def node_weights():
    return [[0.5 * term for term in cheb_terms(point)] for point in nodes_1d()]


def node_grid():
    points = nodes_1d()
    counter = np.arange(64)
    return np.stack([points[counter // 16], points[counter // 4 % 4], points[counter % 4]], -1)


def split_two(table):
    high = table.astype(np.float32).astype(ml_dtypes.bfloat16)
    low = (table - high.astype(np.float64)).astype(np.float32).astype(ml_dtypes.bfloat16)
    return high, low


def upward_tensor():
    points = nodes_1d()
    shifted = (points[None, :] + 2.0 * np.arange(2)[:, None] - 1.0) / 2.0
    factor = 0.25 + 0.0 * shifted[..., None]
    for of_value, of_node in zip(cheb_terms(shifted), cheb_terms(points)):
        factor = factor + 0.5 * of_value[..., None] * of_node
    full = np.einsum("xia,yjb,zkc->xyzijkabc", factor, factor, factor)
    return full.reshape(2, 2, 2, 64, 64)


def inverse_distance(offset):
    grid = node_grid()
    spread = (grid[None, :, :] - grid[:, None, :]) / 2.0 - np.asarray(offset, np.float64)
    return 1.0 / np.sqrt(np.sum(spread * spread, -1))


def adjacent(offset):
    return max(abs(int(step)) for step in offset) <= 1


def canonical_tiles():
    return [
        (cx, cy, cz)
        for cx in range(2)
        for cy in range(2)
        for cz in range(4)
        if not (cx == 0 and cy == 0 and cz <= 1)
    ]


TILES_FIRST = 10


def translation_tiles():
    tiles = []
    for cx, cy, cz in canonical_tiles():
        tile = np.zeros((4, 64, 4, 64))
        for source in range(4):
            for target in range(4):
                offset = (
                    2 * cx + source // 2 - target // 2,
                    2 * cy + source % 2 - target % 2,
                    cz,
                )
                if not adjacent(offset):
                    tile[source, :, target, :] = inverse_distance(offset)
        tiles.append(tile.reshape(256, 256))
    return np.stack(split_two(np.stack(tiles)), 1)


def reflection_matrix(flip_x, flip_y, flip_z):
    index = np.arange(256)
    hx, hy, a, b, c = index // 128, index // 64 % 2, index // 16 % 4, index // 4 % 4, index % 4
    if flip_x:
        hx, a = 1 - hx, 3 - a
    if flip_y:
        hy, b = 1 - hy, 3 - b
    if flip_z:
        c = 3 - c
    matrix = np.zeros((256, 256), np.float32)
    matrix[hx * 128 + hy * 64 + a * 16 + b * 4 + c, index] = 1.0
    return matrix


def reflection_tables():
    pairs = [
        np.concatenate([reflection_matrix(fx, fy, 0), reflection_matrix(fx, fy, 1)], 1)
        for fx in range(2)
        for fy in range(2)
    ]
    return np.stack(pairs).astype(ml_dtypes.bfloat16)


def up_tables():
    upward = upward_tensor()
    table = upward.transpose(0, 1, 3, 2, 4).reshape(256, 128)
    return np.stack(split_two(table))


def down_table():
    upward = upward_tensor()
    table = upward.transpose(4, 2, 0, 1, 3).reshape(64, 512)
    high, low = split_two(table)
    return np.concatenate([high, high, low, np.zeros_like(low)], 0)


def top_tables(boxes_x, boxes_y):
    offsets = range(-(boxes_x - 1), boxes_x), range(-(boxes_y - 1), boxes_y)
    table = np.zeros((len(offsets[0]), len(offsets[1]), 2, 64, 2, 64))
    for (ix, dx), (iy, dy) in itertools.product(enumerate(offsets[0]), enumerate(offsets[1])):
        for source, target in itertools.product(range(2), range(2)):
            offset = (dx, dy, source - target)
            if not adjacent(offset):
                table[ix, iy, source, :, target, :] = 0.125 * inverse_distance(offset)
    return np.stack(split_two(table.reshape(len(offsets[0]), len(offsets[1]), 128, 128)), 2)


def small_tables(boxes_x, boxes_y):
    down = down_table().reshape(256, 4, 128).transpose(1, 0, 2)
    parts = [up_tables(), down, top_tables(boxes_x, boxes_y)]
    return np.concatenate([part.reshape(-1, 128) for part in parts], 0)


def halves(value):
    high = value.astype(BF16)
    return high, (value - high.astype(F32)).astype(BF16)


def dot(left, right):
    return jnp.dot(left, right, preferred_element_type=F32)


def dot_three(value, high_table, low_table):
    rows = value.shape[0]
    high, low = halves(value)
    both = dot(jnp.concatenate([high, low], 0), high_table)
    return both[:rows] + both[rows:] + dot(high, low_table)


def lanes(shape):
    return lax.broadcasted_iota(jnp.int32, shape, len(shape) - 1)


def sublanes(shape):
    return lax.broadcasted_iota(jnp.int32, shape, len(shape) - 2)


def leaf_segments(leaves):
    shape = (leaves, LZ * 64)
    return jnp.where(lanes(shape) // 64 == lax.rem(sublanes(shape), LZ), 1.0, 0.0).astype(BF16)


def lane_flip(value):
    return pltpu.roll(value, 64, 1)


def weight_rows(pattern):
    weights = node_weights()
    index = sublanes((8, 128))
    rows = []
    for term in range(3):
        row = jnp.full((8, 128), weights[pattern(0)][term], F32)
        for sub in range(1, 8):
            row = jnp.where(index == sub, weights[pattern(sub)][term], row)
        rows.append(row)
    return rows


def basis_rows():
    return (
        weight_rows(lambda sub: sub // 4),
        weight_rows(lambda sub: 2 + sub // 4),
        weight_rows(lambda sub: sub % 4),
    )


def basis_tile(row_x, row_y, row_z, scale, tables):
    y_low, y_high, z_all = tables
    wide = [jnp.broadcast_to(2.0 * row - 1.0, (8, 128)) for row in (row_x, row_y, row_z)]
    terms = [cheb_terms(value) for value in wide]

    def mix(weights, term):
        return 0.25 + (weights[0] * term[0] + weights[1] * term[1] + weights[2] * term[2])

    along_z = mix(z_all, terms[2])
    pair = mix(y_low, terms[1]) * along_z, mix(y_high, terms[1]) * along_z
    tiles = []
    for weights in node_weights():
        along_x = mix(weights, terms[0])
        if scale is not None:
            along_x = along_x * scale
        tiles += [along_x * pair[0], along_x * pair[1]]
    return tiles


def three_pieces(value):
    first = value.astype(BF16).astype(F32)
    rest = value - first
    second = rest.astype(BF16).astype(F32)
    return first, second, rest - second


PIECES = 12


def feature_pieces(coords, scale):
    total = coords[0] * coords[0] + coords[1] * coords[1] + coords[2] * coords[2]
    return [piece for value in [scale * coord for coord in coords] + [total] for piece in three_pieces(value)]


def pick(row, pieces, choice):
    value = jnp.broadcast_to(pieces[choice[0]], (8, 128))
    for piece in sorted(set(choice) - {choice[0]}):
        mask = None
        for place, chosen in enumerate(choice):
            if chosen == piece:
                mask = row == place if mask is None else mask | (row == place)
        value = jnp.where(mask, jnp.broadcast_to(pieces[piece], (8, 128)), value)
    return value


def feature_block(read, choice, length_choice):
    row = sublanes((8, 128))
    zero, one = jnp.zeros((1, 128), F32), jnp.ones((1, 128), F32)
    blocks = [
        pick(row, [read(3 * c), read(3 * c + 1), read(3 * c + 2), zero], choice) for c in range(3)
    ]
    blocks.append(pick(row, [read(9), read(10), read(11), one, zero], length_choice))
    return jnp.concatenate(blocks, 0)


SOURCE_CHOICE = (0, 1, 0, 1, 2, 0, 0, 0), (3, 3, 3, 0, 1, 2, 3, 3)
TARGET_CHOICE = (0, 0, 1, 1, 0, 2, 3, 3), (0, 1, 2, 3, 3, 3, 4, 4)


def column(raw, x, y):
    return raw(0) + (x - 2.0), raw(1) + (y - 2.0), raw(2), raw(3)


class Near:
    def __init__(self, wide_ref, charge_ref, target_ref):
        self.wide_ref = wide_ref
        self.charge_ref = charge_ref
        self.target_ref = target_ref
        self.groups = 0
        self.charges = 0
        self.upper = lanes((ROWS, 128)) >= 64
        self.row = sublanes((ROWS, 128))

    def in_pair(self, along_z):
        return along_z + jnp.where(self.upper, 0.0, -1.0)

    def targets(self, columns):
        for ab, (x, y, z, _) in enumerate(columns):
            pieces = feature_pieces((x, y, self.in_pair(z)), -2.0)
            for j in range(ROWS):
                block = feature_block(lambda k: pieces[k][j : j + 1], *TARGET_CHOICE)
                self.target_ref[ab, j] = block.T.astype(BF16)

    def add_group(self, coords):
        for k, piece in enumerate(feature_pieces(coords, 1.0)):
            self.wide_ref[self.groups, k] = piece
        self.groups += 1
        return self.groups - 1

    def add_charge(self, charge):
        self.charge_ref[self.charges] = charge
        self.charges += 1
        return self.charges - 1

    def main(self, source):
        x, y, z, charge = source
        return self.add_group((x, y, self.in_pair(z))), self.add_charge(charge)

    def outer(self, first, second, side, keep=False):
        def merge(one, two):
            if side == 0:
                value = jnp.where(self.upper, two, lane_flip(one))
                return pltpu.roll(value, 1, 0)
            value = jnp.where(self.upper, lane_flip(two), one)
            return pltpu.roll(value, ROWS - 1, 0)

        x, y, z, charge = [merge(one, two) for one, two in zip(first, second)]
        charge = jnp.where(self.row == (0 if side == 0 else ROWS - 1), 0.0, charge)
        group = self.add_group((x, y, z + (-2.0 if side == 0 else 1.0)))
        if not keep:
            return group, self.add_charge(charge)
        low = self.add_charge(jnp.where(self.upper, 0.0, charge))
        high = self.add_charge(jnp.where(self.upper, charge, 0.0))
        return (group, low), (group, high)

    def run(self, plan, emit):
        eye = sublanes((128, 128)) == lanes((128, 128))

        def source(group, j, built):
            if group not in built:
                read = lambda k: self.wide_ref[group, k, pl.ds(j, 1), :]
                built[group] = feature_block(read, *SOURCE_CHOICE).astype(BF16)
            return built[group]

        def pairs(targets, tiles, j, own, total, built):
            block = jnp.concatenate([source(group, j, built) for group, _ in tiles], 1)
            squared = dot(targets, block)
            for position, (group, charge) in enumerate(tiles):
                inverse = lax.rsqrt(squared[:, 128 * position : 128 * position + 128])
                if group == own:
                    inverse = jnp.where(eye, 0.0, inverse)
                total = total + inverse * self.charge_ref[charge, pl.ds(j, 1), :]
            return total

        def step(j, carry):
            built = {}
            for ab, mains, below, above, own in plan:
                targets = self.target_ref[ab, j]
                total = pairs(targets, mains, j, own, jnp.zeros((128, 128), F32), built)
                lower = pairs(targets[:64], below, j, None, total[:64], built)
                higher = pairs(targets[64:], above, j, None, total[64:], built)
                total = jnp.concatenate([lower, higher], 0)
                emit(ab, j, jnp.sum(total.T, 0, keepdims=True))
            return carry

        lax.fori_loop(0, ROWS, step, 0, unroll=True)


def plan_own(near, columns):
    mains = [near.main(source) for source in columns]
    outer = [
        [near.outer(columns[2 * x], columns[2 * x + 1], side) for x in range(2)]
        for side in range(2)
    ]
    return [(ab, mains, outer[0], outer[1], mains[ab][0]) for ab in range(4)]


def plan_beside_y(near, columns):
    plan = []
    for b in range(2):
        mains = [near.main(source) for source in columns[b]]
        outer = [[near.outer(*columns[b], side)] for side in range(2)]
        plan += [(2 * a + b, mains, outer[0], outer[1], None) for a in range(2)]
    return plan


def plan_beside_x(near, columns, side_x):
    mains = [near.main(source) for source in columns]
    middle = [near.outer(columns[1], columns[2], side) for side in range(2)]
    ends = [near.outer(columns[0], columns[3], side, keep=True) for side in range(2)]
    return [
        (2 * side_x + b, mains[b : b + 3], [middle[0], ends[0][b]], [middle[1], ends[1][b]], None)
        for b in range(2)
    ]


def near_scratch(groups, charges):
    return [
        pltpu.VMEM((groups, PIECES, ROWS, 128), F32),
        pltpu.VMEM((charges, ROWS, 128), F32),
    ]


NEAR_SHAPE = (4, ROWS, 128)


def near_cost(pairs):
    return pl.CostEstimate(flops=40 * pairs, bytes_accessed=600_000, transcendentals=pairs)


ONE_ROWS = 8
LEAF_ROWS = 32
PART_ROWS = 4 * CX * CY * ROWS
OWN_ROWS = ONE_ROWS + LEAF_ROWS + PART_ROWS


def part_row(c, x, y):
    return ONE_ROWS + LEAF_ROWS + ((c * CX + x) * CY + y) * ROWS


def moments_kernel(
    offsets_hbm, charges_hbm, small_hbm, block, offsets, charges, up, basis, sums, semaphores
):
    index_y = lax.axis_index("gy")
    copies = [
        pltpu.make_async_copy(offsets_hbm, offsets, semaphores.at[0]),
        pltpu.make_async_copy(charges_hbm, charges, semaphores.at[1]),
        pltpu.make_async_copy(small_hbm.at[0:512], up, semaphores.at[2]),
    ]
    for copy in copies:
        copy.start()
    tables = basis_rows()
    segments = leaf_segments(LZ)
    copies[0].wait()
    copies[1].wait()
    for x in range(CX):
        for y in range(CY):
            for j in range(ROWS):
                span = slice(128 * j, 128 * j + 128)
                rows = [offsets[c, x, y : y + 1, span] for c in range(3)]
                charge = charges[x, y : y + 1, span]
                for c, row in enumerate(rows + [charge]):
                    place = part_row(c, x, y) + j
                    block[place : place + 1, :] = row
                tiles = basis_tile(*rows, charge, tables)
                for k in range(4):
                    pair = jnp.concatenate(tiles[2 * k : 2 * k + 2], 0)
                    high, low = halves(pair)
                    first = (x * CY + y) * 64 + 16 * k
                    basis[0, first : first + 16, span] = high
                    basis[1, first : first + 16, span] = low
    contract = (((1,), (1,)), ((), ()))
    leaf = lax.dot_general(segments, basis[0], contract, preferred_element_type=F32)
    leaf = leaf + lax.dot_general(segments, basis[1], contract, preferred_element_type=F32)
    copies[2].wait()
    sums[...] = dot_three(leaf, up[0:256], up[256:512])
    first = sums[pl.ds(0, 8, stride=2), :] + lane_flip(sums[pl.ds(1, 8, stride=2), :])
    first = jnp.where(lanes((8, 128)) < 64, first, 0.0)
    first = jnp.where(lax.rem(index_y, 2) == 1, lane_flip(first), first)
    block[0:8, :] = first
    block[8:24, :] = leaf[:, :128]
    block[24:40, :] = leaf[:, 128:]


def moments_call(offsets, charges, small):
    return pl.pallas_call(
        moments_kernel,
        out_shape=jax.ShapeDtypeStruct((OWN_ROWS, 128), F32),
        in_specs=[HBM] * 3,
        out_specs=VMEM,
        scratch_shapes=[
            pltpu.VMEM(offsets.shape, F32),
            pltpu.VMEM(charges.shape, F32),
            pltpu.VMEM((512, 128), BF16),
            pltpu.VMEM((2, 256, 1024), BF16),
            pltpu.VMEM((16, 128), F32),
            pltpu.SemaphoreType.DMA((3,)),
        ],
        compiler_params=pltpu.CompilerParams(vmem_limit_bytes=8 * MIB),
        cost_estimate=pl.CostEstimate(flops=10_000_000, bytes_accessed=300_000, transcendentals=0),
        name="moments",
    )(offsets, charges, small)


EDGE_ROWS = LEAF_ROWS + 4 * CX * ROWS


def bits_below(index, bit):
    return lax.rem(index, 1 << bit)


def bit_of(index, bit):
    return lax.rem(index // (1 << bit), 2)


def in_order(is_first, own, other):
    return jnp.concatenate([jnp.where(is_first, own, other), jnp.where(is_first, other, own)], 0)


def edge_block(block, y):
    rows = [block[ONE_ROWS : ONE_ROWS + LEAF_ROWS, :]]
    for c in range(4):
        for x in range(CX):
            rows.append(block[part_row(c, x, y) : part_row(c, x, y) + ROWS, :])
    return jnp.concatenate(rows, 0)


def group_kernel(level, last_level, own_ref, other_ref, after, out):
    index = lax.axis_index("gy")
    ones = ONE_ROWS << (level - 1)
    is_first = bit_of(index, level - 1) == 0
    if level == 1:
        out[0:ones, :] = own_ref[0:ones, :] + other_ref[0:ones, :]
        first = jnp.where(is_first, edge_block(own_ref, 0), edge_block(other_ref, 0))
        last = jnp.where(is_first, edge_block(other_ref, 1), edge_block(own_ref, 1))
    else:
        half = ones // 2
        out[0:ones, :] = in_order(is_first, own_ref[0:half, :], other_ref[0:half, :])
        own_far = own_ref[half + EDGE_ROWS : half + 2 * EDGE_ROWS, :]
        other_far = other_ref[half + EDGE_ROWS : half + 2 * EDGE_ROWS, :]
        first = jnp.where(is_first, own_far, other_far)
        last = jnp.where(is_first, other_far, own_far)
    lower = bit_of(index, level) == 0
    out[ones : ones + EDGE_ROWS, :] = jnp.where(lower, last, first)
    if not last_level:
        out[ones + EDGE_ROWS : ones + 2 * EDGE_ROWS, :] = jnp.where(lower, first, last)


def pack_call(kernel, rows, operands, name):
    return pl.pallas_call(
        kernel,
        out_shape=jax.ShapeDtypeStruct((rows, 128), F32),
        in_specs=[VMEM] * len(operands),
        out_specs=VMEM,
        compiler_params=pltpu.CompilerParams(vmem_limit_bytes=8 * MIB),
        cost_estimate=pl.CostEstimate(flops=100_000, bytes_accessed=300_000, transcendentals=0),
        name=name,
    )(*operands)


ROW_LEAF = 3 * LEAF_ROWS
ROW_PART = 4 * 4 * ROWS
ROW_ROWS = ROW_LEAF + ROW_PART
ROW_BOTH = ROW_ROWS + ROW_PART


def row_part(c, y):
    return ROW_LEAF + (c * 4 + y) * ROWS


def row_kernel(levels, block, other, *refs):
    exchanged, (ones_out, out) = refs[: 2 * (levels - 1)], refs[-2:]
    index = lax.axis_index("gy")
    even = lax.rem(lax.axis_index("gx"), 2) == 0
    is_first = bit_of(index, 0) == 0
    low = jnp.where(is_first, 0.0, edge_block(other, 1))
    high = jnp.where(is_first, edge_block(other, 0), 0.0)
    ones = ONE_ROWS
    for level in range(1, levels):
        own, received = exchanged[2 * level - 2 : 2 * level]
        ones = ONE_ROWS << (level - 1)
        facing = received[ones : ones + EDGE_ROWS, :]
        below = bits_below(index, level)
        upper = bit_of(index, level) == 1
        low = jnp.where(upper & (below == 0), facing, low)
        high = jnp.where(~upper & (below == (1 << level) - 1), facing, high)
        if level == levels - 1:
            ones_out[...] = in_order(~upper, own[0:ones, :], received[0:ones, :])
    leaf = block[ONE_ROWS : ONE_ROWS + LEAF_ROWS, :]
    for piece, rows in enumerate((low[0:LEAF_ROWS], leaf, high[0:LEAF_ROWS])):
        out[LEAF_ROWS * piece : LEAF_ROWS * (piece + 1), :] = rows
    for c in range(4):
        columns = []
        for x in range(CX):
            row = LEAF_ROWS + (c * CX + x) * ROWS
            own = [block[part_row(c, x, y) : part_row(c, x, y) + ROWS, :] for y in range(CY)]
            columns.append([low[row : row + ROWS], *own, high[row : row + ROWS]])
        for y in range(4):
            facing, far = row_part(c, y), row_part(c, y) + ROW_PART
            out[facing : facing + ROWS, :] = jnp.where(even, columns[1][y], columns[0][y])
            out[far : far + ROWS, :] = jnp.where(even, columns[0][y], columns[1][y])


def row_call(levels, operands):
    return pl.pallas_call(
        lambda *refs: row_kernel(levels, *refs[: 2 * levels], *refs[-2:]),
        out_shape=[
            jax.ShapeDtypeStruct((rows, 128), F32) for rows in (ONE_ROWS << (levels - 1), ROW_BOTH)
        ],
        in_specs=[VMEM] * len(operands),
        out_specs=[VMEM] * 2,
        compiler_params=pltpu.CompilerParams(vmem_limit_bytes=8 * MIB),
        cost_estimate=pl.CostEstimate(flops=100_000, bytes_accessed=600_000, transcendentals=0),
        name="row",
    )(*operands)


def merge_call(bit, own, other, after):
    def kernel(own_ref, other_ref, after_ref, out):
        is_first = bit_of(lax.axis_index("gx"), bit) == 0
        out[...] = in_order(is_first, own_ref[...], other_ref[...])

    return pack_call(kernel, 2 * own.shape[0], (own, other, after), "merge")


def hand_on_call(halo, after):
    def kernel(halo_ref, after_ref, out):
        out[...] = halo_ref[...]

    return pack_call(kernel, halo.shape[0], (halo, after), "hand_on")


def relay_call(received, after):
    def kernel(received_ref, after_ref, out):
        out[0:ROW_LEAF, :] = received_ref[0:ROW_LEAF, :]
        out[ROW_LEAF:ROW_ROWS, :] = received_ref[ROW_ROWS:ROW_BOTH, :]

    return pack_call(kernel, ROW_ROWS, (received, after), "relay")


def own_kernel(block, targets, features, charges):
    near = Near(features, charges, targets)

    def raw(x, y):
        return lambda c: block[part_row(c, x, y) : part_row(c, x, y) + ROWS, :]

    columns = [column(raw(ab // 2, ab % 2), ab // 2 + 1, ab % 2 + 1) for ab in range(4)]
    near.targets(columns)
    return near, plan_own(near, columns)


def own_call(block, after, small, tiles):
    plans = []

    def prepare(block_ref, small, targets, features, charges, small_out, semaphore):
        copy = pltpu.make_async_copy(small, small_out, semaphore)
        copy.start()
        plans.append(own_kernel(block_ref, targets, features, charges)[1])
        copy.wait()

    def run(targets, features, charges, after_ref, tiles, out, tiles_out, semaphore):
        copy = pltpu.make_async_copy(tiles, tiles_out, semaphore)
        copy.start()

        def emit(ab, j, row):
            out[ab, pl.ds(j, 1), :] = row

        Near(features, charges, targets).run(plans[0], emit)
        copy.wait()

    prepared = pl.pallas_call(
        prepare,
        out_shape=(
            jax.ShapeDtypeStruct((4, ROWS, 128, FEATURES), BF16),
            jax.ShapeDtypeStruct((8, PIECES, ROWS, 128), F32),
            jax.ShapeDtypeStruct((8, ROWS, 128), F32),
            jax.ShapeDtypeStruct(small.shape, BF16),
        ),
        in_specs=[VMEM, HBM],
        out_specs=(VMEM,) * 4,
        scratch_shapes=[pltpu.SemaphoreType.DMA],
        compiler_params=pltpu.CompilerParams(vmem_limit_bytes=8 * MIB),
        cost_estimate=near_cost(500_000),
        name="features",
    )(block, small)
    near, tiles_near = pl.pallas_call(
        run,
        out_shape=(
            jax.ShapeDtypeStruct(NEAR_SHAPE, F32),
            jax.ShapeDtypeStruct(tiles.shape, BF16),
        ),
        in_specs=[VMEM] * 4 + [HBM],
        out_specs=(VMEM,) * 2,
        scratch_shapes=[pltpu.SemaphoreType.DMA],
        compiler_params=pltpu.CompilerParams(vmem_limit_bytes=8 * MIB),
        cost_estimate=near_cost(4_500_000),
        name="near_own",
    )(*prepared[:3], after(prepared[2]), tiles)
    return near, prepared[0], prepared[3], tiles_near


def beside_y_kernel(
    row_ref, targets, before, flips, tiles, out, flips_out, tiles_out, wide_ref, charge_ref, semaphores
):
    copies = [
        pltpu.make_async_copy(flips, flips_out, semaphores.at[0]),
        pltpu.make_async_copy(tiles, tiles_out, semaphores.at[1]),
    ]
    for copy in copies:
        copy.start()
    even = lax.rem(lax.axis_index("gx"), 2) == 0
    near = Near(wide_ref, charge_ref, targets)

    def raw(x, y):
        def read(c):
            facing, far = row_part(c, y), row_part(c, y) + ROW_PART
            own = row_ref[facing : facing + ROWS, :], row_ref[far : far + ROWS, :]
            return jnp.where(even == (x == 1), *own)

        return read

    columns = [[column(raw(x, y), x + 1, y) for x in range(2)] for y in (0, 3)]
    plan = plan_beside_y(near, columns)
    out[...] = before[...]

    def emit(ab, j, row):
        out[ab, pl.ds(j, 1), :] = out[ab, pl.ds(j, 1), :] + row

    near.run(plan, emit)
    for copy in copies:
        copy.wait()


def beside_y_call(row, targets, before, constants):
    near_shape = jax.ShapeDtypeStruct(NEAR_SHAPE, F32)
    tables = [jax.ShapeDtypeStruct(constant.shape, BF16) for constant in constants]
    return pl.pallas_call(
        beside_y_kernel,
        out_shape=(near_shape, *tables),
        in_specs=[VMEM] * 3 + [HBM] * 2,
        out_specs=(VMEM,) * 3,
        scratch_shapes=near_scratch(8, 8) + [pltpu.SemaphoreType.DMA((2,))],
        compiler_params=pltpu.CompilerParams(vmem_limit_bytes=8 * MIB),
        cost_estimate=near_cost(2_200_000),
        name="near_y",
    )(row, targets, before, *constants)


def beside_x(parity, received, targets, out, wide_ref, charge_ref):
    index, count = lax.axis_index("gx"), lax.axis_size("gx")
    even = lax.rem(index, 2) == 0
    side = jnp.where(even == (parity == 0), 1, 0)
    alone = (index == 0) | (index == count - 1)
    near = Near(wide_ref, charge_ref, targets)

    def raw(y):
        def coordinate(c):
            value = received[row_part(c, y) : row_part(c, y) + ROWS, :]
            return jnp.where(alone, 0.0, value) if c == 3 and parity == 1 else value

        return coordinate

    columns = [column(raw(y), 3.0 * side.astype(F32), y) for y in range(4)]
    plan = plan_beside_x(near, columns, side)

    def emit(ab, j, row):
        out[ab, pl.ds(j, 1), :] = out[ab, pl.ds(j, 1), :] + row

    near.run(plan, emit)


def beside_x_kernel(received, targets, before, after, out, wide_ref, charge_ref):
    out[...] = before[...]
    beside_x(0, received, targets, out, wide_ref, charge_ref)


def near_call(kernel, operands, groups, charges, pairs, name):
    return pl.pallas_call(
        kernel,
        out_shape=jax.ShapeDtypeStruct(NEAR_SHAPE, F32),
        in_specs=[VMEM] * len(operands),
        out_specs=VMEM,
        scratch_shapes=near_scratch(groups, charges),
        compiler_params=pltpu.CompilerParams(vmem_limit_bytes=12 * MIB),
        cost_estimate=near_cost(pairs),
        name=name,
    )(*operands)


def store_reflected(boxes, flips, flipped, gx, gy):
    high, low = halves(boxes[...])
    rows = high.shape[0]
    mixed = dot(jnp.concatenate([high, low], 0), flips[2 * (gx < 0) + (gy < 0)])
    for z in range(2):
        flipped[gx + 1, gy + 1, z, 0] = mixed[:rows, 256 * z : 256 * z + 256]
        flipped[gx + 1, gy + 1, z, 1] = mixed[rows:, 256 * z : 256 * z + 256]


def far_sums(columns, spans, flipped, flips, tiles):
    odd_row = lax.rem(sublanes((16, 256)), 2) == 1
    totals = {}
    for position, (cx, cy, cz) in enumerate(canonical_tiles()):
        entries = [
            (gx, gy, dz)
            for gx in sorted({cx, -cx})
            for gy in sorted({cy, -cy})
            for dz in sorted({cz, -cz})
            if gx in columns
        ]
        if not entries:
            continue
        pieces = [[], []]
        for gx, gy, dz in entries:
            for part in range(2):
                view = flipped.at[gx + 1, gy + 1, int(dz < 0), part]
                windows = [view[first + dz : first + dz + size, :] for first, size in spans]
                block = jnp.concatenate(windows, 0)
                if abs(dz) == 3:
                    block = jnp.where(odd_row if dz < 0 else ~odd_row, block, 0.0)
                pieces[part].append(block.astype(BF16))
        rows = 16 * len(entries)
        part = tiles[0] if position < TILES_FIRST else tiles[1]
        tile = part.at[position % TILES_FIRST]
        both = dot(jnp.concatenate(pieces[0] + pieces[1], 0), tile[0])
        result = both[:rows] + both[rows:] + dot(jnp.concatenate(pieces[0], 0), tile[1])
        for order, (gx, gy, dz) in enumerate(entries):
            key = (int(gx < 0), int(gy < 0), int(dz < 0))
            piece = result[16 * order : 16 * order + 16]
            totals[key] = totals[key] + piece if key in totals else piece
    far = None
    for (fx, fy, fz), total in totals.items():
        if (fx, fy, fz) != (0, 0, 0):
            high, low = halves(total)
            table = flips[2 * fx + fy, :, 256 * fz : 256 * fz + 256]
            both = dot(jnp.concatenate([high, low], 0), table)
            total = both[:16] + both[16:]
        far = total if far is None else far + total
    return far


def leaf_far(columns, halos, flips, tiles, boxes, flipped):
    index, count = lax.axis_index("gx"), lax.axis_size("gx")
    is_even = lax.rem(index, 2) == 0
    boxes[...] = jnp.zeros_like(boxes)
    for gx in columns:
        for gy in (-1, 0, 1):
            for h in range(2):
                row = LEAF_ROWS * (gy + 1) + 16 * h
                rows = slice(row, row + 16)
                moments = halos[0][rows, :]
                if gx != 0:
                    moments = jnp.where(is_even == (gx == 1), moments, halos[1][rows, :])
                    inside = index > 0 if gx < 0 else index < count - 1
                    moments = jnp.where(inside, moments, 0.0)
                boxes[8:24, 128 * h : 128 * h + 128] = moments
            store_reflected(boxes, flips, flipped, gx, gy)
    return far_sums(columns, ((8, 16),), flipped, flips, tiles)


LEAF_SCRATCH = [pltpu.VMEM((32, 256), F32), pltpu.VMEM((3, 3, 2, 2, 32, 256), F32)]


def far_own_call(row, flips, tiles, after):
    def kernel(row_ref, flips_ref, tiles_ref, after_ref, out, boxes, flipped):
        out[...] = leaf_far((0,), (row_ref,), flips_ref, (tiles_ref,), boxes, flipped)

    return pl.pallas_call(
        kernel,
        out_shape=jax.ShapeDtypeStruct((LZ, 256), F32),
        in_specs=[VMEM] * 4,
        out_specs=VMEM,
        scratch_shapes=LEAF_SCRATCH,
        compiler_params=pltpu.CompilerParams(vmem_limit_bytes=8 * MIB),
        cost_estimate=pl.CostEstimate(flops=500_000_000, bytes_accessed=600_000, transcendentals=0),
        name="far_own",
    )(row, flips, tiles, after)


def upper_kernel(count_x, count_y, refs):
    own_ones, other_ones, small, flips, *tiles, _, out = refs[:8]
    refs = refs[8:]
    level_one, level_two, boxes, flipped, sums, local = refs

    index_x, index_y = lax.axis_index("gx"), lax.axis_index("gy")
    pairs_y = count_y // 2

    level_one[...] = jnp.zeros_like(level_one)
    level_two[...] = jnp.zeros_like(level_two)
    half_x = count_x // 2
    lower = index_x < half_x
    for x in range(half_x):
        for pair in range(pairs_y):
            row = 8 * (x * pairs_y + pair)
            one, two = own_ones[row : row + 8, :], other_ones[row : row + 8, :]
            level_one[x + 2, pair + 1] = jnp.where(lower, one, two)
            level_one[x + half_x + 2, pair + 1] = jnp.where(lower, two, one)
    children = jnp.concatenate(
        [
            jnp.concatenate([level_one[2 * x + 2, y + 1], level_one[2 * x + 3, y + 1]], 1)
            for x in range(half_x)
            for y in range(pairs_y)
        ],
        0,
    )
    below = half_x * pairs_y * 8
    low_lanes = lanes((4, 128)) < 64
    sums[0:below, :] = dot_three(children, small[0:256], small[256:512])
    for x in range(half_x):
        for y in range(pairs_y):
            row = (x * pairs_y + y) * 8
            even = sums[pl.ds(row, 4, stride=2), :]
            odd = sums[pl.ds(row + 1, 4, stride=2), :]
            level_two[x + 2, y + 2, 0:4] = jnp.where(low_lanes, even + lane_flip(odd), 0.0)

    def second_group(group_x, group_y):
        return jnp.concatenate(
            [
                level_two[2 * group_x + h + 2, 2 * group_y + 2]
                + lane_flip(level_two[2 * group_x + h + 2, 2 * group_y + 3])
                for h in range(2)
            ],
            1,
        )

    quarter_x, quarter_y = index_x // 4, index_y // 4
    tops = [(x, y) for x in range(count_x // 4) for y in range(count_y // 4)]
    stacked = jnp.concatenate([second_group(x, y) for x, y in tops], 0)
    if stacked.shape[0] % 16 != 0:
        stacked = jnp.concatenate([stacked, jnp.zeros((8, 256), F32)], 0)
    sums[0 : stacked.shape[0], :] = dot_three(stacked, small[0:256], small[256:512])
    top_far = jnp.zeros((16, 128), F32)
    for position, (x, y) in enumerate(tops):
        even = sums[pl.ds(8 * position, 2, stride=2), :]
        odd = sums[pl.ds(8 * position + 1, 2, stride=2), :]
        third = jnp.where(lanes((2, 128)) < 64, even + lane_flip(odd), 0.0)
        third = third[0:1] + lane_flip(third)[1:2]
        step_x, step_y = x - quarter_x + count_x // 4 - 1, y - quarter_y + count_y // 4 - 1
        row = 1536 + 256 * (step_x * (count_y // 4 * 2 - 1) + step_y)
        table = [small[pl.ds(pl.multiple_of(row + 128 * k, 128), 128), :] for k in range(2)]
        top_far = top_far + dot_three(jnp.broadcast_to(third, (16, 128)), table[0], table[1])

    boxes[...] = jnp.zeros_like(boxes)
    for gx in (-1, 0, 1):
        for gy in (-1, 0, 1):
            for h in range(2):
                step = 2 * (index_x // 2 + gx) + h + 2
                boxes[8:16, 128 * h : 128 * h + 128] = level_one[step, index_y // 2 + gy + 1]
            boxes[24:32, :] = second_group(quarter_x + gx, quarter_y + gy)
            store_reflected(boxes, flips, flipped, gx, gy)
    far = far_sums((-1, 0, 1), ((8, 8), (24, 8)), flipped, flips, tiles)

    def select(block, hx, hy):
        tile = jnp.where(hx == 1, block[:, 128:256], block[:, 0:128])
        return jnp.where(hy == 1, lane_flip(tile), tile)

    def refine(parent):
        keep = lanes((16, 128)) < 64
        parent = jnp.where(keep, parent, 0.0)
        high = parent.astype(BF16).astype(F32)
        low = parent - high
        left = jnp.concatenate([high + lane_flip(low), high], 1).astype(BF16)
        down = jnp.concatenate([small[512 + 256 * k : 768 + 256 * k, :] for k in range(4)], 1)
        spread = dot(left, down)
        for half in range(2):
            for h in range(2):
                span = slice(256 * half + 128 * h, 256 * half + 128 * h + 128)
                local[h, pl.ds(half, 16, stride=2), :] = spread[:, span]
        return jnp.concatenate([local[0], local[1]], 1)

    top_local = jnp.where(
        sublanes((16, 128)) == 0, top_far, jnp.where(sublanes((16, 128)) == 1, lane_flip(top_far), 0.0)
    )
    children_far = refine(top_local)
    half_index_x, half_index_y = index_x // 2, index_y // 2
    second = select(children_far[0:8], lax.rem(half_index_x, 2), lax.rem(half_index_y, 2))
    second = second + 0.25 * select(far[8:16], lax.rem(half_index_x, 2), lax.rem(half_index_y, 2))
    zeros = jnp.zeros((8, 128), F32)
    children_far = refine(jnp.concatenate([second, zeros], 0))
    first = select(children_far[0:8], lax.rem(index_x, 2), lax.rem(index_y, 2))
    first = first + 0.5 * select(far[0:8], lax.rem(index_x, 2), lax.rem(index_y, 2))
    out[...] = refine(jnp.concatenate([first, zeros], 0))[0:16]


def upper_call(count_x, count_y, operands):
    half_x, half_y = count_x // 2, count_y // 2
    scratch = [
        pltpu.VMEM((count_x + 4, half_y + 2, 8, 128), F32),
        pltpu.VMEM((half_x + 4, half_y + 4, 8, 128), F32),
        pltpu.VMEM((40, 256), F32),
        pltpu.VMEM((3, 3, 2, 2, 40, 256), F32),
        pltpu.VMEM((max(16, half_x * half_y * 8), 128), F32),
        pltpu.VMEM((2, 32, 128), F32),
    ]
    return pl.pallas_call(
        lambda *refs: upper_kernel(count_x, count_y, refs),
        out_shape=jax.ShapeDtypeStruct((LZ, 256), F32),
        in_specs=[VMEM] * len(operands),
        out_specs=VMEM,
        scratch_shapes=scratch,
        compiler_params=pltpu.CompilerParams(vmem_limit_bytes=8 * MIB),
        cost_estimate=pl.CostEstimate(flops=900_000_000, bytes_accessed=600_000, transcendentals=0),
        name="upper",
    )(*operands)


def last_kernel(
    own_block, before, local, far_own, partner, beyond, targets, flips, one, two, out, near_rows, *scratch
):
    near_rows[...] = before[...]
    beside_x(1, beyond, targets, near_rows, *scratch[:2])
    far_beside = leaf_far((-1, 1), (partner, beyond), flips, (one, two), *scratch[2:])
    leaf = local[...] + far_own[...] + far_beside
    one, two = halves(leaf)
    turned = jnp.concatenate([one.astype(F32), two.astype(F32)], 0).T.astype(BF16)
    table = leaf_segments(2 * LZ)
    tables = basis_rows()
    for x in range(CX):
        for y in range(CY):
            column = x * CY + y
            spread = dot(turned[64 * column : 64 * column + 64], table)
            for j in range(ROWS):
                span = slice(128 * j, 128 * j + 128)
                places = [part_row(c, x, y) + j for c in range(3)]
                rows = [own_block[place : place + 1, :] for place in places]
                basis = basis_tile(*rows, None, tables)
                total = None
                for k in range(8):
                    term = basis[k] * spread[8 * k : 8 * k + 8, span]
                    total = term if total is None else total + term
                value = jnp.sum(total, 0, keepdims=True) + near_rows[column, j : j + 1, :]
                out[x, y : y + 1, span] = value


def last_call(operands):
    return pl.pallas_call(
        last_kernel,
        out_shape=jax.ShapeDtypeStruct((CX, CY, LZ * 64), F32),
        in_specs=[VMEM] * len(operands),
        out_specs=VMEM,
        scratch_shapes=[pltpu.VMEM(NEAR_SHAPE, F32), *near_scratch(8, 10), *LEAF_SCRATCH],
        compiler_params=pltpu.CompilerParams(vmem_limit_bytes=12 * MIB),
        name="last",
    )(*operands)


def in_hbm(value):
    return pltpu.with_memory_space_constraint(value, pltpu.HBM)


def swap_bit(value, axis, bit):
    return lax.ppermute(value, axis, [(i, i ^ (1 << bit)) for i in range(lax.axis_size(axis))])


def relay_ring(value, axis):
    count = lax.axis_size(axis)
    steps = {i: i + 2 if i % 2 == 0 else i - 2 for i in range(count)}
    steps[count - 2], steps[1] = count - 1, 0
    return lax.ppermute(value, axis, list(steps.items()))


def solution(mesh):
    count_x, count_y = mesh.shape["gx"], mesh.shape["gy"]
    levels_x, levels_y = count_x.bit_length() - 1, count_y.bit_length() - 1
    tiles = translation_tiles()
    small = small_tables(count_x // 4, count_y // 4)
    tables = small, reflection_tables(), tiles[:TILES_FIRST], tiles[TILES_FIRST:]

    def body(offsets, charges):
        small, flips, *tiles = [in_hbm(jnp.asarray(table)) for table in tables]
        block = moments_call(in_hbm(offsets), in_hbm(charges), small)
        other = swap_bit(block, "gy", 0)
        exchanged = []

        def exchange_y(after):
            pair = block, other
            for level in range(1, levels_y):
                last = level == levels_y - 1
                rows = (ONE_ROWS << (level - 1)) + EDGE_ROWS * (1 if last else 2)
                kernel = functools.partial(group_kernel, level, last)
                sent = pack_call(kernel, rows, (*pair, after), "group")
                pair = sent, swap_bit(sent, "gy", level)
                exchanged.extend(pair)
            return exchanged[0]

        near, targets, small, first_tiles = own_call(block, exchange_y, small, tiles[0])
        ones, row = row_call(levels_y, (block, other, *exchanged, near))
        other_ones = swap_bit(ones, "gx", 0)
        near, flips, other_tiles = beside_y_call(row, targets, near, (flips, tiles[1]))
        tables_near = flips, first_tiles, other_tiles
        ones = merge_call(0, ones, other_ones, near)
        other_ones = swap_bit(ones, "gx", 1)
        partner = swap_bit(hand_on_call(row, ones), "gx", 0)
        far_own = far_own_call(row, flips, first_tiles, ones)
        for bit in range(1, levels_x - 1):
            ones = merge_call(bit, ones, other_ones, far_own)
            other_ones = swap_bit(ones, "gx", bit + 1)
        beyond = relay_ring(relay_call(partner, ones), "gx")
        near = near_call(beside_x_kernel, (partner, targets, near, ones), 8, 10, 1_200_000, "near_x")
        local = upper_call(count_x, count_y, (ones, other_ones, small, *tables_near, near))
        return last_call((block, near, local, far_own, partner, beyond, targets, *tables_near))

    in_specs = (P(None, "gx", "gy", None), P("gx", "gy", None))
    out_specs = P("gx", "gy", None)
    return jax.shard_map(body, mesh=mesh, in_specs=in_specs, out_specs=out_specs, check_vma=False)
```

```python
import functools
import itertools

import jax
import jax.numpy as jnp
import ml_dtypes
import numpy as np
from jax import lax
from jax.experimental import pallas as pl
from jax.experimental.pallas import tpu as pltpu
from jax.sharding import PartitionSpec as P

F32 = jnp.float32
BF16 = jnp.bfloat16
MIB = 1 << 20

CX = 2
CY = 2
LZ = 16
ROWS = 8
FEATURES = 32
VMEM = pl.BlockSpec(memory_space=pltpu.VMEM)
HBM = pl.BlockSpec(memory_space=pltpu.HBM)


def nodes_1d():
    return np.cos((2.0 * np.arange(4) + 1.0) * np.pi / 8.0)


def cheb_terms(value):
    return value, 2.0 * value * value - 1.0, 4.0 * value**3 - 3.0 * value


def node_weights():
    return [[0.5 * term for term in cheb_terms(point)] for point in nodes_1d()]


def node_grid():
    points = nodes_1d()
    counter = np.arange(64)
    return np.stack([points[counter // 16], points[counter // 4 % 4], points[counter % 4]], -1)


def split_two(table):
    high = table.astype(np.float32).astype(ml_dtypes.bfloat16)
    low = (table - high.astype(np.float64)).astype(np.float32).astype(ml_dtypes.bfloat16)
    return high, low


def upward_tensor():
    points = nodes_1d()
    shifted = (points[None, :] + 2.0 * np.arange(2)[:, None] - 1.0) / 2.0
    factor = 0.25 + 0.0 * shifted[..., None]
    for of_value, of_node in zip(cheb_terms(shifted), cheb_terms(points)):
        factor = factor + 0.5 * of_value[..., None] * of_node
    full = np.einsum("xia,yjb,zkc->xyzijkabc", factor, factor, factor)
    return full.reshape(2, 2, 2, 64, 64)


def inverse_distance(offset):
    grid = node_grid()
    spread = (grid[None, :, :] - grid[:, None, :]) / 2.0 - np.asarray(offset, np.float64)
    return 1.0 / np.sqrt(np.sum(spread * spread, -1))


def adjacent(offset):
    return max(abs(int(step)) for step in offset) <= 1


def canonical_tiles():
    return [
        (cx, cy, cz)
        for cx in range(2)
        for cy in range(2)
        for cz in range(4)
        if not (cx == 0 and cy == 0 and cz <= 1)
    ]


TILES_FIRST = 10


def translation_tiles():
    tiles = []
    for cx, cy, cz in canonical_tiles():
        tile = np.zeros((4, 64, 4, 64))
        for source in range(4):
            for target in range(4):
                offset = (
                    2 * cx + source // 2 - target // 2,
                    2 * cy + source % 2 - target % 2,
                    cz,
                )
                if not adjacent(offset):
                    tile[source, :, target, :] = inverse_distance(offset)
        tiles.append(tile.reshape(256, 256))
    return np.stack(split_two(np.stack(tiles)), 1)


def reflection_matrix(flip_x, flip_y, flip_z):
    index = np.arange(256)
    hx, hy, a, b, c = index // 128, index // 64 % 2, index // 16 % 4, index // 4 % 4, index % 4
    if flip_x:
        hx, a = 1 - hx, 3 - a
    if flip_y:
        hy, b = 1 - hy, 3 - b
    if flip_z:
        c = 3 - c
    matrix = np.zeros((256, 256), np.float32)
    matrix[hx * 128 + hy * 64 + a * 16 + b * 4 + c, index] = 1.0
    return matrix


def reflection_tables():
    pairs = [
        np.concatenate([reflection_matrix(fx, fy, 0), reflection_matrix(fx, fy, 1)], 1)
        for fx in range(2)
        for fy in range(2)
    ]
    return np.stack(pairs).astype(ml_dtypes.bfloat16)


def up_tables():
    upward = upward_tensor()
    table = upward.transpose(0, 1, 3, 2, 4).reshape(256, 128)
    return np.stack(split_two(table))


def down_table():
    upward = upward_tensor()
    table = upward.transpose(4, 2, 0, 1, 3).reshape(64, 512)
    high, low = split_two(table)
    return np.concatenate([high, high, low, np.zeros_like(low)], 0)


def top_tables(boxes_x, boxes_y):
    offsets = range(-(boxes_x - 1), boxes_x), range(-(boxes_y - 1), boxes_y)
    table = np.zeros((len(offsets[0]), len(offsets[1]), 2, 64, 2, 64))
    for (ix, dx), (iy, dy) in itertools.product(enumerate(offsets[0]), enumerate(offsets[1])):
        for source, target in itertools.product(range(2), range(2)):
            offset = (dx, dy, source - target)
            if not adjacent(offset):
                table[ix, iy, source, :, target, :] = 0.125 * inverse_distance(offset)
    return np.stack(split_two(table.reshape(len(offsets[0]), len(offsets[1]), 128, 128)), 2)


def small_tables(boxes_x, boxes_y):
    down = down_table().reshape(256, 4, 128).transpose(1, 0, 2)
    parts = [up_tables(), down, top_tables(boxes_x, boxes_y)]
    return np.concatenate([part.reshape(-1, 128) for part in parts], 0)


def halves(value):
    high = value.astype(BF16)
    return high, (value - high.astype(F32)).astype(BF16)


def dot(left, right):
    return jnp.dot(left, right, preferred_element_type=F32)


def dot_three(value, high_table, low_table):
    rows = value.shape[0]
    high, low = halves(value)
    both = dot(jnp.concatenate([high, low], 0), high_table)
    return both[:rows] + both[rows:] + dot(high, low_table)


def lanes(shape):
    return lax.broadcasted_iota(jnp.int32, shape, len(shape) - 1)


def sublanes(shape):
    return lax.broadcasted_iota(jnp.int32, shape, len(shape) - 2)


def leaf_segments(leaves):
    shape = (leaves, LZ * 64)
    return jnp.where(lanes(shape) // 64 == lax.rem(sublanes(shape), LZ), 1.0, 0.0).astype(BF16)


def lane_flip(value):
    return pltpu.roll(value, 64, 1)


def weight_rows(pattern):
    weights = node_weights()
    index = sublanes((8, 128))
    rows = []
    for term in range(3):
        row = jnp.full((8, 128), weights[pattern(0)][term], F32)
        for sub in range(1, 8):
            row = jnp.where(index == sub, weights[pattern(sub)][term], row)
        rows.append(row)
    return rows


def basis_rows():
    return (
        weight_rows(lambda sub: sub // 4),
        weight_rows(lambda sub: 2 + sub // 4),
        weight_rows(lambda sub: sub % 4),
    )


def basis_tile(row_x, row_y, row_z, scale, tables):
    y_low, y_high, z_all = tables
    wide = [jnp.broadcast_to(2.0 * row - 1.0, (8, 128)) for row in (row_x, row_y, row_z)]
    terms = [cheb_terms(value) for value in wide]

    def mix(weights, term):
        return 0.25 + (weights[0] * term[0] + weights[1] * term[1] + weights[2] * term[2])

    along_z = mix(z_all, terms[2])
    pair = mix(y_low, terms[1]) * along_z, mix(y_high, terms[1]) * along_z
    tiles = []
    for weights in node_weights():
        along_x = mix(weights, terms[0])
        if scale is not None:
            along_x = along_x * scale
        tiles += [along_x * pair[0], along_x * pair[1]]
    return tiles


def three_pieces(value):
    first = value.astype(BF16).astype(F32)
    rest = value - first
    second = rest.astype(BF16).astype(F32)
    return first, second, rest - second


PIECES = 12


def feature_pieces(coords, scale):
    total = coords[0] * coords[0] + coords[1] * coords[1] + coords[2] * coords[2]
    return [piece for value in [scale * coord for coord in coords] + [total] for piece in three_pieces(value)]


def pick(row, pieces, choice):
    value = jnp.broadcast_to(pieces[choice[0]], (8, 128))
    for piece in sorted(set(choice) - {choice[0]}):
        mask = None
        for place, chosen in enumerate(choice):
            if chosen == piece:
                mask = row == place if mask is None else mask | (row == place)
        value = jnp.where(mask, jnp.broadcast_to(pieces[piece], (8, 128)), value)
    return value


def feature_block(read, choice, length_choice):
    row = sublanes((8, 128))
    zero, one = jnp.zeros((1, 128), F32), jnp.ones((1, 128), F32)
    blocks = [
        pick(row, [read(3 * c), read(3 * c + 1), read(3 * c + 2), zero], choice) for c in range(3)
    ]
    blocks.append(pick(row, [read(9), read(10), read(11), one, zero], length_choice))
    return jnp.concatenate(blocks, 0)


SOURCE_CHOICE = (0, 1, 0, 1, 2, 0, 0, 0), (3, 3, 3, 0, 1, 2, 3, 3)
TARGET_CHOICE = (0, 0, 1, 1, 0, 2, 3, 3), (0, 1, 2, 3, 3, 3, 4, 4)


def column(raw, x, y):
    return raw(0) + (x - 2.0), raw(1) + (y - 2.0), raw(2), raw(3)


class Near:
    def __init__(self, wide_ref, charge_ref, target_ref):
        self.wide_ref = wide_ref
        self.charge_ref = charge_ref
        self.target_ref = target_ref
        self.groups = 0
        self.charges = 0
        self.upper = lanes((ROWS, 128)) >= 64
        self.row = sublanes((ROWS, 128))

    def in_pair(self, along_z):
        return along_z + jnp.where(self.upper, 0.0, -1.0)

    def targets(self, columns):
        for ab, (x, y, z, _) in enumerate(columns):
            pieces = feature_pieces((x, y, self.in_pair(z)), -2.0)
            for j in range(ROWS):
                block = feature_block(lambda k: pieces[k][j : j + 1], *TARGET_CHOICE)
                self.target_ref[ab, j] = block.T.astype(BF16)

    def add_group(self, coords):
        for k, piece in enumerate(feature_pieces(coords, 1.0)):
            self.wide_ref[self.groups, k] = piece
        self.groups += 1
        return self.groups - 1

    def add_charge(self, charge):
        self.charge_ref[self.charges] = charge
        self.charges += 1
        return self.charges - 1

    def main(self, source):
        x, y, z, charge = source
        return self.add_group((x, y, self.in_pair(z))), self.add_charge(charge)

    def outer(self, first, second, side, keep=False):
        def merge(one, two):
            if side == 0:
                value = jnp.where(self.upper, two, lane_flip(one))
                return pltpu.roll(value, 1, 0)
            value = jnp.where(self.upper, lane_flip(two), one)
            return pltpu.roll(value, ROWS - 1, 0)

        x, y, z, charge = [merge(one, two) for one, two in zip(first, second)]
        charge = jnp.where(self.row == (0 if side == 0 else ROWS - 1), 0.0, charge)
        group = self.add_group((x, y, z + (-2.0 if side == 0 else 1.0)))
        if not keep:
            return group, self.add_charge(charge)
        low = self.add_charge(jnp.where(self.upper, 0.0, charge))
        high = self.add_charge(jnp.where(self.upper, charge, 0.0))
        return (group, low), (group, high)

    def run(self, plan, emit):
        eye = sublanes((128, 128)) == lanes((128, 128))

        def source(group, j, built):
            if group not in built:
                read = lambda k: self.wide_ref[group, k, pl.ds(j, 1), :]
                built[group] = feature_block(read, *SOURCE_CHOICE).astype(BF16)
            return built[group]

        def pairs(targets, tiles, j, own, total, built):
            block = jnp.concatenate([source(group, j, built) for group, _ in tiles], 1)
            squared = dot(targets, block)
            for position, (group, charge) in enumerate(tiles):
                inverse = lax.rsqrt(squared[:, 128 * position : 128 * position + 128])
                if group == own:
                    inverse = jnp.where(eye, 0.0, inverse)
                total = total + inverse * self.charge_ref[charge, pl.ds(j, 1), :]
            return total

        def step(j, carry):
            built = {}
            for ab, mains, below, above, own in plan:
                targets = self.target_ref[ab, j]
                total = pairs(targets, mains, j, own, jnp.zeros((128, 128), F32), built)
                lower = pairs(targets[:64], below, j, None, total[:64], built)
                higher = pairs(targets[64:], above, j, None, total[64:], built)
                total = jnp.concatenate([lower, higher], 0)
                emit(ab, j, jnp.sum(total.T, 0, keepdims=True))
            return carry

        lax.fori_loop(0, ROWS, step, 0, unroll=True)


def plan_own(near, columns):
    mains = [near.main(source) for source in columns]
    outer = [
        [near.outer(columns[2 * x], columns[2 * x + 1], side) for x in range(2)]
        for side in range(2)
    ]
    return [(ab, mains, outer[0], outer[1], mains[ab][0]) for ab in range(4)]


def plan_beside_y(near, columns):
    plan = []
    for b in range(2):
        mains = [near.main(source) for source in columns[b]]
        outer = [[near.outer(*columns[b], side)] for side in range(2)]
        plan += [(2 * a + b, mains, outer[0], outer[1], None) for a in range(2)]
    return plan


def plan_beside_x(near, columns, side_x):
    mains = [near.main(source) for source in columns]
    middle = [near.outer(columns[1], columns[2], side) for side in range(2)]
    ends = [near.outer(columns[0], columns[3], side, keep=True) for side in range(2)]
    return [
        (2 * side_x + b, mains[b : b + 3], [middle[0], ends[0][b]], [middle[1], ends[1][b]], None)
        for b in range(2)
    ]


def near_scratch(groups, charges):
    return [
        pltpu.VMEM((groups, PIECES, ROWS, 128), F32),
        pltpu.VMEM((charges, ROWS, 128), F32),
    ]


NEAR_SHAPE = (4, ROWS, 128)


def near_cost(pairs):
    return pl.CostEstimate(flops=40 * pairs, bytes_accessed=600_000, transcendentals=pairs)


ONE_ROWS = 8
LEAF_ROWS = 32
PART_ROWS = 4 * CX * CY * ROWS
OWN_ROWS = ONE_ROWS + LEAF_ROWS + PART_ROWS


def part_row(c, x, y):
    return ONE_ROWS + LEAF_ROWS + ((c * CX + x) * CY + y) * ROWS


def moments_kernel(
    offsets_hbm, charges_hbm, small_hbm, block, offsets, charges, up, basis, sums, semaphores
):
    index_y = lax.axis_index("gy")
    copies = [
        pltpu.make_async_copy(offsets_hbm, offsets, semaphores.at[0]),
        pltpu.make_async_copy(charges_hbm, charges, semaphores.at[1]),
        pltpu.make_async_copy(small_hbm.at[0:512], up, semaphores.at[2]),
    ]
    for copy in copies:
        copy.start()
    tables = basis_rows()
    segments = leaf_segments(LZ)
    copies[0].wait()
    copies[1].wait()
    for x in range(CX):
        for y in range(CY):
            for j in range(ROWS):
                span = slice(128 * j, 128 * j + 128)
                rows = [offsets[c, x, y : y + 1, span] for c in range(3)]
                charge = charges[x, y : y + 1, span]
                for c, row in enumerate(rows + [charge]):
                    place = part_row(c, x, y) + j
                    block[place : place + 1, :] = row
                tiles = basis_tile(*rows, charge, tables)
                for k in range(4):
                    pair = jnp.concatenate(tiles[2 * k : 2 * k + 2], 0)
                    high, low = halves(pair)
                    first = (x * CY + y) * 64 + 16 * k
                    basis[0, first : first + 16, span] = high
                    basis[1, first : first + 16, span] = low
    contract = (((1,), (1,)), ((), ()))
    leaf = lax.dot_general(segments, basis[0], contract, preferred_element_type=F32)
    leaf = leaf + lax.dot_general(segments, basis[1], contract, preferred_element_type=F32)
    copies[2].wait()
    sums[...] = dot_three(leaf, up[0:256], up[256:512])
    first = sums[pl.ds(0, 8, stride=2), :] + lane_flip(sums[pl.ds(1, 8, stride=2), :])
    first = jnp.where(lanes((8, 128)) < 64, first, 0.0)
    first = jnp.where(lax.rem(index_y, 2) == 1, lane_flip(first), first)
    block[0:8, :] = first
    block[8:24, :] = leaf[:, :128]
    block[24:40, :] = leaf[:, 128:]


def moments_call(offsets, charges, small):
    return pl.pallas_call(
        moments_kernel,
        out_shape=jax.ShapeDtypeStruct((OWN_ROWS, 128), F32),
        in_specs=[HBM] * 3,
        out_specs=VMEM,
        scratch_shapes=[
            pltpu.VMEM(offsets.shape, F32),
            pltpu.VMEM(charges.shape, F32),
            pltpu.VMEM((512, 128), BF16),
            pltpu.VMEM((2, 256, 1024), BF16),
            pltpu.VMEM((16, 128), F32),
            pltpu.SemaphoreType.DMA((3,)),
        ],
        compiler_params=pltpu.CompilerParams(vmem_limit_bytes=8 * MIB),
        cost_estimate=pl.CostEstimate(flops=10_000_000, bytes_accessed=300_000, transcendentals=0),
        name="moments",
    )(offsets, charges, small)


EDGE_ROWS = LEAF_ROWS + 4 * CX * ROWS


def bits_below(index, bit):
    return lax.rem(index, 1 << bit)


def bit_of(index, bit):
    return lax.rem(index // (1 << bit), 2)


def in_order(is_first, own, other):
    return jnp.concatenate([jnp.where(is_first, own, other), jnp.where(is_first, other, own)], 0)


def edge_block(block, y):
    rows = [block[ONE_ROWS : ONE_ROWS + LEAF_ROWS, :]]
    for c in range(4):
        for x in range(CX):
            rows.append(block[part_row(c, x, y) : part_row(c, x, y) + ROWS, :])
    return jnp.concatenate(rows, 0)


def group_kernel(level, last_level, own_ref, other_ref, after, out):
    index = lax.axis_index("gy")
    ones = ONE_ROWS << (level - 1)
    is_first = bit_of(index, level - 1) == 0
    if level == 1:
        out[0:ones, :] = own_ref[0:ones, :] + other_ref[0:ones, :]
        first = jnp.where(is_first, edge_block(own_ref, 0), edge_block(other_ref, 0))
        last = jnp.where(is_first, edge_block(other_ref, 1), edge_block(own_ref, 1))
    else:
        half = ones // 2
        out[0:ones, :] = in_order(is_first, own_ref[0:half, :], other_ref[0:half, :])
        own_far = own_ref[half + EDGE_ROWS : half + 2 * EDGE_ROWS, :]
        other_far = other_ref[half + EDGE_ROWS : half + 2 * EDGE_ROWS, :]
        first = jnp.where(is_first, own_far, other_far)
        last = jnp.where(is_first, other_far, own_far)
    lower = bit_of(index, level) == 0
    out[ones : ones + EDGE_ROWS, :] = jnp.where(lower, last, first)
    if not last_level:
        out[ones + EDGE_ROWS : ones + 2 * EDGE_ROWS, :] = jnp.where(lower, first, last)


def pack_call(kernel, rows, operands, name):
    return pl.pallas_call(
        kernel,
        out_shape=jax.ShapeDtypeStruct((rows, 128), F32),
        in_specs=[VMEM] * len(operands),
        out_specs=VMEM,
        compiler_params=pltpu.CompilerParams(vmem_limit_bytes=8 * MIB),
        cost_estimate=pl.CostEstimate(flops=100_000, bytes_accessed=300_000, transcendentals=0),
        name=name,
    )(*operands)


ROW_LEAF = 3 * LEAF_ROWS
ROW_PART = 4 * 4 * ROWS
ROW_ROWS = ROW_LEAF + ROW_PART
ROW_BOTH = ROW_ROWS + ROW_PART


def row_part(c, y):
    return ROW_LEAF + (c * 4 + y) * ROWS


def row_kernel(levels, block, other, *refs):
    exchanged, out = refs[: 2 * (levels - 1)], refs[-1]
    index = lax.axis_index("gy")
    even = lax.rem(lax.axis_index("gx"), 2) == 0
    is_first = bit_of(index, 0) == 0
    low = jnp.where(is_first, 0.0, edge_block(other, 1))
    high = jnp.where(is_first, edge_block(other, 0), 0.0)
    ones = ONE_ROWS
    for level in range(1, levels):
        own, received = exchanged[2 * level - 2 : 2 * level]
        ones = ONE_ROWS << (level - 1)
        facing = received[ones : ones + EDGE_ROWS, :]
        below = bits_below(index, level)
        upper = bit_of(index, level) == 1
        low = jnp.where(upper & (below == 0), facing, low)
        high = jnp.where(~upper & (below == (1 << level) - 1), facing, high)
        if level == levels - 1:
            out[ROW_BOTH:, :] = in_order(~upper, own[0:ones, :], received[0:ones, :])
    leaf = block[ONE_ROWS : ONE_ROWS + LEAF_ROWS, :]
    for piece, rows in enumerate((low[0:LEAF_ROWS], leaf, high[0:LEAF_ROWS])):
        out[LEAF_ROWS * piece : LEAF_ROWS * (piece + 1), :] = rows
    for c in range(4):
        columns = []
        for x in range(CX):
            row = LEAF_ROWS + (c * CX + x) * ROWS
            own = [block[part_row(c, x, y) : part_row(c, x, y) + ROWS, :] for y in range(CY)]
            columns.append([low[row : row + ROWS], *own, high[row : row + ROWS]])
        for y in range(4):
            facing, far = row_part(c, y), row_part(c, y) + ROW_PART
            out[facing : facing + ROWS, :] = jnp.where(even, columns[1][y], columns[0][y])
            out[far : far + ROWS, :] = jnp.where(even, columns[0][y], columns[1][y])


def row_call(levels, operands):
    return pl.pallas_call(
        lambda *refs: row_kernel(levels, *refs[: 2 * levels], refs[-1]),
        out_shape=jax.ShapeDtypeStruct((ROW_BOTH + (ONE_ROWS << (levels - 1)), 128), F32),
        in_specs=[VMEM] * len(operands),
        out_specs=VMEM,
        compiler_params=pltpu.CompilerParams(vmem_limit_bytes=8 * MIB),
        cost_estimate=pl.CostEstimate(flops=100_000, bytes_accessed=600_000, transcendentals=0),
        name="row",
    )(*operands)


SENT_ROWS = 192


def merge_call(bit, own, other, first, rows, least, after):
    total = max(2 * rows, least)

    def kernel(own_ref, other_ref, after_ref, out):
        is_first = bit_of(lax.axis_index("gx"), bit) == 0
        span = slice(first, first + rows)
        out[0 : 2 * rows, :] = in_order(is_first, own_ref[span, :], other_ref[span, :])
        if total > 2 * rows:
            out[2 * rows :, :] = jnp.zeros((total - 2 * rows, 128), F32)

    return pack_call(kernel, total, (own, other, after), "merge")


def relay_call(received, after):
    def kernel(received_ref, after_ref, out):
        out[0:ROW_LEAF, :] = received_ref[0:ROW_LEAF, :]
        out[ROW_LEAF:ROW_ROWS, :] = received_ref[ROW_ROWS:ROW_BOTH, :]

    return pack_call(kernel, ROW_ROWS, (received, after), "relay")


def own_kernel(block, targets, features, charges):
    near = Near(features, charges, targets)

    def raw(x, y):
        return lambda c: block[part_row(c, x, y) : part_row(c, x, y) + ROWS, :]

    columns = [column(raw(ab // 2, ab % 2), ab // 2 + 1, ab % 2 + 1) for ab in range(4)]
    near.targets(columns)
    return near, plan_own(near, columns)


def own_call(block, after, small, tiles):
    plans = []

    def prepare(block_ref, small, targets, features, charges, small_out, semaphore):
        copy = pltpu.make_async_copy(small, small_out, semaphore)
        copy.start()
        plans.append(own_kernel(block_ref, targets, features, charges)[1])
        copy.wait()

    def run(targets, features, charges, after_ref, tiles, out, tiles_out, semaphore):
        copy = pltpu.make_async_copy(tiles, tiles_out, semaphore)
        copy.start()

        def emit(ab, j, row):
            out[ab, pl.ds(j, 1), :] = row

        Near(features, charges, targets).run(plans[0], emit)
        copy.wait()

    prepared = pl.pallas_call(
        prepare,
        out_shape=(
            jax.ShapeDtypeStruct((4, ROWS, 128, FEATURES), BF16),
            jax.ShapeDtypeStruct((8, PIECES, ROWS, 128), F32),
            jax.ShapeDtypeStruct((8, ROWS, 128), F32),
            jax.ShapeDtypeStruct(small.shape, BF16),
        ),
        in_specs=[VMEM, HBM],
        out_specs=(VMEM,) * 4,
        scratch_shapes=[pltpu.SemaphoreType.DMA],
        compiler_params=pltpu.CompilerParams(vmem_limit_bytes=8 * MIB),
        cost_estimate=near_cost(500_000),
        name="features",
    )(block, small)
    near, tiles_near = pl.pallas_call(
        run,
        out_shape=(
            jax.ShapeDtypeStruct(NEAR_SHAPE, F32),
            jax.ShapeDtypeStruct(tiles.shape, BF16),
        ),
        in_specs=[VMEM] * 4 + [HBM],
        out_specs=(VMEM,) * 2,
        scratch_shapes=[pltpu.SemaphoreType.DMA],
        compiler_params=pltpu.CompilerParams(vmem_limit_bytes=8 * MIB),
        cost_estimate=near_cost(4_500_000),
        name="near_own",
    )(*prepared[:3], after(prepared[2]), tiles)
    return near, prepared[0], prepared[3], tiles_near


def beside_y_kernel(
    row_ref, targets, before, flips, tiles, out, flips_out, tiles_out, wide_ref, charge_ref, semaphores
):
    copies = [
        pltpu.make_async_copy(flips, flips_out, semaphores.at[0]),
        pltpu.make_async_copy(tiles, tiles_out, semaphores.at[1]),
    ]
    for copy in copies:
        copy.start()
    even = lax.rem(lax.axis_index("gx"), 2) == 0
    near = Near(wide_ref, charge_ref, targets)

    def raw(x, y):
        def read(c):
            facing, far = row_part(c, y), row_part(c, y) + ROW_PART
            own = row_ref[facing : facing + ROWS, :], row_ref[far : far + ROWS, :]
            return jnp.where(even == (x == 1), *own)

        return read

    columns = [[column(raw(x, y), x + 1, y) for x in range(2)] for y in (0, 3)]
    plan = plan_beside_y(near, columns)
    out[...] = before[...]

    def emit(ab, j, row):
        out[ab, pl.ds(j, 1), :] = out[ab, pl.ds(j, 1), :] + row

    near.run(plan, emit)
    for copy in copies:
        copy.wait()


def beside_y_call(row, targets, before, constants):
    near_shape = jax.ShapeDtypeStruct(NEAR_SHAPE, F32)
    tables = [jax.ShapeDtypeStruct(constant.shape, BF16) for constant in constants]
    return pl.pallas_call(
        beside_y_kernel,
        out_shape=(near_shape, *tables),
        in_specs=[VMEM] * 3 + [HBM] * 2,
        out_specs=(VMEM,) * 3,
        scratch_shapes=near_scratch(8, 8) + [pltpu.SemaphoreType.DMA((2,))],
        compiler_params=pltpu.CompilerParams(vmem_limit_bytes=8 * MIB),
        cost_estimate=near_cost(2_200_000),
        name="near_y",
    )(row, targets, before, *constants)


def beside_x(parity, received, targets, out, wide_ref, charge_ref):
    index, count = lax.axis_index("gx"), lax.axis_size("gx")
    even = lax.rem(index, 2) == 0
    side = jnp.where(even == (parity == 0), 1, 0)
    alone = (index == 0) | (index == count - 1)
    near = Near(wide_ref, charge_ref, targets)

    def raw(y):
        def coordinate(c):
            value = received[row_part(c, y) : row_part(c, y) + ROWS, :]
            return jnp.where(alone, 0.0, value) if c == 3 and parity == 1 else value

        return coordinate

    columns = [column(raw(y), 3.0 * side.astype(F32), y) for y in range(4)]
    plan = plan_beside_x(near, columns, side)

    def emit(ab, j, row):
        out[ab, pl.ds(j, 1), :] = out[ab, pl.ds(j, 1), :] + row

    near.run(plan, emit)


def beside_x_kernel(received, targets, before, after, out, wide_ref, charge_ref):
    out[...] = before[...]
    beside_x(0, received, targets, out, wide_ref, charge_ref)


def near_call(kernel, operands, groups, charges, pairs, name):
    return pl.pallas_call(
        kernel,
        out_shape=jax.ShapeDtypeStruct(NEAR_SHAPE, F32),
        in_specs=[VMEM] * len(operands),
        out_specs=VMEM,
        scratch_shapes=near_scratch(groups, charges),
        compiler_params=pltpu.CompilerParams(vmem_limit_bytes=12 * MIB),
        cost_estimate=near_cost(pairs),
        name=name,
    )(*operands)


def store_reflected(moments, flips, flipped):
    def store(group, z, part, value):
        for half in range(2):
            place = flipped.at[group[0] + 1, group[1] + 1, z, part, half]
            place[...] = value[:, 128 * half : 128 * half + 128]

    parts = {group: halves(value) for group, value in moments.items()}
    for fx in range(2):
        for fy in range(2):
            groups = [group for group in moments if (group[0] < 0, group[1] < 0) == (fx == 1, fy == 1)]
            if not groups:
                continue
            stacked = jnp.concatenate([part for group in groups for part in parts[group]], 0)
            rows = stacked.shape[0] // (2 * len(groups))
            first = 0 if fx + fy > 0 else 1
            mixed = dot(stacked, flips[2 * fx + fy, :, 256 * first :])
            for order, group in enumerate(groups):
                for part in range(2):
                    start = rows * (2 * order + part)
                    if first == 1:
                        store(group, 0, part, parts[group][part].astype(F32))
                    for z in range(first, 2):
                        span = slice(256 * (z - first), 256 * (z - first) + 256)
                        store(group, z, part, mixed[start : start + rows, span])


def far_sums(columns, spans, flipped, flips, tiles):
    odd_row = lax.rem(sublanes((16, 256)), 2) == 1
    totals = {}
    for position, (cx, cy, cz) in enumerate(canonical_tiles()):
        entries = [
            (gx, gy, dz)
            for gx in sorted({cx, -cx})
            for gy in sorted({cy, -cy})
            for dz in sorted({cz, -cz})
            if gx in columns
        ]
        if not entries:
            continue
        pieces = [[], []]
        for gx, gy, dz in entries:
            for part in range(2):
                view = flipped.at[gx + 1, gy + 1, int(dz < 0), part]
                windows = [
                    [view[half, first + dz : first + dz + size, :] for first, size in spans]
                    for half in range(2)
                ]
                block = jnp.concatenate([jnp.concatenate(window, 0) for window in windows], 1)
                if abs(dz) == 3:
                    block = jnp.where(odd_row if dz < 0 else ~odd_row, block, 0.0)
                pieces[part].append(block.astype(BF16))
        rows = 16 * len(entries)
        part = tiles[0] if position < TILES_FIRST else tiles[1]
        tile = part.at[position % TILES_FIRST]
        both = dot(jnp.concatenate(pieces[0] + pieces[1], 0), tile[0])
        result = both[:rows] + both[rows:] + dot(jnp.concatenate(pieces[0], 0), tile[1])
        for order, (gx, gy, dz) in enumerate(entries):
            key = (int(gx < 0), int(gy < 0), int(dz < 0))
            piece = result[16 * order : 16 * order + 16]
            totals[key] = totals[key] + piece if key in totals else piece
    far = None
    for (fx, fy, fz), total in totals.items():
        if (fx, fy, fz) != (0, 0, 0):
            high, low = halves(total)
            table = flips[2 * fx + fy, :, 256 * fz : 256 * fz + 256]
            both = dot(jnp.concatenate([high, low], 0), table)
            total = both[:16] + both[16:]
        far = total if far is None else far + total
    return far


def store_leaves(columns, halos, flips, flipped):
    index, count = lax.axis_index("gx"), lax.axis_size("gx")
    is_even = lax.rem(index, 2) == 0
    edge = jnp.zeros((8, 128), F32)
    groups = {}
    for gx in columns:
        for gy in (-1, 0, 1):
            tiles_h = []
            for h in range(2):
                row = LEAF_ROWS * (gy + 1) + 16 * h
                rows = slice(row, row + 16)
                moments = halos[0][rows, :]
                if gx != 0:
                    moments = jnp.where(is_even == (gx == 1), moments, halos[1][rows, :])
                    inside = index > 0 if gx < 0 else index < count - 1
                    moments = jnp.where(inside, moments, 0.0)
                tiles_h.append(jnp.concatenate([edge, moments, edge], 0))
            groups[gx, gy] = jnp.concatenate(tiles_h, 1)
    store_reflected(groups, flips, flipped)


LEAF_SHAPE = (3, 3, 2, 2, 2, 32, 128)
LEAF_SPANS = ((8, 16),)


def far_call(kernel, shape, operands, name):
    return pl.pallas_call(
        kernel,
        out_shape=jax.ShapeDtypeStruct(shape, F32),
        in_specs=[VMEM] * len(operands),
        out_specs=VMEM,
        compiler_params=pltpu.CompilerParams(vmem_limit_bytes=8 * MIB),
        cost_estimate=pl.CostEstimate(flops=300_000_000, bytes_accessed=600_000, transcendentals=0),
        name=name,
    )(*operands)


def own_leaves_call(row, flips, block):
    def kernel(row_ref, flips_ref, block_ref, out, basis_out):
        store_leaves((0,), (row_ref,), flips_ref, out)
        tables = basis_rows()
        for x in range(CX):
            for y in range(CY):
                for j in range(ROWS):
                    places = [part_row(c, x, y) + j for c in range(3)]
                    rows = [block_ref[place : place + 1, :] for place in places]
                    for k, tile in enumerate(basis_tile(*rows, None, tables)):
                        basis_out[x * CY + y, j, 8 * k : 8 * k + 8, :] = tile

    shapes = LEAF_SHAPE, (CX * CY, ROWS, 64, 128)
    return pl.pallas_call(
        kernel,
        out_shape=[jax.ShapeDtypeStruct(shape, F32) for shape in shapes],
        in_specs=[VMEM] * 3,
        out_specs=[VMEM] * 2,
        compiler_params=pltpu.CompilerParams(vmem_limit_bytes=8 * MIB),
        cost_estimate=near_cost(100_000),
        name="own_leaves",
    )(row, flips, block)


def far_own_call(leaves, flips, tiles):
    def kernel(leaves_ref, flips_ref, tiles_ref, out):
        out[...] = far_sums((0,), LEAF_SPANS, leaves_ref, flips_ref, (tiles_ref,))

    return far_call(kernel, (LZ, 256), (leaves, flips, tiles), "far_own")


def beyond_kernel(
    before, partner, beyond, targets, flips, one, two, after, out, far_out, wide_ref, charge_ref, leaves
):
    out[...] = before[...]
    beside_x(1, beyond, targets, out, wide_ref, charge_ref)
    store_leaves((-1, 1), (partner, beyond), flips, leaves)
    far_out[...] = far_sums((-1, 1), LEAF_SPANS, leaves, flips, (one, two))


def beyond_call(operands):
    return pl.pallas_call(
        beyond_kernel,
        out_shape=(jax.ShapeDtypeStruct(NEAR_SHAPE, F32), jax.ShapeDtypeStruct((LZ, 256), F32)),
        in_specs=[VMEM] * len(operands),
        out_specs=(VMEM,) * 2,
        scratch_shapes=near_scratch(8, 10) + [pltpu.VMEM(LEAF_SHAPE, F32)],
        compiler_params=pltpu.CompilerParams(vmem_limit_bytes=12 * MIB),
        cost_estimate=near_cost(2_400_000),
        name="beyond",
    )(*operands)


def upper_kernel(count_x, count_y, refs):
    own_ones, other_ones, small, flips, *tiles, _, out = refs[:8]
    refs = refs[8:]
    level_one, level_two, flipped, sums, local = refs

    index_x, index_y = lax.axis_index("gx"), lax.axis_index("gy")
    pairs_y = count_y // 2

    level_one[...] = jnp.zeros_like(level_one)
    level_two[...] = jnp.zeros_like(level_two)
    half_x = count_x // 2
    lower = index_x < half_x
    for x in range(half_x):
        for pair in range(pairs_y):
            row = 8 * (x * pairs_y + pair)
            one, two = own_ones[row : row + 8, :], other_ones[row : row + 8, :]
            level_one[x + 2, pair + 1] = jnp.where(lower, one, two)
            level_one[x + half_x + 2, pair + 1] = jnp.where(lower, two, one)
    children = jnp.concatenate(
        [
            jnp.concatenate([level_one[2 * x + 2, y + 1], level_one[2 * x + 3, y + 1]], 1)
            for x in range(half_x)
            for y in range(pairs_y)
        ],
        0,
    )
    below = half_x * pairs_y * 8
    low_lanes = lanes((4, 128)) < 64
    sums[0:below, :] = dot_three(children, small[0:256], small[256:512])
    for x in range(half_x):
        for y in range(pairs_y):
            row = (x * pairs_y + y) * 8
            even = sums[pl.ds(row, 4, stride=2), :]
            odd = sums[pl.ds(row + 1, 4, stride=2), :]
            level_two[x + 2, y + 2, 0:4] = jnp.where(low_lanes, even + lane_flip(odd), 0.0)

    def second_group(group_x, group_y):
        return jnp.concatenate(
            [
                level_two[2 * group_x + h + 2, 2 * group_y + 2]
                + lane_flip(level_two[2 * group_x + h + 2, 2 * group_y + 3])
                for h in range(2)
            ],
            1,
        )

    quarter_x, quarter_y = index_x // 4, index_y // 4
    tops = [(x, y) for x in range(count_x // 4) for y in range(count_y // 4)]
    stacked = jnp.concatenate([second_group(x, y) for x, y in tops], 0)
    if stacked.shape[0] % 16 != 0:
        stacked = jnp.concatenate([stacked, jnp.zeros((8, 256), F32)], 0)
    sums[0 : stacked.shape[0], :] = dot_three(stacked, small[0:256], small[256:512])
    top_far = jnp.zeros((16, 128), F32)
    for position, (x, y) in enumerate(tops):
        even = sums[pl.ds(8 * position, 2, stride=2), :]
        odd = sums[pl.ds(8 * position + 1, 2, stride=2), :]
        third = jnp.where(lanes((2, 128)) < 64, even + lane_flip(odd), 0.0)
        third = third[0:1] + lane_flip(third)[1:2]
        step_x, step_y = x - quarter_x + count_x // 4 - 1, y - quarter_y + count_y // 4 - 1
        row = 1536 + 256 * (step_x * (count_y // 4 * 2 - 1) + step_y)
        table = [small[pl.ds(pl.multiple_of(row + 128 * k, 128), 128), :] for k in range(2)]
        top_far = top_far + dot_three(jnp.broadcast_to(third, (16, 128)), table[0], table[1])

    edge = jnp.zeros((8, 256), F32)
    groups = {}
    for gx in (-1, 0, 1):
        for gy in (-1, 0, 1):
            steps = [2 * (index_x // 2 + gx) + h + 2 for h in range(2)]
            first_level = [level_one[step, index_y // 2 + gy + 1] for step in steps]
            second_level = second_group(quarter_x + gx, quarter_y + gy)
            blocks = [edge, jnp.concatenate(first_level, 1), edge, second_level, edge, edge]
            groups[gx, gy] = jnp.concatenate(blocks, 0)
    store_reflected(groups, flips, flipped)
    far = far_sums((-1, 0, 1), ((8, 8), (24, 8)), flipped, flips, tiles)

    def select(block, hx, hy):
        tile = jnp.where(hx == 1, block[:, 128:256], block[:, 0:128])
        return jnp.where(hy == 1, lane_flip(tile), tile)

    def refine(parent):
        keep = lanes((16, 128)) < 64
        parent = jnp.where(keep, parent, 0.0)
        high = parent.astype(BF16).astype(F32)
        low = parent - high
        left = jnp.concatenate([high + lane_flip(low), high], 1).astype(BF16)
        down = jnp.concatenate([small[512 + 256 * k : 768 + 256 * k, :] for k in range(4)], 1)
        spread = dot(left, down)
        for half in range(2):
            for h in range(2):
                span = slice(256 * half + 128 * h, 256 * half + 128 * h + 128)
                local[h, pl.ds(half, 16, stride=2), :] = spread[:, span]
        return jnp.concatenate([local[0], local[1]], 1)

    top_local = jnp.where(
        sublanes((16, 128)) == 0, top_far, jnp.where(sublanes((16, 128)) == 1, lane_flip(top_far), 0.0)
    )
    children_far = refine(top_local)
    half_index_x, half_index_y = index_x // 2, index_y // 2
    second = select(children_far[0:8], lax.rem(half_index_x, 2), lax.rem(half_index_y, 2))
    second = second + 0.25 * select(far[8:16], lax.rem(half_index_x, 2), lax.rem(half_index_y, 2))
    zeros = jnp.zeros((8, 128), F32)
    children_far = refine(jnp.concatenate([second, zeros], 0))
    first = select(children_far[0:8], lax.rem(index_x, 2), lax.rem(index_y, 2))
    first = first + 0.5 * select(far[0:8], lax.rem(index_x, 2), lax.rem(index_y, 2))
    out[...] = refine(jnp.concatenate([first, zeros], 0))[0:16]


def upper_call(count_x, count_y, operands):
    half_x, half_y = count_x // 2, count_y // 2
    scratch = [
        pltpu.VMEM((count_x + 4, half_y + 2, 8, 128), F32),
        pltpu.VMEM((half_x + 4, half_y + 4, 8, 128), F32),
        pltpu.VMEM((3, 3, 2, 2, 2, 48, 128), F32),
        pltpu.VMEM((max(16, half_x * half_y * 8), 128), F32),
        pltpu.VMEM((2, 32, 128), F32),
    ]
    return pl.pallas_call(
        lambda *refs: upper_kernel(count_x, count_y, refs),
        out_shape=jax.ShapeDtypeStruct((LZ, 256), F32),
        in_specs=[VMEM] * len(operands),
        out_specs=VMEM,
        scratch_shapes=scratch,
        compiler_params=pltpu.CompilerParams(vmem_limit_bytes=8 * MIB),
        cost_estimate=pl.CostEstimate(flops=900_000_000, bytes_accessed=600_000, transcendentals=0),
        name="upper",
    )(*operands)


def last_kernel(basis, near_rows, local, far_own, far_beside, out):
    leaf = local[...] + far_own[...] + far_beside[...]

    one, two = halves(leaf)
    turned = jnp.concatenate([one.astype(F32), two.astype(F32)], 0).T.astype(BF16)
    table = leaf_segments(2 * LZ)
    for x in range(CX):
        for y in range(CY):
            column = x * CY + y
            spread = dot(turned[64 * column : 64 * column + 64], table)
            for j in range(ROWS):
                span = slice(128 * j, 128 * j + 128)
                total = None
                for k in range(8):
                    term = basis[column, j, 8 * k : 8 * k + 8, :] * spread[8 * k : 8 * k + 8, span]
                    total = term if total is None else total + term
                value = jnp.sum(total, 0, keepdims=True) + near_rows[column, j : j + 1, :]
                out[x, y : y + 1, span] = value


def last_call(operands):
    return pl.pallas_call(
        last_kernel,
        out_shape=jax.ShapeDtypeStruct((CX, CY, LZ * 64), F32),
        in_specs=[VMEM] * len(operands),
        out_specs=VMEM,
        compiler_params=pltpu.CompilerParams(vmem_limit_bytes=8 * MIB),
        name="last",
    )(*operands)


def in_hbm(value):
    return pltpu.with_memory_space_constraint(value, pltpu.HBM)


def swap_bit(value, axis, bit):
    return lax.ppermute(value, axis, [(i, i ^ (1 << bit)) for i in range(lax.axis_size(axis))])


def relay_ring(value, axis):
    count = lax.axis_size(axis)
    steps = {i: i + 2 if i % 2 == 0 else i - 2 for i in range(count)}
    steps[count - 2], steps[1] = count - 1, 0
    return lax.ppermute(value, axis, list(steps.items()))


def solution(mesh):
    count_x, count_y = mesh.shape["gx"], mesh.shape["gy"]
    levels_x, levels_y = count_x.bit_length() - 1, count_y.bit_length() - 1
    tiles = translation_tiles()
    small = small_tables(count_x // 4, count_y // 4)
    tables = small, reflection_tables(), tiles[:TILES_FIRST], tiles[TILES_FIRST:]

    def body(offsets, charges):
        small, flips, *tiles = [in_hbm(jnp.asarray(table)) for table in tables]
        block = moments_call(in_hbm(offsets), in_hbm(charges), small)
        other = swap_bit(block, "gy", 0)
        exchanged = []

        def exchange_y(after):
            pair = block, other
            for level in range(1, levels_y):
                last = level == levels_y - 1
                rows = (ONE_ROWS << (level - 1)) + EDGE_ROWS * (1 if last else 2)
                kernel = functools.partial(group_kernel, level, last)
                sent = pack_call(kernel, rows, (*pair, after), "group")
                pair = sent, swap_bit(sent, "gy", level)
                exchanged.extend(pair)
            return exchanged[0]

        near, targets, small, first_tiles = own_call(block, exchange_y, small, tiles[0])
        row = row_call(levels_y, (block, other, *exchanged, near))
        partner = swap_bit(row, "gx", 0)
        near, flips, other_tiles = beside_y_call(row, targets, near, (flips, tiles[1]))
        leaves, basis = own_leaves_call(row, flips, block)
        far_own = far_own_call(leaves, flips, first_tiles)
        rows = ONE_ROWS << (levels_y - 1)
        ones = merge_call(0, row, partner, ROW_BOTH, rows, SENT_ROWS, far_own)
        other_ones = swap_bit(ones, "gx", 1)
        beyond = relay_ring(relay_call(partner, ones), "gx")
        near = near_call(beside_x_kernel, (partner, targets, near, ones), 8, 10, 1_200_000, "near_x")
        for bit in range(1, levels_x - 1):
            ones = merge_call(bit, ones, other_ones, 0, rows << bit, 0, near)
            other_ones = swap_bit(ones, "gx", bit + 1)
        far_tables = flips, first_tiles, other_tiles
        near, far_beside = beyond_call((near, partner, beyond, targets, *far_tables, ones))
        local = upper_call(count_x, count_y, (ones, other_ones, small, *far_tables, near))
        return last_call((basis, near, local, far_own, far_beside))

    in_specs = (P(None, "gx", "gy", None), P("gx", "gy", None))
    out_specs = P("gx", "gy", None)
    return jax.shard_map(body, mesh=mesh, in_specs=in_specs, out_specs=out_specs, check_vma=False)
```

```python
import functools
import itertools

import jax
import jax.numpy as jnp
import ml_dtypes
import numpy as np
from jax import lax
from jax.experimental import pallas as pl
from jax.experimental.pallas import tpu as pltpu
from jax.sharding import PartitionSpec as P

F32 = jnp.float32
BF16 = jnp.bfloat16
MIB = 1 << 20

CX = 2
CY = 2
LZ = 16
ROWS = 8
FEATURES = 32
VMEM = pl.BlockSpec(memory_space=pltpu.VMEM)
HBM = pl.BlockSpec(memory_space=pltpu.HBM)


def nodes_1d():
    return np.cos((2.0 * np.arange(4) + 1.0) * np.pi / 8.0)


def cheb_terms(value):
    return value, 2.0 * value * value - 1.0, 4.0 * value**3 - 3.0 * value


def node_weights():
    return [[0.5 * term for term in cheb_terms(point)] for point in nodes_1d()]


def node_grid():
    points = nodes_1d()
    counter = np.arange(64)
    return np.stack([points[counter // 16], points[counter // 4 % 4], points[counter % 4]], -1)


def split_two(table):
    high = table.astype(np.float32).astype(ml_dtypes.bfloat16)
    low = (table - high.astype(np.float64)).astype(np.float32).astype(ml_dtypes.bfloat16)
    return high, low


def upward_tensor():
    points = nodes_1d()
    shifted = (points[None, :] + 2.0 * np.arange(2)[:, None] - 1.0) / 2.0
    factor = 0.25 + 0.0 * shifted[..., None]
    for of_value, of_node in zip(cheb_terms(shifted), cheb_terms(points)):
        factor = factor + 0.5 * of_value[..., None] * of_node
    full = np.einsum("xia,yjb,zkc->xyzijkabc", factor, factor, factor)
    return full.reshape(2, 2, 2, 64, 64)


def inverse_distance(offset):
    grid = node_grid()
    spread = (grid[None, :, :] - grid[:, None, :]) / 2.0 - np.asarray(offset, np.float64)
    return 1.0 / np.sqrt(np.sum(spread * spread, -1))


def adjacent(offset):
    return max(abs(int(step)) for step in offset) <= 1


def canonical_tiles():
    return [
        (cx, cy, cz)
        for cx in range(2)
        for cy in range(2)
        for cz in range(4)
        if not (cx == 0 and cy == 0 and cz <= 1)
    ]


TILES_FIRST = 10


def translation_tiles():
    tiles = []
    for cx, cy, cz in canonical_tiles():
        tile = np.zeros((4, 64, 4, 64))
        for source in range(4):
            for target in range(4):
                offset = (
                    2 * cx + source // 2 - target // 2,
                    2 * cy + source % 2 - target % 2,
                    cz,
                )
                if not adjacent(offset):
                    tile[source, :, target, :] = inverse_distance(offset)
        tiles.append(tile.reshape(256, 256))
    return np.stack(split_two(np.stack(tiles)), 1)


def reflection_matrix(flip_x, flip_y, flip_z):
    index = np.arange(256)
    hx, hy, a, b, c = index // 128, index // 64 % 2, index // 16 % 4, index // 4 % 4, index % 4
    if flip_x:
        hx, a = 1 - hx, 3 - a
    if flip_y:
        hy, b = 1 - hy, 3 - b
    if flip_z:
        c = 3 - c
    matrix = np.zeros((256, 256), np.float32)
    matrix[hx * 128 + hy * 64 + a * 16 + b * 4 + c, index] = 1.0
    return matrix


def reflection_tables():
    pairs = [
        np.concatenate([reflection_matrix(fx, fy, 0), reflection_matrix(fx, fy, 1)], 1)
        for fx in range(2)
        for fy in range(2)
    ]
    return np.stack(pairs).astype(ml_dtypes.bfloat16)


def up_tables():
    upward = upward_tensor()
    table = upward.transpose(0, 1, 3, 2, 4).reshape(256, 128)
    return np.stack(split_two(table))


def down_table():
    upward = upward_tensor()
    table = upward.transpose(4, 2, 0, 1, 3).reshape(64, 512)
    high, low = split_two(table)
    return np.concatenate([high, high, low, np.zeros_like(low)], 0)


def top_tables(boxes_x, boxes_y):
    offsets = range(-(boxes_x - 1), boxes_x), range(-(boxes_y - 1), boxes_y)
    table = np.zeros((len(offsets[0]), len(offsets[1]), 2, 64, 2, 64))
    for (ix, dx), (iy, dy) in itertools.product(enumerate(offsets[0]), enumerate(offsets[1])):
        for source, target in itertools.product(range(2), range(2)):
            offset = (dx, dy, source - target)
            if not adjacent(offset):
                table[ix, iy, source, :, target, :] = 0.125 * inverse_distance(offset)
    return np.stack(split_two(table.reshape(len(offsets[0]), len(offsets[1]), 128, 128)), 2)


def small_tables(boxes_x, boxes_y):
    down = down_table().reshape(256, 4, 128).transpose(1, 0, 2)
    parts = [up_tables(), down, top_tables(boxes_x, boxes_y)]
    return np.concatenate([part.reshape(-1, 128) for part in parts], 0)


def halves(value):
    high = value.astype(BF16)
    return high, (value - high.astype(F32)).astype(BF16)


def dot(left, right):
    return jnp.dot(left, right, preferred_element_type=F32)


def dot_three(value, high_table, low_table):
    rows = value.shape[0]
    high, low = halves(value)
    both = dot(jnp.concatenate([high, low], 0), high_table)
    return both[:rows] + both[rows:] + dot(high, low_table)


def lanes(shape):
    return lax.broadcasted_iota(jnp.int32, shape, len(shape) - 1)


def sublanes(shape):
    return lax.broadcasted_iota(jnp.int32, shape, len(shape) - 2)


def leaf_segments(leaves):
    shape = (leaves, LZ * 64)
    return jnp.where(lanes(shape) // 64 == lax.rem(sublanes(shape), LZ), 1.0, 0.0).astype(BF16)


def lane_flip(value):
    return pltpu.roll(value, 64, 1)


def weight_rows(pattern):
    weights = node_weights()
    index = sublanes((8, 128))
    rows = []
    for term in range(3):
        row = jnp.full((8, 128), weights[pattern(0)][term], F32)
        for sub in range(1, 8):
            row = jnp.where(index == sub, weights[pattern(sub)][term], row)
        rows.append(row)
    return rows


def basis_rows():
    return (
        weight_rows(lambda sub: sub // 4),
        weight_rows(lambda sub: 2 + sub // 4),
        weight_rows(lambda sub: sub % 4),
    )


def basis_tile(row_x, row_y, row_z, scale, tables):
    y_low, y_high, z_all = tables
    wide = [jnp.broadcast_to(2.0 * row - 1.0, (8, 128)) for row in (row_x, row_y, row_z)]
    terms = [cheb_terms(value) for value in wide]

    def mix(weights, term):
        return 0.25 + (weights[0] * term[0] + weights[1] * term[1] + weights[2] * term[2])

    along_z = mix(z_all, terms[2])
    pair = mix(y_low, terms[1]) * along_z, mix(y_high, terms[1]) * along_z
    tiles = []
    for weights in node_weights():
        along_x = mix(weights, terms[0])
        if scale is not None:
            along_x = along_x * scale
        tiles += [along_x * pair[0], along_x * pair[1]]
    return tiles


def three_pieces(value):
    first = value.astype(BF16).astype(F32)
    rest = value - first
    second = rest.astype(BF16).astype(F32)
    return first, second, rest - second


PIECES = 12


def feature_pieces(coords, scale):
    total = coords[0] * coords[0] + coords[1] * coords[1] + coords[2] * coords[2]
    return [piece for value in [scale * coord for coord in coords] + [total] for piece in three_pieces(value)]


def pick(row, pieces, choice):
    value = jnp.broadcast_to(pieces[choice[0]], (8, 128))
    for piece in sorted(set(choice) - {choice[0]}):
        mask = None
        for place, chosen in enumerate(choice):
            if chosen == piece:
                mask = row == place if mask is None else mask | (row == place)
        value = jnp.where(mask, jnp.broadcast_to(pieces[piece], (8, 128)), value)
    return value


def feature_block(read, choice, length_choice):
    row = sublanes((8, 128))
    zero, one = jnp.zeros((1, 128), F32), jnp.ones((1, 128), F32)
    blocks = [
        pick(row, [read(3 * c), read(3 * c + 1), read(3 * c + 2), zero], choice) for c in range(3)
    ]
    blocks.append(pick(row, [read(9), read(10), read(11), one, zero], length_choice))
    return jnp.concatenate(blocks, 0)


SOURCE_CHOICE = (0, 1, 0, 1, 2, 0, 0, 0), (3, 3, 3, 0, 1, 2, 3, 3)
TARGET_CHOICE = (0, 0, 1, 1, 0, 2, 3, 3), (0, 1, 2, 3, 3, 3, 4, 4)


def column(raw, x, y):
    return raw(0) + (x - 2.0), raw(1) + (y - 2.0), raw(2), raw(3)


class Near:
    def __init__(self, wide_ref, charge_ref, target_ref):
        self.wide_ref = wide_ref
        self.charge_ref = charge_ref
        self.target_ref = target_ref
        self.groups = 0
        self.charges = 0
        self.upper = lanes((ROWS, 128)) >= 64
        self.row = sublanes((ROWS, 128))

    def in_pair(self, along_z):
        return along_z + jnp.where(self.upper, 0.0, -1.0)

    def targets(self, columns):
        for ab, (x, y, z, _) in enumerate(columns):
            pieces = feature_pieces((x, y, self.in_pair(z)), -2.0)
            for j in range(ROWS):
                block = feature_block(lambda k: pieces[k][j : j + 1], *TARGET_CHOICE)
                self.target_ref[ab, j] = block.T.astype(BF16)

    def add_group(self, coords):
        for k, piece in enumerate(feature_pieces(coords, 1.0)):
            self.wide_ref[self.groups, k] = piece
        self.groups += 1
        return self.groups - 1

    def add_charge(self, charge):
        self.charge_ref[self.charges] = charge
        self.charges += 1
        return self.charges - 1

    def main(self, source):
        x, y, z, charge = source
        return self.add_group((x, y, self.in_pair(z))), self.add_charge(charge)

    def outer(self, first, second, side, keep=False):
        def merge(one, two):
            if side == 0:
                value = jnp.where(self.upper, two, lane_flip(one))
                return pltpu.roll(value, 1, 0)
            value = jnp.where(self.upper, lane_flip(two), one)
            return pltpu.roll(value, ROWS - 1, 0)

        x, y, z, charge = [merge(one, two) for one, two in zip(first, second)]
        charge = jnp.where(self.row == (0 if side == 0 else ROWS - 1), 0.0, charge)
        group = self.add_group((x, y, z + (-2.0 if side == 0 else 1.0)))
        if not keep:
            return group, self.add_charge(charge)
        low = self.add_charge(jnp.where(self.upper, 0.0, charge))
        high = self.add_charge(jnp.where(self.upper, charge, 0.0))
        return (group, low), (group, high)

    def run(self, plan, emit):
        eye = sublanes((128, 128)) == lanes((128, 128))

        def source(group, j, built):
            if group not in built:
                read = lambda k: self.wide_ref[group, k, pl.ds(j, 1), :]
                built[group] = feature_block(read, *SOURCE_CHOICE).astype(BF16)
            return built[group]

        def pairs(targets, tiles, j, own, total, built):
            block = jnp.concatenate([source(group, j, built) for group, _ in tiles], 1)
            squared = dot(targets, block)
            for position, (group, charge) in enumerate(tiles):
                inverse = lax.rsqrt(squared[:, 128 * position : 128 * position + 128])
                if group == own:
                    inverse = jnp.where(eye, 0.0, inverse)
                total = total + inverse * self.charge_ref[charge, pl.ds(j, 1), :]
            return total

        def step(j, carry):
            built = {}
            for ab, mains, below, above, own in plan:
                targets = self.target_ref[ab, j]
                total = pairs(targets, mains, j, own, jnp.zeros((128, 128), F32), built)
                lower = pairs(targets[:64], below, j, None, total[:64], built)
                higher = pairs(targets[64:], above, j, None, total[64:], built)
                total = jnp.concatenate([lower, higher], 0)
                emit(ab, j, jnp.sum(total.T, 0, keepdims=True))
            return carry

        lax.fori_loop(0, ROWS, step, 0, unroll=True)


def plan_own(near, columns):
    mains = [near.main(source) for source in columns]
    outer = [
        [near.outer(columns[2 * x], columns[2 * x + 1], side) for x in range(2)]
        for side in range(2)
    ]
    return [(ab, mains, outer[0], outer[1], mains[ab][0]) for ab in range(4)]


def plan_beside_y(near, columns):
    plan = []
    for b in range(2):
        mains = [near.main(source) for source in columns[b]]
        outer = [[near.outer(*columns[b], side)] for side in range(2)]
        plan += [(2 * a + b, mains, outer[0], outer[1], None) for a in range(2)]
    return plan


def plan_beside_x(near, columns, side_x):
    mains = [near.main(source) for source in columns]
    middle = [near.outer(columns[1], columns[2], side) for side in range(2)]
    ends = [near.outer(columns[0], columns[3], side, keep=True) for side in range(2)]
    return [
        (2 * side_x + b, mains[b : b + 3], [middle[0], ends[0][b]], [middle[1], ends[1][b]], None)
        for b in range(2)
    ]


def near_scratch(groups, charges):
    return [
        pltpu.VMEM((groups, PIECES, ROWS, 128), F32),
        pltpu.VMEM((charges, ROWS, 128), F32),
    ]


NEAR_SHAPE = (4, ROWS, 128)


def near_cost(pairs):
    return pl.CostEstimate(flops=40 * pairs, bytes_accessed=600_000, transcendentals=pairs)


ONE_ROWS = 8
LEAF_ROWS = 32
PART_ROWS = 4 * CX * CY * ROWS
OWN_ROWS = ONE_ROWS + LEAF_ROWS + PART_ROWS


def part_row(c, x, y):
    return ONE_ROWS + LEAF_ROWS + ((c * CX + x) * CY + y) * ROWS


def moments_kernel(
    offsets_hbm, charges_hbm, small_hbm, block, offsets, charges, up, basis, sums, semaphores
):
    index_y = lax.axis_index("gy")
    copies = [
        pltpu.make_async_copy(offsets_hbm, offsets, semaphores.at[0]),
        pltpu.make_async_copy(charges_hbm, charges, semaphores.at[1]),
        pltpu.make_async_copy(small_hbm.at[0:512], up, semaphores.at[2]),
    ]
    for copy in copies:
        copy.start()
    tables = basis_rows()
    segments = leaf_segments(LZ)
    copies[0].wait()
    copies[1].wait()
    for x in range(CX):
        for y in range(CY):
            for j in range(ROWS):
                span = slice(128 * j, 128 * j + 128)
                rows = [offsets[c, x, y : y + 1, span] for c in range(3)]
                charge = charges[x, y : y + 1, span]
                for c, row in enumerate(rows + [charge]):
                    place = part_row(c, x, y) + j
                    block[place : place + 1, :] = row
                tiles = basis_tile(*rows, charge, tables)
                for k in range(4):
                    pair = jnp.concatenate(tiles[2 * k : 2 * k + 2], 0)
                    high, low = halves(pair)
                    first = (x * CY + y) * 64 + 16 * k
                    basis[0, first : first + 16, span] = high
                    basis[1, first : first + 16, span] = low
    contract = (((1,), (1,)), ((), ()))
    leaf = lax.dot_general(segments, basis[0], contract, preferred_element_type=F32)
    leaf = leaf + lax.dot_general(segments, basis[1], contract, preferred_element_type=F32)
    copies[2].wait()
    sums[...] = dot_three(leaf, up[0:256], up[256:512])
    first = sums[pl.ds(0, 8, stride=2), :] + lane_flip(sums[pl.ds(1, 8, stride=2), :])
    first = jnp.where(lanes((8, 128)) < 64, first, 0.0)
    first = jnp.where(lax.rem(index_y, 2) == 1, lane_flip(first), first)
    block[0:8, :] = first
    block[8:24, :] = leaf[:, :128]
    block[24:40, :] = leaf[:, 128:]


def moments_call(offsets, charges, small):
    return pl.pallas_call(
        moments_kernel,
        out_shape=jax.ShapeDtypeStruct((OWN_ROWS, 128), F32),
        in_specs=[HBM] * 3,
        out_specs=VMEM,
        scratch_shapes=[
            pltpu.VMEM(offsets.shape, F32),
            pltpu.VMEM(charges.shape, F32),
            pltpu.VMEM((512, 128), BF16),
            pltpu.VMEM((2, 256, 1024), BF16),
            pltpu.VMEM((16, 128), F32),
            pltpu.SemaphoreType.DMA((3,)),
        ],
        compiler_params=pltpu.CompilerParams(vmem_limit_bytes=8 * MIB),
        cost_estimate=pl.CostEstimate(flops=10_000_000, bytes_accessed=300_000, transcendentals=0),
        name="moments",
    )(offsets, charges, small)


EDGE_ROWS = LEAF_ROWS + 4 * CX * ROWS


def bits_below(index, bit):
    return lax.rem(index, 1 << bit)


def bit_of(index, bit):
    return lax.rem(index // (1 << bit), 2)


def in_order(is_first, own, other):
    return jnp.concatenate([jnp.where(is_first, own, other), jnp.where(is_first, other, own)], 0)


def edge_block(block, y):
    rows = [block[ONE_ROWS : ONE_ROWS + LEAF_ROWS, :]]
    for c in range(4):
        for x in range(CX):
            rows.append(block[part_row(c, x, y) : part_row(c, x, y) + ROWS, :])
    return jnp.concatenate(rows, 0)


def group_kernel(level, last_level, own_ref, other_ref, after, out):
    index = lax.axis_index("gy")
    ones = ONE_ROWS << (level - 1)
    is_first = bit_of(index, level - 1) == 0
    if level == 1:
        out[0:ones, :] = own_ref[0:ones, :] + other_ref[0:ones, :]
        first = jnp.where(is_first, edge_block(own_ref, 0), edge_block(other_ref, 0))
        last = jnp.where(is_first, edge_block(other_ref, 1), edge_block(own_ref, 1))
    else:
        half = ones // 2
        out[0:ones, :] = in_order(is_first, own_ref[0:half, :], other_ref[0:half, :])
        own_far = own_ref[half + EDGE_ROWS : half + 2 * EDGE_ROWS, :]
        other_far = other_ref[half + EDGE_ROWS : half + 2 * EDGE_ROWS, :]
        first = jnp.where(is_first, own_far, other_far)
        last = jnp.where(is_first, other_far, own_far)
    lower = bit_of(index, level) == 0
    out[ones : ones + EDGE_ROWS, :] = jnp.where(lower, last, first)
    if not last_level:
        out[ones + EDGE_ROWS : ones + 2 * EDGE_ROWS, :] = jnp.where(lower, first, last)


def pack_call(kernel, rows, operands, name):
    return pl.pallas_call(
        kernel,
        out_shape=jax.ShapeDtypeStruct((rows, 128), F32),
        in_specs=[VMEM] * len(operands),
        out_specs=VMEM,
        compiler_params=pltpu.CompilerParams(vmem_limit_bytes=8 * MIB),
        cost_estimate=pl.CostEstimate(flops=100_000, bytes_accessed=300_000, transcendentals=0),
        name=name,
    )(*operands)


ROW_LEAF = 3 * LEAF_ROWS
ROW_PART = 4 * 4 * ROWS
ROW_ROWS = ROW_LEAF + ROW_PART


def row_part(c, y):
    return ROW_LEAF + (c * 4 + y) * ROWS


def row_kernel(levels, block, other, *refs):
    exchanged, (out, far_out) = refs[: 2 * (levels - 1)], refs[-2:]
    index = lax.axis_index("gy")
    even = lax.rem(lax.axis_index("gx"), 2) == 0
    is_first = bit_of(index, 0) == 0
    low = jnp.where(is_first, 0.0, edge_block(other, 1))
    high = jnp.where(is_first, edge_block(other, 0), 0.0)
    ones = ONE_ROWS
    for level in range(1, levels):
        own, received = exchanged[2 * level - 2 : 2 * level]
        ones = ONE_ROWS << (level - 1)
        facing = received[ones : ones + EDGE_ROWS, :]
        below = bits_below(index, level)
        upper = bit_of(index, level) == 1
        low = jnp.where(upper & (below == 0), facing, low)
        high = jnp.where(~upper & (below == (1 << level) - 1), facing, high)
        if level == levels - 1:
            out[ROW_ROWS:, :] = in_order(~upper, own[0:ones, :], received[0:ones, :])
    leaf = block[ONE_ROWS : ONE_ROWS + LEAF_ROWS, :]
    for piece, rows in enumerate((low[0:LEAF_ROWS], leaf, high[0:LEAF_ROWS])):
        out[LEAF_ROWS * piece : LEAF_ROWS * (piece + 1), :] = rows
    for c in range(4):
        columns = []
        for x in range(CX):
            row = LEAF_ROWS + (c * CX + x) * ROWS
            own = [block[part_row(c, x, y) : part_row(c, x, y) + ROWS, :] for y in range(CY)]
            columns.append([low[row : row + ROWS], *own, high[row : row + ROWS]])
        for y in range(4):
            facing, far = row_part(c, y), row_part(c, y) - ROW_LEAF
            out[facing : facing + ROWS, :] = jnp.where(even, columns[1][y], columns[0][y])
            far_out[far : far + ROWS, :] = jnp.where(even, columns[0][y], columns[1][y])


def row_call(levels, operands):
    return pl.pallas_call(
        lambda *refs: row_kernel(levels, *refs[: 2 * levels], *refs[-2:]),
        out_shape=[
            jax.ShapeDtypeStruct((rows, 128), F32)
            for rows in (ROW_ROWS + (ONE_ROWS << (levels - 1)), ROW_PART)
        ],
        in_specs=[VMEM] * len(operands),
        out_specs=[VMEM] * 2,
        compiler_params=pltpu.CompilerParams(vmem_limit_bytes=8 * MIB),
        cost_estimate=pl.CostEstimate(flops=100_000, bytes_accessed=600_000, transcendentals=0),
        name="row",
    )(*operands)


SENT_ROWS = 192


def merge_call(bit, own, other, first, rows, least, after):
    total = max(2 * rows, least)

    def kernel(own_ref, other_ref, after_ref, out):
        is_first = bit_of(lax.axis_index("gx"), bit) == 0
        span = slice(first, first + rows)
        out[0 : 2 * rows, :] = in_order(is_first, own_ref[span, :], other_ref[span, :])
        if total > 2 * rows:
            out[2 * rows :, :] = jnp.zeros((total - 2 * rows, 128), F32)

    return pack_call(kernel, total, (own, other, after), "merge")


def relay_call(received, received_far, after):
    def kernel(received_ref, far_ref, after_ref, out):
        out[0:ROW_LEAF, :] = received_ref[0:ROW_LEAF, :]
        out[ROW_LEAF:ROW_ROWS, :] = far_ref[...]

    return pack_call(kernel, ROW_ROWS, (received, received_far, after), "relay")


def own_kernel(block, targets, features, charges):
    near = Near(features, charges, targets)

    def raw(x, y):
        return lambda c: block[part_row(c, x, y) : part_row(c, x, y) + ROWS, :]

    columns = [column(raw(ab // 2, ab % 2), ab // 2 + 1, ab % 2 + 1) for ab in range(4)]
    near.targets(columns)
    return near, plan_own(near, columns)


def own_call(block, after, small, tiles):
    plans = []

    def prepare(block_ref, small, targets, features, charges, small_out, semaphore):
        copy = pltpu.make_async_copy(small, small_out, semaphore)
        copy.start()
        plans.append(own_kernel(block_ref, targets, features, charges)[1])
        copy.wait()

    def run(targets, features, charges, after_ref, tiles, out, tiles_out, semaphore):
        copy = pltpu.make_async_copy(tiles, tiles_out, semaphore)
        copy.start()

        def emit(ab, j, row):
            out[ab, pl.ds(j, 1), :] = row

        Near(features, charges, targets).run(plans[0], emit)
        copy.wait()

    prepared = pl.pallas_call(
        prepare,
        out_shape=(
            jax.ShapeDtypeStruct((4, ROWS, 128, FEATURES), BF16),
            jax.ShapeDtypeStruct((8, PIECES, ROWS, 128), F32),
            jax.ShapeDtypeStruct((8, ROWS, 128), F32),
            jax.ShapeDtypeStruct(small.shape, BF16),
        ),
        in_specs=[VMEM, HBM],
        out_specs=(VMEM,) * 4,
        scratch_shapes=[pltpu.SemaphoreType.DMA],
        compiler_params=pltpu.CompilerParams(vmem_limit_bytes=8 * MIB),
        cost_estimate=near_cost(500_000),
        name="features",
    )(block, small)
    near, tiles_near = pl.pallas_call(
        run,
        out_shape=(
            jax.ShapeDtypeStruct(NEAR_SHAPE, F32),
            jax.ShapeDtypeStruct(tiles.shape, BF16),
        ),
        in_specs=[VMEM] * 4 + [HBM],
        out_specs=(VMEM,) * 2,
        scratch_shapes=[pltpu.SemaphoreType.DMA],
        compiler_params=pltpu.CompilerParams(vmem_limit_bytes=8 * MIB),
        cost_estimate=near_cost(4_500_000),
        name="near_own",
    )(*prepared[:3], after(prepared[2]), tiles)
    return near, prepared[0], prepared[3], tiles_near


def beside_y_kernel(
    row_ref, far_ref, targets, before, flips, tiles, out, flips_out, tiles_out, wide_ref, charge_ref, semaphores
):
    copies = [
        pltpu.make_async_copy(flips, flips_out, semaphores.at[0]),
        pltpu.make_async_copy(tiles, tiles_out, semaphores.at[1]),
    ]
    for copy in copies:
        copy.start()
    even = lax.rem(lax.axis_index("gx"), 2) == 0
    near = Near(wide_ref, charge_ref, targets)

    def raw(x, y):
        def read(c):
            facing, far = row_part(c, y), row_part(c, y) - ROW_LEAF
            own = row_ref[facing : facing + ROWS, :], far_ref[far : far + ROWS, :]
            return jnp.where(even == (x == 1), *own)

        return read

    columns = [[column(raw(x, y), x + 1, y) for x in range(2)] for y in (0, 3)]
    plan = plan_beside_y(near, columns)
    out[...] = before[...]

    def emit(ab, j, row):
        out[ab, pl.ds(j, 1), :] = out[ab, pl.ds(j, 1), :] + row

    near.run(plan, emit)
    for copy in copies:
        copy.wait()


def beside_y_call(row, far, targets, before, constants):
    near_shape = jax.ShapeDtypeStruct(NEAR_SHAPE, F32)
    tables = [jax.ShapeDtypeStruct(constant.shape, BF16) for constant in constants]
    return pl.pallas_call(
        beside_y_kernel,
        out_shape=(near_shape, *tables),
        in_specs=[VMEM] * 4 + [HBM] * 2,
        out_specs=(VMEM,) * 3,
        scratch_shapes=near_scratch(8, 8) + [pltpu.SemaphoreType.DMA((2,))],
        compiler_params=pltpu.CompilerParams(vmem_limit_bytes=8 * MIB),
        cost_estimate=near_cost(2_200_000),
        name="near_y",
    )(row, far, targets, before, *constants)


def beside_x(parity, received, targets, out, wide_ref, charge_ref):
    index, count = lax.axis_index("gx"), lax.axis_size("gx")
    even = lax.rem(index, 2) == 0
    side = jnp.where(even == (parity == 0), 1, 0)
    alone = (index == 0) | (index == count - 1)
    near = Near(wide_ref, charge_ref, targets)

    def raw(y):
        def coordinate(c):
            value = received[row_part(c, y) : row_part(c, y) + ROWS, :]
            return jnp.where(alone, 0.0, value) if c == 3 and parity == 1 else value

        return coordinate

    columns = [column(raw(y), 3.0 * side.astype(F32), y) for y in range(4)]
    plan = plan_beside_x(near, columns, side)

    def emit(ab, j, row):
        out[ab, pl.ds(j, 1), :] = out[ab, pl.ds(j, 1), :] + row

    near.run(plan, emit)


def beside_x_kernel(received, targets, before, after, out, wide_ref, charge_ref):
    out[...] = before[...]
    beside_x(0, received, targets, out, wide_ref, charge_ref)


def near_call(kernel, operands, groups, charges, pairs, name):
    return pl.pallas_call(
        kernel,
        out_shape=jax.ShapeDtypeStruct(NEAR_SHAPE, F32),
        in_specs=[VMEM] * len(operands),
        out_specs=VMEM,
        scratch_shapes=near_scratch(groups, charges),
        compiler_params=pltpu.CompilerParams(vmem_limit_bytes=12 * MIB),
        cost_estimate=near_cost(pairs),
        name=name,
    )(*operands)


def store_reflected(moments, flips, flipped):
    def store(group, z, part, value):
        for half in range(2):
            place = flipped.at[group[0] + 1, group[1] + 1, z, part, half]
            place[...] = value[:, 128 * half : 128 * half + 128]

    parts = {group: halves(value) for group, value in moments.items()}
    for fx in range(2):
        for fy in range(2):
            groups = [group for group in moments if (group[0] < 0, group[1] < 0) == (fx == 1, fy == 1)]
            if not groups:
                continue
            stacked = jnp.concatenate([part for group in groups for part in parts[group]], 0)
            rows = stacked.shape[0] // (2 * len(groups))
            first = 0 if fx + fy > 0 else 1
            mixed = dot(stacked, flips[2 * fx + fy, :, 256 * first :])
            for order, group in enumerate(groups):
                for part in range(2):
                    start = rows * (2 * order + part)
                    if first == 1:
                        store(group, 0, part, parts[group][part].astype(F32))
                    for z in range(first, 2):
                        span = slice(256 * (z - first), 256 * (z - first) + 256)
                        store(group, z, part, mixed[start : start + rows, span])


def far_sums(columns, spans, flipped, flips, tiles):
    odd_row = lax.rem(sublanes((16, 256)), 2) == 1
    totals = {}
    for position, (cx, cy, cz) in enumerate(canonical_tiles()):
        entries = [
            (gx, gy, dz)
            for gx in sorted({cx, -cx})
            for gy in sorted({cy, -cy})
            for dz in sorted({cz, -cz})
            if gx in columns
        ]
        if not entries:
            continue
        pieces = [[], []]
        for gx, gy, dz in entries:
            for part in range(2):
                view = flipped.at[gx + 1, gy + 1, int(dz < 0), part]
                windows = [
                    [view[half, first + dz : first + dz + size, :] for first, size in spans]
                    for half in range(2)
                ]
                block = jnp.concatenate([jnp.concatenate(window, 0) for window in windows], 1)
                if abs(dz) == 3:
                    block = jnp.where(odd_row if dz < 0 else ~odd_row, block, 0.0)
                pieces[part].append(block.astype(BF16))
        rows = 16 * len(entries)
        part = tiles[0] if position < TILES_FIRST else tiles[1]
        tile = part.at[position % TILES_FIRST]
        both = dot(jnp.concatenate(pieces[0] + pieces[1], 0), tile[0])
        result = both[:rows] + both[rows:] + dot(jnp.concatenate(pieces[0], 0), tile[1])
        for order, (gx, gy, dz) in enumerate(entries):
            key = (int(gx < 0), int(gy < 0), int(dz < 0))
            piece = result[16 * order : 16 * order + 16]
            totals[key] = totals[key] + piece if key in totals else piece
    far = None
    for (fx, fy, fz), total in totals.items():
        if (fx, fy, fz) != (0, 0, 0):
            high, low = halves(total)
            table = flips[2 * fx + fy, :, 256 * fz : 256 * fz + 256]
            both = dot(jnp.concatenate([high, low], 0), table)
            total = both[:16] + both[16:]
        far = total if far is None else far + total
    return far


def store_leaves(columns, halos, flips, flipped):
    index, count = lax.axis_index("gx"), lax.axis_size("gx")
    is_even = lax.rem(index, 2) == 0
    edge = jnp.zeros((8, 128), F32)
    groups = {}
    for gx in columns:
        for gy in (-1, 0, 1):
            tiles_h = []
            for h in range(2):
                row = LEAF_ROWS * (gy + 1) + 16 * h
                rows = slice(row, row + 16)
                moments = halos[0][rows, :]
                if gx != 0:
                    moments = jnp.where(is_even == (gx == 1), moments, halos[1][rows, :])
                    inside = index > 0 if gx < 0 else index < count - 1
                    moments = jnp.where(inside, moments, 0.0)
                tiles_h.append(jnp.concatenate([edge, moments, edge], 0))
            groups[gx, gy] = jnp.concatenate(tiles_h, 1)
    store_reflected(groups, flips, flipped)


LEAF_SHAPE = (3, 3, 2, 2, 2, 32, 128)
LEAF_SPANS = ((8, 16),)


def far_call(kernel, shape, operands, name):
    return pl.pallas_call(
        kernel,
        out_shape=jax.ShapeDtypeStruct(shape, F32),
        in_specs=[VMEM] * len(operands),
        out_specs=VMEM,
        compiler_params=pltpu.CompilerParams(vmem_limit_bytes=8 * MIB),
        cost_estimate=pl.CostEstimate(flops=300_000_000, bytes_accessed=600_000, transcendentals=0),
        name=name,
    )(*operands)


def own_leaves_call(row, flips, block):
    def kernel(row_ref, flips_ref, block_ref, out, basis_out):
        store_leaves((0,), (row_ref,), flips_ref, out)
        tables = basis_rows()
        for x in range(CX):
            for y in range(CY):
                for j in range(ROWS):
                    places = [part_row(c, x, y) + j for c in range(3)]
                    rows = [block_ref[place : place + 1, :] for place in places]
                    for k, tile in enumerate(basis_tile(*rows, None, tables)):
                        basis_out[x * CY + y, j, 8 * k : 8 * k + 8, :] = tile

    shapes = LEAF_SHAPE, (CX * CY, ROWS, 64, 128)
    return pl.pallas_call(
        kernel,
        out_shape=[jax.ShapeDtypeStruct(shape, F32) for shape in shapes],
        in_specs=[VMEM] * 3,
        out_specs=[VMEM] * 2,
        compiler_params=pltpu.CompilerParams(vmem_limit_bytes=8 * MIB),
        cost_estimate=near_cost(100_000),
        name="own_leaves",
    )(row, flips, block)


def far_own_call(leaves, flips, tiles):
    def kernel(leaves_ref, flips_ref, tiles_ref, out):
        out[...] = far_sums((0,), LEAF_SPANS, leaves_ref, flips_ref, (tiles_ref,))

    return far_call(kernel, (LZ, 256), (leaves, flips, tiles), "far_own")


def beyond_kernel(
    before, partner, beyond, targets, flips, one, two, after, out, far_out, wide_ref, charge_ref, leaves
):
    out[...] = before[...]
    beside_x(1, beyond, targets, out, wide_ref, charge_ref)
    store_leaves((-1, 1), (partner, beyond), flips, leaves)
    far_out[...] = far_sums((-1, 1), LEAF_SPANS, leaves, flips, (one, two))


def beyond_call(operands):
    return pl.pallas_call(
        beyond_kernel,
        out_shape=(jax.ShapeDtypeStruct(NEAR_SHAPE, F32), jax.ShapeDtypeStruct((LZ, 256), F32)),
        in_specs=[VMEM] * len(operands),
        out_specs=(VMEM,) * 2,
        scratch_shapes=near_scratch(8, 10) + [pltpu.VMEM(LEAF_SHAPE, F32)],
        compiler_params=pltpu.CompilerParams(vmem_limit_bytes=12 * MIB),
        cost_estimate=near_cost(2_400_000),
        name="beyond",
    )(*operands)


def upper_kernel(count_x, count_y, refs):
    own_ones, other_ones, small, flips, *tiles, _, out = refs[:8]
    refs = refs[8:]
    level_one, level_two, flipped, sums, local = refs

    index_x, index_y = lax.axis_index("gx"), lax.axis_index("gy")
    pairs_y = count_y // 2

    level_one[...] = jnp.zeros_like(level_one)
    level_two[...] = jnp.zeros_like(level_two)
    half_x = count_x // 2
    lower = index_x < half_x
    for x in range(half_x):
        for pair in range(pairs_y):
            row = 8 * (x * pairs_y + pair)
            one, two = own_ones[row : row + 8, :], other_ones[row : row + 8, :]
            level_one[x + 2, pair + 1] = jnp.where(lower, one, two)
            level_one[x + half_x + 2, pair + 1] = jnp.where(lower, two, one)
    children = jnp.concatenate(
        [
            jnp.concatenate([level_one[2 * x + 2, y + 1], level_one[2 * x + 3, y + 1]], 1)
            for x in range(half_x)
            for y in range(pairs_y)
        ],
        0,
    )
    below = half_x * pairs_y * 8
    low_lanes = lanes((4, 128)) < 64
    sums[0:below, :] = dot_three(children, small[0:256], small[256:512])
    for x in range(half_x):
        for y in range(pairs_y):
            row = (x * pairs_y + y) * 8
            even = sums[pl.ds(row, 4, stride=2), :]
            odd = sums[pl.ds(row + 1, 4, stride=2), :]
            level_two[x + 2, y + 2, 0:4] = jnp.where(low_lanes, even + lane_flip(odd), 0.0)

    def second_group(group_x, group_y):
        return jnp.concatenate(
            [
                level_two[2 * group_x + h + 2, 2 * group_y + 2]
                + lane_flip(level_two[2 * group_x + h + 2, 2 * group_y + 3])
                for h in range(2)
            ],
            1,
        )

    quarter_x, quarter_y = index_x // 4, index_y // 4
    tops = [(x, y) for x in range(count_x // 4) for y in range(count_y // 4)]
    stacked = jnp.concatenate([second_group(x, y) for x, y in tops], 0)
    if stacked.shape[0] % 16 != 0:
        stacked = jnp.concatenate([stacked, jnp.zeros((8, 256), F32)], 0)
    sums[0 : stacked.shape[0], :] = dot_three(stacked, small[0:256], small[256:512])
    top_far = jnp.zeros((16, 128), F32)
    for position, (x, y) in enumerate(tops):
        even = sums[pl.ds(8 * position, 2, stride=2), :]
        odd = sums[pl.ds(8 * position + 1, 2, stride=2), :]
        third = jnp.where(lanes((2, 128)) < 64, even + lane_flip(odd), 0.0)
        third = third[0:1] + lane_flip(third)[1:2]
        step_x, step_y = x - quarter_x + count_x // 4 - 1, y - quarter_y + count_y // 4 - 1
        row = 1536 + 256 * (step_x * (count_y // 4 * 2 - 1) + step_y)
        table = [small[pl.ds(pl.multiple_of(row + 128 * k, 128), 128), :] for k in range(2)]
        top_far = top_far + dot_three(jnp.broadcast_to(third, (16, 128)), table[0], table[1])

    edge = jnp.zeros((8, 256), F32)
    groups = {}
    for gx in (-1, 0, 1):
        for gy in (-1, 0, 1):
            steps = [2 * (index_x // 2 + gx) + h + 2 for h in range(2)]
            first_level = [level_one[step, index_y // 2 + gy + 1] for step in steps]
            second_level = second_group(quarter_x + gx, quarter_y + gy)
            blocks = [edge, jnp.concatenate(first_level, 1), edge, second_level, edge, edge]
            groups[gx, gy] = jnp.concatenate(blocks, 0)
    store_reflected(groups, flips, flipped)
    far = far_sums((-1, 0, 1), ((8, 8), (24, 8)), flipped, flips, tiles)

    def select(block, hx, hy):
        tile = jnp.where(hx == 1, block[:, 128:256], block[:, 0:128])
        return jnp.where(hy == 1, lane_flip(tile), tile)

    def refine(parent):
        keep = lanes((16, 128)) < 64
        parent = jnp.where(keep, parent, 0.0)
        high = parent.astype(BF16).astype(F32)
        low = parent - high
        left = jnp.concatenate([high + lane_flip(low), high], 1).astype(BF16)
        down = jnp.concatenate([small[512 + 256 * k : 768 + 256 * k, :] for k in range(4)], 1)
        spread = dot(left, down)
        for half in range(2):
            for h in range(2):
                span = slice(256 * half + 128 * h, 256 * half + 128 * h + 128)
                local[h, pl.ds(half, 16, stride=2), :] = spread[:, span]
        return jnp.concatenate([local[0], local[1]], 1)

    top_local = jnp.where(
        sublanes((16, 128)) == 0, top_far, jnp.where(sublanes((16, 128)) == 1, lane_flip(top_far), 0.0)
    )
    children_far = refine(top_local)
    half_index_x, half_index_y = index_x // 2, index_y // 2
    second = select(children_far[0:8], lax.rem(half_index_x, 2), lax.rem(half_index_y, 2))
    second = second + 0.25 * select(far[8:16], lax.rem(half_index_x, 2), lax.rem(half_index_y, 2))
    zeros = jnp.zeros((8, 128), F32)
    children_far = refine(jnp.concatenate([second, zeros], 0))
    first = select(children_far[0:8], lax.rem(index_x, 2), lax.rem(index_y, 2))
    first = first + 0.5 * select(far[0:8], lax.rem(index_x, 2), lax.rem(index_y, 2))
    out[...] = refine(jnp.concatenate([first, zeros], 0))[0:16]


def upper_call(count_x, count_y, operands):
    half_x, half_y = count_x // 2, count_y // 2
    scratch = [
        pltpu.VMEM((count_x + 4, half_y + 2, 8, 128), F32),
        pltpu.VMEM((half_x + 4, half_y + 4, 8, 128), F32),
        pltpu.VMEM((3, 3, 2, 2, 2, 48, 128), F32),
        pltpu.VMEM((max(16, half_x * half_y * 8), 128), F32),
        pltpu.VMEM((2, 32, 128), F32),
    ]
    return pl.pallas_call(
        lambda *refs: upper_kernel(count_x, count_y, refs),
        out_shape=jax.ShapeDtypeStruct((LZ, 256), F32),
        in_specs=[VMEM] * len(operands),
        out_specs=VMEM,
        scratch_shapes=scratch,
        compiler_params=pltpu.CompilerParams(vmem_limit_bytes=8 * MIB),
        cost_estimate=pl.CostEstimate(flops=900_000_000, bytes_accessed=600_000, transcendentals=0),
        name="upper",
    )(*operands)


def last_kernel(basis, near_rows, local, far_own, far_beside, out):
    leaf = local[...] + far_own[...] + far_beside[...]

    one, two = halves(leaf)
    turned = jnp.concatenate([one.astype(F32), two.astype(F32)], 0).T.astype(BF16)
    table = leaf_segments(2 * LZ)
    for x in range(CX):
        for y in range(CY):
            column = x * CY + y
            spread = dot(turned[64 * column : 64 * column + 64], table)
            for j in range(ROWS):
                span = slice(128 * j, 128 * j + 128)
                total = None
                for k in range(8):
                    term = basis[column, j, 8 * k : 8 * k + 8, :] * spread[8 * k : 8 * k + 8, span]
                    total = term if total is None else total + term
                value = jnp.sum(total, 0, keepdims=True) + near_rows[column, j : j + 1, :]
                out[x, y : y + 1, span] = value


def last_call(operands):
    return pl.pallas_call(
        last_kernel,
        out_shape=jax.ShapeDtypeStruct((CX, CY, LZ * 64), F32),
        in_specs=[VMEM] * len(operands),
        out_specs=VMEM,
        compiler_params=pltpu.CompilerParams(vmem_limit_bytes=8 * MIB),
        name="last",
    )(*operands)


def in_hbm(value):
    return pltpu.with_memory_space_constraint(value, pltpu.HBM)


def swap_bit(value, axis, bit):
    return lax.ppermute(value, axis, [(i, i ^ (1 << bit)) for i in range(lax.axis_size(axis))])


def relay_ring(value, axis):
    count = lax.axis_size(axis)
    steps = {i: i + 2 if i % 2 == 0 else i - 2 for i in range(count)}
    steps[count - 2], steps[1] = count - 1, 0
    return lax.ppermute(value, axis, list(steps.items()))


def solution(mesh):
    count_x, count_y = mesh.shape["gx"], mesh.shape["gy"]
    levels_x, levels_y = count_x.bit_length() - 1, count_y.bit_length() - 1
    tiles = translation_tiles()
    small = small_tables(count_x // 4, count_y // 4)
    tables = small, reflection_tables(), tiles[:TILES_FIRST], tiles[TILES_FIRST:]

    def body(offsets, charges):
        small, flips, *tiles = [in_hbm(jnp.asarray(table)) for table in tables]
        block = moments_call(in_hbm(offsets), in_hbm(charges), small)
        other = swap_bit(block, "gy", 0)
        exchanged = []

        def exchange_y(after):
            pair = block, other
            for level in range(1, levels_y):
                last = level == levels_y - 1
                rows = (ONE_ROWS << (level - 1)) + EDGE_ROWS * (1 if last else 2)
                kernel = functools.partial(group_kernel, level, last)
                sent = pack_call(kernel, rows, (*pair, after), "group")
                pair = sent, swap_bit(sent, "gy", level)
                exchanged.extend(pair)
            return exchanged[0]

        near, targets, small, first_tiles = own_call(block, exchange_y, small, tiles[0])
        row, far = row_call(levels_y, (block, other, *exchanged, near))
        partner = swap_bit(row, "gx", 0)
        partner_far = swap_bit(far, "gx", 0)
        near, flips, other_tiles = beside_y_call(row, far, targets, near, (flips, tiles[1]))
        leaves, basis = own_leaves_call(row, flips, block)
        far_own = far_own_call(leaves, flips, first_tiles)
        rows = ONE_ROWS << (levels_y - 1)
        ones = merge_call(0, row, partner, ROW_ROWS, rows, SENT_ROWS, far_own)
        other_ones = swap_bit(ones, "gx", 1)
        beyond = relay_ring(relay_call(partner, partner_far, ones), "gx")
        near = near_call(beside_x_kernel, (partner, targets, near, ones), 8, 10, 1_200_000, "near_x")
        for bit in range(1, levels_x - 1):
            ones = merge_call(bit, ones, other_ones, 0, rows << bit, 0, near)
            other_ones = swap_bit(ones, "gx", bit + 1)
        far_tables = flips, first_tiles, other_tiles
        near, far_beside = beyond_call((near, partner, beyond, targets, *far_tables, ones))
        local = upper_call(count_x, count_y, (ones, other_ones, small, *far_tables, near))
        return last_call((basis, near, local, far_own, far_beside))

    in_specs = (P(None, "gx", "gy", None), P("gx", "gy", None))
    out_specs = P("gx", "gy", None)
    return jax.shard_map(body, mesh=mesh, in_specs=in_specs, out_specs=out_specs, check_vma=False)
```

```python
import functools
import itertools

import jax
import jax.numpy as jnp
import ml_dtypes
import numpy as np
from jax import lax
from jax.experimental import pallas as pl
from jax.experimental.pallas import tpu as pltpu
from jax.sharding import PartitionSpec as P

F32 = jnp.float32
BF16 = jnp.bfloat16
MIB = 1 << 20

CX = 2
CY = 2
LZ = 16
ROWS = 8
FEATURES = 32
VMEM = pl.BlockSpec(memory_space=pltpu.VMEM)
HBM = pl.BlockSpec(memory_space=pltpu.HBM)


def nodes_1d():
    return np.cos((2.0 * np.arange(4) + 1.0) * np.pi / 8.0)


def cheb_terms(value):
    return value, 2.0 * value * value - 1.0, 4.0 * value**3 - 3.0 * value


def node_weights():
    return [[0.5 * term for term in cheb_terms(point)] for point in nodes_1d()]


def node_grid():
    points = nodes_1d()
    counter = np.arange(64)
    return np.stack([points[counter // 16], points[counter // 4 % 4], points[counter % 4]], -1)


def split_two(table):
    high = table.astype(np.float32).astype(ml_dtypes.bfloat16)
    low = (table - high.astype(np.float64)).astype(np.float32).astype(ml_dtypes.bfloat16)
    return high, low


def upward_tensor():
    points = nodes_1d()
    shifted = (points[None, :] + 2.0 * np.arange(2)[:, None] - 1.0) / 2.0
    factor = 0.25 + 0.0 * shifted[..., None]
    for of_value, of_node in zip(cheb_terms(shifted), cheb_terms(points)):
        factor = factor + 0.5 * of_value[..., None] * of_node
    full = np.einsum("xia,yjb,zkc->xyzijkabc", factor, factor, factor)
    return full.reshape(2, 2, 2, 64, 64)


def inverse_distance(offset):
    grid = node_grid()
    spread = (grid[None, :, :] - grid[:, None, :]) / 2.0 - np.asarray(offset, np.float64)
    return 1.0 / np.sqrt(np.sum(spread * spread, -1))


def adjacent(offset):
    return max(abs(int(step)) for step in offset) <= 1


def canonical_tiles():
    return [
        (cx, cy, cz)
        for cx in range(2)
        for cy in range(2)
        for cz in range(4)
        if not (cx == 0 and cy == 0 and cz <= 1)
    ]


TILES_FIRST = 10


def translation_tiles():
    tiles = []
    for cx, cy, cz in canonical_tiles():
        tile = np.zeros((4, 64, 4, 64))
        for source in range(4):
            for target in range(4):
                offset = (
                    2 * cx + source // 2 - target // 2,
                    2 * cy + source % 2 - target % 2,
                    cz,
                )
                if not adjacent(offset):
                    tile[source, :, target, :] = inverse_distance(offset)
        tiles.append(tile.reshape(256, 256))
    return np.stack(split_two(np.stack(tiles)), 1)


def reflection_matrix(flip_x, flip_y, flip_z):
    index = np.arange(256)
    hx, hy, a, b, c = index // 128, index // 64 % 2, index // 16 % 4, index // 4 % 4, index % 4
    if flip_x:
        hx, a = 1 - hx, 3 - a
    if flip_y:
        hy, b = 1 - hy, 3 - b
    if flip_z:
        c = 3 - c
    matrix = np.zeros((256, 256), np.float32)
    matrix[hx * 128 + hy * 64 + a * 16 + b * 4 + c, index] = 1.0
    return matrix


def reflection_tables():
    pairs = [
        np.concatenate([reflection_matrix(fx, fy, 0), reflection_matrix(fx, fy, 1)], 1)
        for fx in range(2)
        for fy in range(2)
    ]
    return np.stack(pairs).astype(ml_dtypes.bfloat16)


def up_tables():
    upward = upward_tensor()
    table = upward.transpose(0, 1, 3, 2, 4).reshape(256, 128)
    return np.stack(split_two(table))


def down_table():
    upward = upward_tensor()
    table = upward.transpose(4, 2, 0, 1, 3).reshape(64, 512)
    high, low = split_two(table)
    return np.concatenate([high, high, low, np.zeros_like(low)], 0)


def top_tables(boxes_x, boxes_y):
    offsets = range(-(boxes_x - 1), boxes_x), range(-(boxes_y - 1), boxes_y)
    table = np.zeros((len(offsets[0]), len(offsets[1]), 2, 64, 2, 64))
    for (ix, dx), (iy, dy) in itertools.product(enumerate(offsets[0]), enumerate(offsets[1])):
        for source, target in itertools.product(range(2), range(2)):
            offset = (dx, dy, source - target)
            if not adjacent(offset):
                table[ix, iy, source, :, target, :] = 0.125 * inverse_distance(offset)
    return np.stack(split_two(table.reshape(len(offsets[0]), len(offsets[1]), 128, 128)), 2)


def small_tables(boxes_x, boxes_y):
    down = down_table().reshape(256, 4, 128).transpose(1, 0, 2)
    parts = [up_tables(), down, top_tables(boxes_x, boxes_y)]
    return np.concatenate([part.reshape(-1, 128) for part in parts], 0)


def halves(value):
    high = value.astype(BF16)
    return high, (value - high.astype(F32)).astype(BF16)


def dot(left, right):
    return jnp.dot(left, right, preferred_element_type=F32)


def dot_three(value, high_table, low_table):
    rows = value.shape[0]
    high, low = halves(value)
    both = dot(jnp.concatenate([high, low], 0), high_table)
    return both[:rows] + both[rows:] + dot(high, low_table)


def lanes(shape):
    return lax.broadcasted_iota(jnp.int32, shape, len(shape) - 1)


def sublanes(shape):
    return lax.broadcasted_iota(jnp.int32, shape, len(shape) - 2)


def leaf_segments(leaves):
    shape = (leaves, LZ * 64)
    return jnp.where(lanes(shape) // 64 == lax.rem(sublanes(shape), LZ), 1.0, 0.0).astype(BF16)


def lane_flip(value):
    return pltpu.roll(value, 64, 1)


def weight_rows(pattern):
    weights = node_weights()
    index = sublanes((8, 128))
    rows = []
    for term in range(3):
        row = jnp.full((8, 128), weights[pattern(0)][term], F32)
        for sub in range(1, 8):
            row = jnp.where(index == sub, weights[pattern(sub)][term], row)
        rows.append(row)
    return rows


def basis_rows():
    return (
        weight_rows(lambda sub: sub // 4),
        weight_rows(lambda sub: 2 + sub // 4),
        weight_rows(lambda sub: sub % 4),
    )


def basis_tile(row_x, row_y, row_z, scale, tables):
    y_low, y_high, z_all = tables
    wide = [jnp.broadcast_to(2.0 * row - 1.0, (8, 128)) for row in (row_x, row_y, row_z)]
    terms = [cheb_terms(value) for value in wide]

    def mix(weights, term):
        return 0.25 + (weights[0] * term[0] + weights[1] * term[1] + weights[2] * term[2])

    along_z = mix(z_all, terms[2])
    pair = mix(y_low, terms[1]) * along_z, mix(y_high, terms[1]) * along_z
    tiles = []
    for weights in node_weights():
        along_x = mix(weights, terms[0])
        if scale is not None:
            along_x = along_x * scale
        tiles += [along_x * pair[0], along_x * pair[1]]
    return tiles


def three_pieces(value):
    first = value.astype(BF16).astype(F32)
    rest = value - first
    second = rest.astype(BF16).astype(F32)
    return first, second, rest - second


PIECES = 12


def feature_pieces(coords, scale):
    total = coords[0] * coords[0] + coords[1] * coords[1] + coords[2] * coords[2]
    return [piece for value in [scale * coord for coord in coords] + [total] for piece in three_pieces(value)]


def pick(row, pieces, choice):
    value = jnp.broadcast_to(pieces[choice[0]], (8, 128))
    for piece in sorted(set(choice) - {choice[0]}):
        mask = None
        for place, chosen in enumerate(choice):
            if chosen == piece:
                mask = row == place if mask is None else mask | (row == place)
        value = jnp.where(mask, jnp.broadcast_to(pieces[piece], (8, 128)), value)
    return value


def feature_block(read, choice, length_choice):
    row = sublanes((8, 128))
    zero, one = jnp.zeros((1, 128), F32), jnp.ones((1, 128), F32)
    blocks = [
        pick(row, [read(3 * c), read(3 * c + 1), read(3 * c + 2), zero], choice) for c in range(3)
    ]
    blocks.append(pick(row, [read(9), read(10), read(11), one, zero], length_choice))
    return jnp.concatenate(blocks, 0)


SOURCE_CHOICE = (0, 1, 0, 1, 2, 0, 0, 0), (3, 3, 3, 0, 1, 2, 3, 3)
TARGET_CHOICE = (0, 0, 1, 1, 0, 2, 3, 3), (0, 1, 2, 3, 3, 3, 4, 4)


def column(raw, x, y):
    return raw(0) + (x - 2.0), raw(1) + (y - 2.0), raw(2), raw(3)


class Near:
    def __init__(self, wide_ref, charge_ref, target_ref):
        self.wide_ref = wide_ref
        self.charge_ref = charge_ref
        self.target_ref = target_ref
        self.groups = 0
        self.charges = 0
        self.upper = lanes((ROWS, 128)) >= 64
        self.row = sublanes((ROWS, 128))

    def in_pair(self, along_z):
        return along_z + jnp.where(self.upper, 0.0, -1.0)

    def targets(self, columns):
        for ab, (x, y, z, _) in enumerate(columns):
            pieces = feature_pieces((x, y, self.in_pair(z)), -2.0)
            for j in range(ROWS):
                block = feature_block(lambda k: pieces[k][j : j + 1], *TARGET_CHOICE)
                self.target_ref[ab, j] = block.T.astype(BF16)

    def add_group(self, coords):
        for k, piece in enumerate(feature_pieces(coords, 1.0)):
            self.wide_ref[self.groups, k] = piece
        self.groups += 1
        return self.groups - 1

    def add_charge(self, charge):
        self.charge_ref[self.charges] = charge
        self.charges += 1
        return self.charges - 1

    def main(self, source):
        x, y, z, charge = source
        return self.add_group((x, y, self.in_pair(z))), self.add_charge(charge)

    def outer(self, first, second, side, keep=False):
        def merge(one, two):
            if side == 0:
                value = jnp.where(self.upper, two, lane_flip(one))
                return pltpu.roll(value, 1, 0)
            value = jnp.where(self.upper, lane_flip(two), one)
            return pltpu.roll(value, ROWS - 1, 0)

        x, y, z, charge = [merge(one, two) for one, two in zip(first, second)]
        charge = jnp.where(self.row == (0 if side == 0 else ROWS - 1), 0.0, charge)
        group = self.add_group((x, y, z + (-2.0 if side == 0 else 1.0)))
        if not keep:
            return group, self.add_charge(charge)
        low = self.add_charge(jnp.where(self.upper, 0.0, charge))
        high = self.add_charge(jnp.where(self.upper, charge, 0.0))
        return (group, low), (group, high)

    def run(self, plan, emit):
        eye = sublanes((128, 128)) == lanes((128, 128))

        def source(group, j, built):
            if group not in built:
                read = lambda k: self.wide_ref[group, k, pl.ds(j, 1), :]
                built[group] = feature_block(read, *SOURCE_CHOICE).astype(BF16)
            return built[group]

        def pairs(targets, tiles, j, own, total, built):
            block = jnp.concatenate([source(group, j, built) for group, _ in tiles], 1)
            squared = dot(targets, block)
            for position, (group, charge) in enumerate(tiles):
                inverse = lax.rsqrt(squared[:, 128 * position : 128 * position + 128])
                if group == own:
                    inverse = jnp.where(eye, 0.0, inverse)
                total = total + inverse * self.charge_ref[charge, pl.ds(j, 1), :]
            return total

        def step(j, carry):
            built = {}
            for ab, mains, below, above, own in plan:
                targets = self.target_ref[ab, j]
                total = pairs(targets, mains, j, own, jnp.zeros((128, 128), F32), built)
                lower = pairs(targets[:64], below, j, None, total[:64], built)
                higher = pairs(targets[64:], above, j, None, total[64:], built)
                total = jnp.concatenate([lower, higher], 0)
                emit(ab, j, jnp.sum(total.T, 0, keepdims=True))
            return carry

        lax.fori_loop(0, ROWS, step, 0, unroll=True)


def plan_own(near, columns):
    mains = [near.main(source) for source in columns]
    outer = [
        [near.outer(columns[2 * x], columns[2 * x + 1], side) for x in range(2)]
        for side in range(2)
    ]
    return [(ab, mains, outer[0], outer[1], mains[ab][0]) for ab in range(4)]


def plan_beside_y(near, columns):
    plan = []
    for b in range(2):
        mains = [near.main(source) for source in columns[b]]
        outer = [[near.outer(*columns[b], side)] for side in range(2)]
        plan += [(2 * a + b, mains, outer[0], outer[1], None) for a in range(2)]
    return plan


def plan_beside_x(near, columns, side_x):
    mains = [near.main(source) for source in columns]
    middle = [near.outer(columns[1], columns[2], side) for side in range(2)]
    ends = [near.outer(columns[0], columns[3], side, keep=True) for side in range(2)]
    return [
        (2 * side_x + b, mains[b : b + 3], [middle[0], ends[0][b]], [middle[1], ends[1][b]], None)
        for b in range(2)
    ]


def near_scratch(groups, charges):
    return [
        pltpu.VMEM((groups, PIECES, ROWS, 128), F32),
        pltpu.VMEM((charges, ROWS, 128), F32),
    ]


NEAR_SHAPE = (4, ROWS, 128)


def near_cost(pairs):
    return pl.CostEstimate(flops=40 * pairs, bytes_accessed=600_000, transcendentals=pairs)


ONE_ROWS = 8
LEAF_ROWS = 32
PART_ROWS = 4 * CX * CY * ROWS
OWN_ROWS = ONE_ROWS + LEAF_ROWS + PART_ROWS


def part_row(c, x, y):
    return ONE_ROWS + LEAF_ROWS + ((c * CX + x) * CY + y) * ROWS


def moments_kernel(
    offsets_hbm, charges_hbm, small_hbm, block, offsets, charges, up, basis, sums, semaphores
):
    index_y = lax.axis_index("gy")
    copies = [
        pltpu.make_async_copy(offsets_hbm, offsets, semaphores.at[0]),
        pltpu.make_async_copy(charges_hbm, charges, semaphores.at[1]),
        pltpu.make_async_copy(small_hbm.at[0:512], up, semaphores.at[2]),
    ]
    for copy in copies:
        copy.start()
    tables = basis_rows()
    segments = leaf_segments(LZ)
    copies[0].wait()
    copies[1].wait()
    for x in range(CX):
        for y in range(CY):
            for j in range(ROWS):
                span = slice(128 * j, 128 * j + 128)
                rows = [offsets[c, x, y : y + 1, span] for c in range(3)]
                charge = charges[x, y : y + 1, span]
                for c, row in enumerate(rows + [charge]):
                    place = part_row(c, x, y) + j
                    block[place : place + 1, :] = row
                tiles = basis_tile(*rows, charge, tables)
                for k in range(4):
                    pair = jnp.concatenate(tiles[2 * k : 2 * k + 2], 0)
                    high, low = halves(pair)
                    first = (x * CY + y) * 64 + 16 * k
                    basis[0, first : first + 16, span] = high
                    basis[1, first : first + 16, span] = low
    contract = (((1,), (1,)), ((), ()))
    leaf = lax.dot_general(segments, basis[0], contract, preferred_element_type=F32)
    leaf = leaf + lax.dot_general(segments, basis[1], contract, preferred_element_type=F32)
    copies[2].wait()
    sums[...] = dot_three(leaf, up[0:256], up[256:512])
    first = sums[pl.ds(0, 8, stride=2), :] + lane_flip(sums[pl.ds(1, 8, stride=2), :])
    first = jnp.where(lanes((8, 128)) < 64, first, 0.0)
    first = jnp.where(lax.rem(index_y, 2) == 1, lane_flip(first), first)
    block[0:8, :] = first
    block[8:24, :] = leaf[:, :128]
    block[24:40, :] = leaf[:, 128:]


def moments_call(offsets, charges, small):
    return pl.pallas_call(
        moments_kernel,
        out_shape=jax.ShapeDtypeStruct((OWN_ROWS, 128), F32),
        in_specs=[HBM] * 3,
        out_specs=VMEM,
        scratch_shapes=[
            pltpu.VMEM(offsets.shape, F32),
            pltpu.VMEM(charges.shape, F32),
            pltpu.VMEM((512, 128), BF16),
            pltpu.VMEM((2, 256, 1024), BF16),
            pltpu.VMEM((16, 128), F32),
            pltpu.SemaphoreType.DMA((3,)),
        ],
        compiler_params=pltpu.CompilerParams(vmem_limit_bytes=8 * MIB),
        cost_estimate=pl.CostEstimate(flops=10_000_000, bytes_accessed=300_000, transcendentals=0),
        name="moments",
    )(offsets, charges, small)


EDGE_ROWS = LEAF_ROWS + 4 * CX * ROWS


def bits_below(index, bit):
    return lax.rem(index, 1 << bit)


def bit_of(index, bit):
    return lax.rem(index // (1 << bit), 2)


def in_order(is_first, own, other):
    return jnp.concatenate([jnp.where(is_first, own, other), jnp.where(is_first, other, own)], 0)


def edge_block(block, y):
    rows = [block[ONE_ROWS : ONE_ROWS + LEAF_ROWS, :]]
    for c in range(4):
        for x in range(CX):
            rows.append(block[part_row(c, x, y) : part_row(c, x, y) + ROWS, :])
    return jnp.concatenate(rows, 0)


def group_kernel(level, last_level, own_ref, other_ref, after, out):
    index = lax.axis_index("gy")
    ones = ONE_ROWS << (level - 1)
    is_first = bit_of(index, level - 1) == 0
    if level == 1:
        out[0:ones, :] = own_ref[0:ones, :] + other_ref[0:ones, :]
        first = jnp.where(is_first, edge_block(own_ref, 0), edge_block(other_ref, 0))
        last = jnp.where(is_first, edge_block(other_ref, 1), edge_block(own_ref, 1))
    else:
        half = ones // 2
        out[0:ones, :] = in_order(is_first, own_ref[0:half, :], other_ref[0:half, :])
        own_far = own_ref[half + EDGE_ROWS : half + 2 * EDGE_ROWS, :]
        other_far = other_ref[half + EDGE_ROWS : half + 2 * EDGE_ROWS, :]
        first = jnp.where(is_first, own_far, other_far)
        last = jnp.where(is_first, other_far, own_far)
    lower = bit_of(index, level) == 0
    out[ones : ones + EDGE_ROWS, :] = jnp.where(lower, last, first)
    if not last_level:
        out[ones + EDGE_ROWS : ones + 2 * EDGE_ROWS, :] = jnp.where(lower, first, last)


def pack_call(kernel, rows, operands, name):
    return pl.pallas_call(
        kernel,
        out_shape=jax.ShapeDtypeStruct((rows, 128), F32),
        in_specs=[VMEM] * len(operands),
        out_specs=VMEM,
        compiler_params=pltpu.CompilerParams(vmem_limit_bytes=8 * MIB),
        cost_estimate=pl.CostEstimate(flops=100_000, bytes_accessed=300_000, transcendentals=0),
        name=name,
    )(*operands)


ROW_LEAF = 3 * LEAF_ROWS
ROW_PART = 4 * 4 * ROWS
ROW_ROWS = ROW_LEAF + ROW_PART


def row_part(c, y):
    return ROW_LEAF + (c * 4 + y) * ROWS


def row_kernel(levels, block, other, *refs):
    exchanged, (out, far_out) = refs[: 2 * (levels - 1)], refs[-2:]
    index = lax.axis_index("gy")
    even = lax.rem(lax.axis_index("gx"), 2) == 0
    is_first = bit_of(index, 0) == 0
    low = jnp.where(is_first, 0.0, edge_block(other, 1))
    high = jnp.where(is_first, edge_block(other, 0), 0.0)
    ones = ONE_ROWS
    for level in range(1, levels):
        own, received = exchanged[2 * level - 2 : 2 * level]
        ones = ONE_ROWS << (level - 1)
        facing = received[ones : ones + EDGE_ROWS, :]
        below = bits_below(index, level)
        upper = bit_of(index, level) == 1
        low = jnp.where(upper & (below == 0), facing, low)
        high = jnp.where(~upper & (below == (1 << level) - 1), facing, high)
        if level == levels - 1:
            out[ROW_ROWS:, :] = in_order(~upper, own[0:ones, :], received[0:ones, :])
    leaf = block[ONE_ROWS : ONE_ROWS + LEAF_ROWS, :]
    for piece, rows in enumerate((low[0:LEAF_ROWS], leaf, high[0:LEAF_ROWS])):
        out[LEAF_ROWS * piece : LEAF_ROWS * (piece + 1), :] = rows
    for c in range(4):
        columns = []
        for x in range(CX):
            row = LEAF_ROWS + (c * CX + x) * ROWS
            own = [block[part_row(c, x, y) : part_row(c, x, y) + ROWS, :] for y in range(CY)]
            columns.append([low[row : row + ROWS], *own, high[row : row + ROWS]])
        for y in range(4):
            facing, far = row_part(c, y), row_part(c, y) - ROW_LEAF
            out[facing : facing + ROWS, :] = jnp.where(even, columns[1][y], columns[0][y])
            far_out[far : far + ROWS, :] = jnp.where(even, columns[0][y], columns[1][y])


def row_call(levels, operands):
    return pl.pallas_call(
        lambda *refs: row_kernel(levels, *refs[: 2 * levels], *refs[-2:]),
        out_shape=[
            jax.ShapeDtypeStruct((rows, 128), F32)
            for rows in (ROW_ROWS + (ONE_ROWS << (levels - 1)), ROW_PART)
        ],
        in_specs=[VMEM] * len(operands),
        out_specs=[VMEM] * 2,
        compiler_params=pltpu.CompilerParams(vmem_limit_bytes=8 * MIB),
        cost_estimate=pl.CostEstimate(flops=100_000, bytes_accessed=600_000, transcendentals=0),
        name="row",
    )(*operands)


SENT_ROWS = 192


def merge_call(bit, own, other, first, rows, least, after):
    total = max(2 * rows, least)

    def kernel(own_ref, other_ref, after_ref, out):
        is_first = bit_of(lax.axis_index("gx"), bit) == 0
        span = slice(first, first + rows)
        out[0 : 2 * rows, :] = in_order(is_first, own_ref[span, :], other_ref[span, :])
        if total > 2 * rows:
            out[2 * rows :, :] = jnp.zeros((total - 2 * rows, 128), F32)

    return pack_call(kernel, total, (own, other, after), "merge")


def relay_call(received, received_far, after):
    def kernel(received_ref, far_ref, after_ref, out):
        out[0:ROW_LEAF, :] = received_ref[0:ROW_LEAF, :]
        out[ROW_LEAF:ROW_ROWS, :] = far_ref[...]

    return pack_call(kernel, ROW_ROWS, (received, received_far, after), "relay")


def own_kernel(block, targets, features, charges):
    near = Near(features, charges, targets)

    def raw(x, y):
        return lambda c: block[part_row(c, x, y) : part_row(c, x, y) + ROWS, :]

    columns = [column(raw(ab // 2, ab % 2), ab // 2 + 1, ab % 2 + 1) for ab in range(4)]
    near.targets(columns)
    return near, plan_own(near, columns)


def own_call(block, after, small, tiles):
    plans = []

    def prepare(block_ref, small, targets, features, charges, small_out, semaphore):
        copy = pltpu.make_async_copy(small, small_out, semaphore)
        copy.start()
        plans.append(own_kernel(block_ref, targets, features, charges)[1])
        copy.wait()

    def run(targets, features, charges, after_ref, tiles, out, tiles_out, semaphore):
        copy = pltpu.make_async_copy(tiles, tiles_out, semaphore)
        copy.start()

        def emit(ab, j, row):
            out[ab, pl.ds(j, 1), :] = row

        Near(features, charges, targets).run(plans[0], emit)
        copy.wait()

    prepared = pl.pallas_call(
        prepare,
        out_shape=(
            jax.ShapeDtypeStruct((4, ROWS, 128, FEATURES), BF16),
            jax.ShapeDtypeStruct((8, PIECES, ROWS, 128), F32),
            jax.ShapeDtypeStruct((8, ROWS, 128), F32),
            jax.ShapeDtypeStruct(small.shape, BF16),
        ),
        in_specs=[VMEM, HBM],
        out_specs=(VMEM,) * 4,
        scratch_shapes=[pltpu.SemaphoreType.DMA],
        compiler_params=pltpu.CompilerParams(vmem_limit_bytes=8 * MIB),
        cost_estimate=near_cost(500_000),
        name="features",
    )(block, small)
    near, tiles_near = pl.pallas_call(
        run,
        out_shape=(
            jax.ShapeDtypeStruct(NEAR_SHAPE, F32),
            jax.ShapeDtypeStruct(tiles.shape, BF16),
        ),
        in_specs=[VMEM] * 4 + [HBM],
        out_specs=(VMEM,) * 2,
        scratch_shapes=[pltpu.SemaphoreType.DMA],
        compiler_params=pltpu.CompilerParams(vmem_limit_bytes=8 * MIB),
        cost_estimate=near_cost(4_500_000),
        name="near_own",
    )(*prepared[:3], after(prepared[2]), tiles)
    return near, prepared[0], prepared[3], tiles_near


def beside_y_kernel(
    row_ref, far_ref, targets, before, flips, tiles, out, flips_out, tiles_out, wide_ref, charge_ref, semaphores
):
    copies = [
        pltpu.make_async_copy(flips, flips_out, semaphores.at[0]),
        pltpu.make_async_copy(tiles, tiles_out, semaphores.at[1]),
    ]
    for copy in copies:
        copy.start()
    even = lax.rem(lax.axis_index("gx"), 2) == 0
    near = Near(wide_ref, charge_ref, targets)

    def raw(x, y):
        def read(c):
            facing, far = row_part(c, y), row_part(c, y) - ROW_LEAF
            own = row_ref[facing : facing + ROWS, :], far_ref[far : far + ROWS, :]
            return jnp.where(even == (x == 1), *own)

        return read

    columns = [[column(raw(x, y), x + 1, y) for x in range(2)] for y in (0, 3)]
    plan = plan_beside_y(near, columns)
    out[...] = before[...]

    def emit(ab, j, row):
        out[ab, pl.ds(j, 1), :] = out[ab, pl.ds(j, 1), :] + row

    near.run(plan, emit)
    for copy in copies:
        copy.wait()


def beside_y_call(row, far, targets, before, constants):
    near_shape = jax.ShapeDtypeStruct(NEAR_SHAPE, F32)
    tables = [jax.ShapeDtypeStruct(constant.shape, BF16) for constant in constants]
    return pl.pallas_call(
        beside_y_kernel,
        out_shape=(near_shape, *tables),
        in_specs=[VMEM] * 4 + [HBM] * 2,
        out_specs=(VMEM,) * 3,
        scratch_shapes=near_scratch(8, 8) + [pltpu.SemaphoreType.DMA((2,))],
        compiler_params=pltpu.CompilerParams(vmem_limit_bytes=8 * MIB),
        cost_estimate=near_cost(2_200_000),
        name="near_y",
    )(row, far, targets, before, *constants)


def beside_x(parity, received, targets, out, wide_ref, charge_ref):
    index, count = lax.axis_index("gx"), lax.axis_size("gx")
    even = lax.rem(index, 2) == 0
    side = jnp.where(even == (parity == 0), 1, 0)
    alone = (index == 0) | (index == count - 1)
    near = Near(wide_ref, charge_ref, targets)

    def raw(y):
        def coordinate(c):
            value = received[row_part(c, y) : row_part(c, y) + ROWS, :]
            return jnp.where(alone, 0.0, value) if c == 3 and parity == 1 else value

        return coordinate

    columns = [column(raw(y), 3.0 * side.astype(F32), y) for y in range(4)]
    plan = plan_beside_x(near, columns, side)

    def emit(ab, j, row):
        out[ab, pl.ds(j, 1), :] = out[ab, pl.ds(j, 1), :] + row

    near.run(plan, emit)


def beside_x_kernel(received, targets, before, after, out, wide_ref, charge_ref):
    out[...] = before[...]
    beside_x(0, received, targets, out, wide_ref, charge_ref)


def near_call(kernel, operands, groups, charges, pairs, name):
    return pl.pallas_call(
        kernel,
        out_shape=jax.ShapeDtypeStruct(NEAR_SHAPE, F32),
        in_specs=[VMEM] * len(operands),
        out_specs=VMEM,
        scratch_shapes=near_scratch(groups, charges),
        compiler_params=pltpu.CompilerParams(vmem_limit_bytes=12 * MIB),
        cost_estimate=near_cost(pairs),
        name=name,
    )(*operands)


def store_reflected(moments, flips, flipped):
    def store(group, z, part, value):
        for half in range(2):
            place = flipped.at[group[0] + 1, group[1] + 1, z, part, half]
            place[...] = value[:, 128 * half : 128 * half + 128]

    parts = {group: halves(value) for group, value in moments.items()}
    for fx in range(2):
        for fy in range(2):
            groups = [group for group in moments if (group[0] < 0, group[1] < 0) == (fx == 1, fy == 1)]
            if not groups:
                continue
            stacked = jnp.concatenate([part for group in groups for part in parts[group]], 0)
            rows = stacked.shape[0] // (2 * len(groups))
            first = 0 if fx + fy > 0 else 1
            mixed = dot(stacked, flips[2 * fx + fy, :, 256 * first :])
            for order, group in enumerate(groups):
                for part in range(2):
                    start = rows * (2 * order + part)
                    if first == 1:
                        store(group, 0, part, parts[group][part].astype(F32))
                    for z in range(first, 2):
                        span = slice(256 * (z - first), 256 * (z - first) + 256)
                        store(group, z, part, mixed[start : start + rows, span])


def far_sums(columns, spans, flipped, flips, tiles):
    odd_row = lax.rem(sublanes((16, 256)), 2) == 1
    totals = {}
    for position, (cx, cy, cz) in enumerate(canonical_tiles()):
        entries = [
            (gx, gy, dz)
            for gx in sorted({cx, -cx})
            for gy in sorted({cy, -cy})
            for dz in sorted({cz, -cz})
            if gx in columns
        ]
        if not entries:
            continue
        pieces = [[], []]
        for gx, gy, dz in entries:
            for part in range(2):
                view = flipped.at[gx + 1, gy + 1, int(dz < 0), part]
                windows = [
                    [view[half, first + dz : first + dz + size, :] for first, size in spans]
                    for half in range(2)
                ]
                block = jnp.concatenate([jnp.concatenate(window, 0) for window in windows], 1)
                if abs(dz) == 3:
                    block = jnp.where(odd_row if dz < 0 else ~odd_row, block, 0.0)
                pieces[part].append(block.astype(BF16))
        rows = 16 * len(entries)
        part = tiles[0] if position < TILES_FIRST else tiles[1]
        tile = part.at[position % TILES_FIRST]
        both = dot(jnp.concatenate(pieces[0] + pieces[1], 0), tile[0])
        result = both[:rows] + both[rows:] + dot(jnp.concatenate(pieces[0], 0), tile[1])
        for order, (gx, gy, dz) in enumerate(entries):
            key = (int(gx < 0), int(gy < 0), int(dz < 0))
            piece = result[16 * order : 16 * order + 16]
            totals[key] = totals[key] + piece if key in totals else piece
    return totals


def unreflect(totals, flips):
    far = None
    for (fx, fy, fz), total in totals.items():
        if (fx, fy, fz) != (0, 0, 0):
            table = flips[2 * fx + fy, :, 256 * fz : 256 * fz + 256]
            both = dot(jnp.concatenate(halves(total), 0), table)
            total = both[:16] + both[16:]
        far = total if far is None else far + total
    return far


def store_leaves(row, flips, flipped):
    edge = jnp.zeros((8, 128), F32)
    groups = {}
    for gy in (-1, 0, 1):
        columns = []
        for h in range(2):
            start = LEAF_ROWS * (gy + 1) + 16 * h
            columns.append(jnp.concatenate([edge, row[start : start + 16, :], edge], 0))
        groups[0, gy] = jnp.concatenate(columns, 1)
    store_reflected(groups, flips, flipped)


LEAF_SHAPE = (3, 3, 2, 2, 2, 32, 128)
LEAF_SPANS = ((8, 16),)


def far_call(kernel, shape, operands, name):
    return pl.pallas_call(
        kernel,
        out_shape=jax.ShapeDtypeStruct(shape, F32),
        in_specs=[VMEM] * len(operands),
        out_specs=VMEM,
        compiler_params=pltpu.CompilerParams(vmem_limit_bytes=8 * MIB),
        cost_estimate=pl.CostEstimate(flops=300_000_000, bytes_accessed=600_000, transcendentals=0),
        name=name,
    )(*operands)


def own_leaves_call(row, flips, block):
    def kernel(row_ref, flips_ref, block_ref, out, basis_out):
        store_leaves(row_ref, flips_ref, out)
        tables = basis_rows()
        for x in range(CX):
            for y in range(CY):
                for j in range(ROWS):
                    places = [part_row(c, x, y) + j for c in range(3)]
                    rows = [block_ref[place : place + 1, :] for place in places]
                    for k, tile in enumerate(basis_tile(*rows, None, tables)):
                        basis_out[x * CY + y, j, 8 * k : 8 * k + 8, :] = tile

    shapes = LEAF_SHAPE, (CX * CY, ROWS, 64, 128)
    return pl.pallas_call(
        kernel,
        out_shape=[jax.ShapeDtypeStruct(shape, F32) for shape in shapes],
        in_specs=[VMEM] * 3,
        out_specs=[VMEM] * 2,
        compiler_params=pltpu.CompilerParams(vmem_limit_bytes=8 * MIB),
        cost_estimate=near_cost(100_000),
        name="own_leaves",
    )(row, flips, block)


def far_own_call(leaves, flips, tiles):
    def kernel(leaves_ref, flips_ref, tiles_ref, out):
        out[...] = unreflect(far_sums((0,), LEAF_SPANS, leaves_ref, flips_ref, (tiles_ref,)), flips_ref)

    return far_call(kernel, (LZ, 256), (leaves, flips, tiles), "far_own")


def far_side(halo, side_is_low, inside, flips, tiles, flipped):
    flip_x = jnp.where(side_is_low, 1, 0)
    edge = jnp.zeros((8, 128), F32)
    for flip_y, steps in ((0, (0, 1)), (1, (-1,))):
        stacked = []
        for gy in steps:
            columns = []
            for h in range(2):
                row = LEAF_ROWS * (gy + 1) + 16 * h
                moments = jnp.where(inside, halo[row : row + 16, :], 0.0)
                columns.append(jnp.concatenate([edge, moments, edge], 0))
            stacked += halves(jnp.concatenate(columns, 1))
        mixed = dot(jnp.concatenate(stacked, 0), flips[2 * flip_x + flip_y])
        for order, gy in enumerate(steps):
            for part, z, half in itertools.product(range(2), range(2), range(2)):
                start, lane = 32 * (2 * order + part), 256 * z + 128 * half
                flipped[2, gy + 1, z, part, half] = mixed[start : start + 32, lane : lane + 128]
    far = None
    for (_, fy, fz), total in far_sums((1,), LEAF_SPANS, flipped, flips, tiles).items():
        table = flips[2 * flip_x + fy][:, 256 * fz : 256 * fz + 256]
        both = dot(jnp.concatenate(halves(total), 0), table)
        far = both[:16] + both[16:] if far is None else far + both[:16] + both[16:]
    return far


def far_partner_call(partner, tables, after):
    def kernel(partner_ref, flips, one, two, after_ref, out, flipped):
        odd = lax.rem(lax.axis_index("gx"), 2) == 1
        out[...] = far_side(partner_ref, odd, odd | ~odd, flips, (one, two), flipped)

    return pl.pallas_call(
        kernel,
        out_shape=jax.ShapeDtypeStruct((LZ, 256), F32),
        in_specs=[VMEM] * 5,
        out_specs=VMEM,
        scratch_shapes=[pltpu.VMEM(LEAF_SHAPE, F32)],
        compiler_params=pltpu.CompilerParams(vmem_limit_bytes=8 * MIB),
        cost_estimate=pl.CostEstimate(flops=300_000_000, bytes_accessed=600_000, transcendentals=0),
        name="far_partner",
    )(partner, *tables, after)


def beyond_kernel(
    before, beyond, targets, flips, one, two, after, out, far_out, wide_ref, charge_ref, flipped
):
    out[...] = before[...]
    beside_x(1, beyond, targets, out, wide_ref, charge_ref)
    index, count = lax.axis_index("gx"), lax.axis_size("gx")
    inside = (index > 0) & (index < count - 1)
    far_out[...] = far_side(beyond, lax.rem(index, 2) == 0, inside, flips, (one, two), flipped)


def beyond_call(operands):
    return pl.pallas_call(
        beyond_kernel,
        out_shape=(jax.ShapeDtypeStruct(NEAR_SHAPE, F32), jax.ShapeDtypeStruct((LZ, 256), F32)),
        in_specs=[VMEM] * len(operands),
        out_specs=(VMEM,) * 2,
        scratch_shapes=near_scratch(8, 10) + [pltpu.VMEM(LEAF_SHAPE, F32)],
        compiler_params=pltpu.CompilerParams(vmem_limit_bytes=12 * MIB),
        cost_estimate=near_cost(2_400_000),
        name="beyond",
    )(*operands)


def upper_kernel(count_x, count_y, refs):
    own_ones, other_ones, small, flips, *tiles, _, out = refs[:8]
    refs = refs[8:]
    level_one, level_two, flipped, sums, local = refs

    index_x, index_y = lax.axis_index("gx"), lax.axis_index("gy")
    pairs_y = count_y // 2

    level_one[...] = jnp.zeros_like(level_one)
    level_two[...] = jnp.zeros_like(level_two)
    half_x = count_x // 2
    lower = index_x < half_x
    for x in range(half_x):
        for pair in range(pairs_y):
            row = 8 * (x * pairs_y + pair)
            one, two = own_ones[row : row + 8, :], other_ones[row : row + 8, :]
            level_one[x + 2, pair + 1] = jnp.where(lower, one, two)
            level_one[x + half_x + 2, pair + 1] = jnp.where(lower, two, one)
    children = jnp.concatenate(
        [
            jnp.concatenate([level_one[2 * x + 2, y + 1], level_one[2 * x + 3, y + 1]], 1)
            for x in range(half_x)
            for y in range(pairs_y)
        ],
        0,
    )
    below = half_x * pairs_y * 8
    low_lanes = lanes((4, 128)) < 64
    sums[0:below, :] = dot_three(children, small[0:256], small[256:512])
    for x in range(half_x):
        for y in range(pairs_y):
            row = (x * pairs_y + y) * 8
            even = sums[pl.ds(row, 4, stride=2), :]
            odd = sums[pl.ds(row + 1, 4, stride=2), :]
            level_two[x + 2, y + 2, 0:4] = jnp.where(low_lanes, even + lane_flip(odd), 0.0)

    def second_group(group_x, group_y):
        return jnp.concatenate(
            [
                level_two[2 * group_x + h + 2, 2 * group_y + 2]
                + lane_flip(level_two[2 * group_x + h + 2, 2 * group_y + 3])
                for h in range(2)
            ],
            1,
        )

    quarter_x, quarter_y = index_x // 4, index_y // 4
    tops = [(x, y) for x in range(count_x // 4) for y in range(count_y // 4)]
    stacked = jnp.concatenate([second_group(x, y) for x, y in tops], 0)
    if stacked.shape[0] % 16 != 0:
        stacked = jnp.concatenate([stacked, jnp.zeros((8, 256), F32)], 0)
    sums[0 : stacked.shape[0], :] = dot_three(stacked, small[0:256], small[256:512])
    top_far = jnp.zeros((16, 128), F32)
    for position, (x, y) in enumerate(tops):
        even = sums[pl.ds(8 * position, 2, stride=2), :]
        odd = sums[pl.ds(8 * position + 1, 2, stride=2), :]
        third = jnp.where(lanes((2, 128)) < 64, even + lane_flip(odd), 0.0)
        third = third[0:1] + lane_flip(third)[1:2]
        step_x, step_y = x - quarter_x + count_x // 4 - 1, y - quarter_y + count_y // 4 - 1
        row = 1536 + 256 * (step_x * (count_y // 4 * 2 - 1) + step_y)
        table = [small[pl.ds(pl.multiple_of(row + 128 * k, 128), 128), :] for k in range(2)]
        top_far = top_far + dot_three(jnp.broadcast_to(third, (16, 128)), table[0], table[1])

    edge = jnp.zeros((8, 256), F32)
    groups = {}
    for gx in (-1, 0, 1):
        for gy in (-1, 0, 1):
            steps = [2 * (index_x // 2 + gx) + h + 2 for h in range(2)]
            first_level = [level_one[step, index_y // 2 + gy + 1] for step in steps]
            second_level = second_group(quarter_x + gx, quarter_y + gy)
            blocks = [edge, jnp.concatenate(first_level, 1), edge, second_level, edge, edge]
            groups[gx, gy] = jnp.concatenate(blocks, 0)
    store_reflected(groups, flips, flipped)
    far = unreflect(far_sums((-1, 0, 1), ((8, 8), (24, 8)), flipped, flips, tiles), flips)

    def select(block, hx, hy):
        tile = jnp.where(hx == 1, block[:, 128:256], block[:, 0:128])
        return jnp.where(hy == 1, lane_flip(tile), tile)

    def refine(parent):
        keep = lanes((16, 128)) < 64
        parent = jnp.where(keep, parent, 0.0)
        high = parent.astype(BF16).astype(F32)
        low = parent - high
        left = jnp.concatenate([high + lane_flip(low), high], 1).astype(BF16)
        down = jnp.concatenate([small[512 + 256 * k : 768 + 256 * k, :] for k in range(4)], 1)
        spread = dot(left, down)
        for half in range(2):
            for h in range(2):
                span = slice(256 * half + 128 * h, 256 * half + 128 * h + 128)
                local[h, pl.ds(half, 16, stride=2), :] = spread[:, span]
        return jnp.concatenate([local[0], local[1]], 1)

    top_local = jnp.where(
        sublanes((16, 128)) == 0, top_far, jnp.where(sublanes((16, 128)) == 1, lane_flip(top_far), 0.0)
    )
    children_far = refine(top_local)
    half_index_x, half_index_y = index_x // 2, index_y // 2
    second = select(children_far[0:8], lax.rem(half_index_x, 2), lax.rem(half_index_y, 2))
    second = second + 0.25 * select(far[8:16], lax.rem(half_index_x, 2), lax.rem(half_index_y, 2))
    zeros = jnp.zeros((8, 128), F32)
    children_far = refine(jnp.concatenate([second, zeros], 0))
    first = select(children_far[0:8], lax.rem(index_x, 2), lax.rem(index_y, 2))
    first = first + 0.5 * select(far[0:8], lax.rem(index_x, 2), lax.rem(index_y, 2))
    out[...] = refine(jnp.concatenate([first, zeros], 0))[0:16]


def upper_call(count_x, count_y, operands):
    half_x, half_y = count_x // 2, count_y // 2
    scratch = [
        pltpu.VMEM((count_x + 4, half_y + 2, 8, 128), F32),
        pltpu.VMEM((half_x + 4, half_y + 4, 8, 128), F32),
        pltpu.VMEM((3, 3, 2, 2, 2, 48, 128), F32),
        pltpu.VMEM((max(16, half_x * half_y * 8), 128), F32),
        pltpu.VMEM((2, 32, 128), F32),
    ]
    return pl.pallas_call(
        lambda *refs: upper_kernel(count_x, count_y, refs),
        out_shape=jax.ShapeDtypeStruct((LZ, 256), F32),
        in_specs=[VMEM] * len(operands),
        out_specs=VMEM,
        scratch_shapes=scratch,
        compiler_params=pltpu.CompilerParams(vmem_limit_bytes=8 * MIB),
        cost_estimate=pl.CostEstimate(flops=900_000_000, bytes_accessed=600_000, transcendentals=0),
        name="upper",
    )(*operands)


def last_kernel(basis, near_rows, local, far_own, far_partner, far_beyond, out):
    leaf = local[...] + far_own[...] + far_partner[...] + far_beyond[...]

    one, two = halves(leaf)
    turned = jnp.concatenate([one.astype(F32), two.astype(F32)], 0).T.astype(BF16)
    table = leaf_segments(2 * LZ)
    for x in range(CX):
        for y in range(CY):
            column = x * CY + y
            spread = dot(turned[64 * column : 64 * column + 64], table)
            for j in range(ROWS):
                span = slice(128 * j, 128 * j + 128)
                total = None
                for k in range(8):
                    term = basis[column, j, 8 * k : 8 * k + 8, :] * spread[8 * k : 8 * k + 8, span]
                    total = term if total is None else total + term
                value = jnp.sum(total, 0, keepdims=True) + near_rows[column, j : j + 1, :]
                out[x, y : y + 1, span] = value


def last_call(operands):
    return pl.pallas_call(
        last_kernel,
        out_shape=jax.ShapeDtypeStruct((CX, CY, LZ * 64), F32),
        in_specs=[VMEM] * len(operands),
        out_specs=VMEM,
        compiler_params=pltpu.CompilerParams(vmem_limit_bytes=8 * MIB),
        name="last",
    )(*operands)


def in_hbm(value):
    return pltpu.with_memory_space_constraint(value, pltpu.HBM)


def swap_bit(value, axis, bit):
    return lax.ppermute(value, axis, [(i, i ^ (1 << bit)) for i in range(lax.axis_size(axis))])


def relay_ring(value, axis):
    count = lax.axis_size(axis)
    steps = {i: i + 2 if i % 2 == 0 else i - 2 for i in range(count)}
    steps[count - 2], steps[1] = count - 1, 0
    return lax.ppermute(value, axis, list(steps.items()))


def solution(mesh):
    count_x, count_y = mesh.shape["gx"], mesh.shape["gy"]
    levels_x, levels_y = count_x.bit_length() - 1, count_y.bit_length() - 1
    tiles = translation_tiles()
    small = small_tables(count_x // 4, count_y // 4)
    tables = small, reflection_tables(), tiles[:TILES_FIRST], tiles[TILES_FIRST:]

    def body(offsets, charges):
        small, flips, *tiles = [in_hbm(jnp.asarray(table)) for table in tables]
        block = moments_call(in_hbm(offsets), in_hbm(charges), small)
        other = swap_bit(block, "gy", 0)
        exchanged = []

        def exchange_y(after):
            pair = block, other
            for level in range(1, levels_y):
                last = level == levels_y - 1
                rows = (ONE_ROWS << (level - 1)) + EDGE_ROWS * (1 if last else 2)
                kernel = functools.partial(group_kernel, level, last)
                sent = pack_call(kernel, rows, (*pair, after), "group")
                pair = sent, swap_bit(sent, "gy", level)
                exchanged.extend(pair)
            return exchanged[0]

        near, targets, small, first_tiles = own_call(block, exchange_y, small, tiles[0])
        row, far = row_call(levels_y, (block, other, *exchanged, near))
        partner = swap_bit(row, "gx", 0)
        partner_far = swap_bit(far, "gx", 0)
        near, flips, other_tiles = beside_y_call(row, far, targets, near, (flips, tiles[1]))
        leaves, basis = own_leaves_call(row, flips, block)
        far_own = far_own_call(leaves, flips, first_tiles)
        rows = ONE_ROWS << (levels_y - 1)
        ones = merge_call(0, row, partner, ROW_ROWS, rows, SENT_ROWS, far_own)
        other_ones = swap_bit(ones, "gx", 1)
        beyond = relay_ring(relay_call(partner, partner_far, ones), "gx")
        far_tables = flips, first_tiles, other_tiles
        far_partner = far_partner_call(partner, far_tables, ones)
        near = near_call(beside_x_kernel, (partner, targets, near, far_partner), 8, 10, 1_200_000, "near_x")
        for bit in range(1, levels_x - 1):
            ones = merge_call(bit, ones, other_ones, 0, rows << bit, 0, near)
            other_ones = swap_bit(ones, "gx", bit + 1)
        near, far_beyond = beyond_call((near, beyond, targets, *far_tables, ones))
        local = upper_call(count_x, count_y, (ones, other_ones, small, *far_tables, near))
        return last_call((basis, near, local, far_own, far_partner, far_beyond))

    in_specs = (P(None, "gx", "gy", None), P("gx", "gy", None))
    out_specs = P("gx", "gy", None)
    return jax.shard_map(body, mesh=mesh, in_specs=in_specs, out_specs=out_specs, check_vma=False)
```

```python
import functools
import itertools

import jax
import jax.numpy as jnp
import ml_dtypes
import numpy as np
from jax import lax
from jax.experimental import pallas as pl
from jax.experimental.pallas import tpu as pltpu
from jax.sharding import PartitionSpec as P

F32 = jnp.float32
BF16 = jnp.bfloat16
MIB = 1 << 20

CX = 2
CY = 2
LZ = 16
ROWS = 8
FEATURES = 32
VMEM = pl.BlockSpec(memory_space=pltpu.VMEM)
HBM = pl.BlockSpec(memory_space=pltpu.HBM)


def nodes_1d():
    return np.cos((2.0 * np.arange(4) + 1.0) * np.pi / 8.0)


def cheb_terms(value):
    return value, 2.0 * value * value - 1.0, 4.0 * value**3 - 3.0 * value


def node_weights():
    return [[0.5 * term for term in cheb_terms(point)] for point in nodes_1d()]


def node_grid():
    points = nodes_1d()
    counter = np.arange(64)
    return np.stack([points[counter // 16], points[counter // 4 % 4], points[counter % 4]], -1)


def split_two(table):
    high = table.astype(np.float32).astype(ml_dtypes.bfloat16)
    low = (table - high.astype(np.float64)).astype(np.float32).astype(ml_dtypes.bfloat16)
    return high, low


def upward_tensor():
    points = nodes_1d()
    shifted = (points[None, :] + 2.0 * np.arange(2)[:, None] - 1.0) / 2.0
    factor = 0.25 + 0.0 * shifted[..., None]
    for of_value, of_node in zip(cheb_terms(shifted), cheb_terms(points)):
        factor = factor + 0.5 * of_value[..., None] * of_node
    full = np.einsum("xia,yjb,zkc->xyzijkabc", factor, factor, factor)
    return full.reshape(2, 2, 2, 64, 64)


def inverse_distance(offset):
    grid = node_grid()
    spread = (grid[None, :, :] - grid[:, None, :]) / 2.0 - np.asarray(offset, np.float64)
    return 1.0 / np.sqrt(np.sum(spread * spread, -1))


def adjacent(offset):
    return max(abs(int(step)) for step in offset) <= 1


def canonical_tiles():
    return [
        (cx, cy, cz)
        for cx in range(2)
        for cy in range(2)
        for cz in range(4)
        if not (cx == 0 and cy == 0 and cz <= 1)
    ]


TILES_FIRST = 10


def translation_tiles():
    tiles = []
    for cx, cy, cz in canonical_tiles():
        tile = np.zeros((4, 64, 4, 64))
        for source in range(4):
            for target in range(4):
                offset = (
                    2 * cx + source // 2 - target // 2,
                    2 * cy + source % 2 - target % 2,
                    cz,
                )
                if not adjacent(offset):
                    tile[source, :, target, :] = inverse_distance(offset)
        tiles.append(tile.reshape(256, 256))
    return np.stack(split_two(np.stack(tiles)), 1)


def reflection_matrix(flip_x, flip_y, flip_z):
    index = np.arange(256)
    hx, hy, a, b, c = index // 128, index // 64 % 2, index // 16 % 4, index // 4 % 4, index % 4
    if flip_x:
        hx, a = 1 - hx, 3 - a
    if flip_y:
        hy, b = 1 - hy, 3 - b
    if flip_z:
        c = 3 - c
    matrix = np.zeros((256, 256), np.float32)
    matrix[hx * 128 + hy * 64 + a * 16 + b * 4 + c, index] = 1.0
    return matrix


def reflection_tables():
    pairs = [
        np.concatenate([reflection_matrix(fx, fy, 0), reflection_matrix(fx, fy, 1)], 1)
        for fx in range(2)
        for fy in range(2)
    ]
    return np.stack(pairs).astype(ml_dtypes.bfloat16)


def up_tables():
    upward = upward_tensor()
    table = upward.transpose(0, 1, 3, 2, 4).reshape(256, 128)
    return np.stack(split_two(table))


def down_table():
    upward = upward_tensor()
    table = upward.transpose(4, 2, 0, 1, 3).reshape(64, 512)
    high, low = split_two(table)
    return np.concatenate([high, high, low, np.zeros_like(low)], 0)


def top_tables(boxes_x, boxes_y):
    offsets = range(-(boxes_x - 1), boxes_x), range(-(boxes_y - 1), boxes_y)
    table = np.zeros((len(offsets[0]), len(offsets[1]), 2, 64, 2, 64))
    for (ix, dx), (iy, dy) in itertools.product(enumerate(offsets[0]), enumerate(offsets[1])):
        for source, target in itertools.product(range(2), range(2)):
            offset = (dx, dy, source - target)
            if not adjacent(offset):
                table[ix, iy, source, :, target, :] = 0.125 * inverse_distance(offset)
    return np.stack(split_two(table.reshape(len(offsets[0]), len(offsets[1]), 128, 128)), 2)


def small_tables(boxes_x, boxes_y):
    down = down_table().reshape(256, 4, 128).transpose(1, 0, 2)
    parts = [up_tables(), down, top_tables(boxes_x, boxes_y)]
    return np.concatenate([part.reshape(-1, 128) for part in parts], 0)


def halves(value):
    high = value.astype(BF16)
    return high, (value - high.astype(F32)).astype(BF16)


def dot(left, right):
    return jnp.dot(left, right, preferred_element_type=F32)


def dot_three(value, high_table, low_table):
    rows = value.shape[0]
    high, low = halves(value)
    both = dot(jnp.concatenate([high, low], 0), high_table)
    return both[:rows] + both[rows:] + dot(high, low_table)


def lanes(shape):
    return lax.broadcasted_iota(jnp.int32, shape, len(shape) - 1)


def sublanes(shape):
    return lax.broadcasted_iota(jnp.int32, shape, len(shape) - 2)


def leaf_segments(leaves):
    shape = (leaves, LZ * 64)
    return jnp.where(lanes(shape) // 64 == lax.rem(sublanes(shape), LZ), 1.0, 0.0).astype(BF16)


def lane_flip(value):
    return pltpu.roll(value, 64, 1)


def weight_rows(pattern):
    weights = node_weights()
    index = sublanes((8, 128))
    rows = []
    for term in range(3):
        row = jnp.full((8, 128), weights[pattern(0)][term], F32)
        for sub in range(1, 8):
            row = jnp.where(index == sub, weights[pattern(sub)][term], row)
        rows.append(row)
    return rows


def basis_rows():
    return (
        weight_rows(lambda sub: sub // 4),
        weight_rows(lambda sub: 2 + sub // 4),
        weight_rows(lambda sub: sub % 4),
    )


def basis_tile(row_x, row_y, row_z, scale, tables):
    y_low, y_high, z_all = tables
    wide = [jnp.broadcast_to(2.0 * row - 1.0, (8, 128)) for row in (row_x, row_y, row_z)]
    terms = [cheb_terms(value) for value in wide]

    def mix(weights, term):
        return 0.25 + (weights[0] * term[0] + weights[1] * term[1] + weights[2] * term[2])

    along_z = mix(z_all, terms[2])
    pair = mix(y_low, terms[1]) * along_z, mix(y_high, terms[1]) * along_z
    tiles = []
    for weights in node_weights():
        along_x = mix(weights, terms[0])
        if scale is not None:
            along_x = along_x * scale
        tiles += [along_x * pair[0], along_x * pair[1]]
    return tiles


def three_pieces(value):
    first = value.astype(BF16).astype(F32)
    rest = value - first
    second = rest.astype(BF16).astype(F32)
    return first, second, rest - second


PIECES = 12


def feature_pieces(coords, scale):
    total = coords[0] * coords[0] + coords[1] * coords[1] + coords[2] * coords[2]
    return [piece for value in [scale * coord for coord in coords] + [total] for piece in three_pieces(value)]


def pick(row, pieces, choice):
    value = jnp.broadcast_to(pieces[choice[0]], (8, 128))
    for piece in sorted(set(choice) - {choice[0]}):
        mask = None
        for place, chosen in enumerate(choice):
            if chosen == piece:
                mask = row == place if mask is None else mask | (row == place)
        value = jnp.where(mask, jnp.broadcast_to(pieces[piece], (8, 128)), value)
    return value


def feature_block(read, choice, length_choice):
    row = sublanes((8, 128))
    zero, one = jnp.zeros((1, 128), F32), jnp.ones((1, 128), F32)
    blocks = [
        pick(row, [read(3 * c), read(3 * c + 1), read(3 * c + 2), zero], choice) for c in range(3)
    ]
    blocks.append(pick(row, [read(9), read(10), read(11), one, zero], length_choice))
    return jnp.concatenate(blocks, 0)


SOURCE_CHOICE = (0, 1, 0, 1, 2, 0, 0, 0), (3, 3, 3, 0, 1, 2, 3, 3)
TARGET_CHOICE = (0, 0, 1, 1, 0, 2, 3, 3), (0, 1, 2, 3, 3, 3, 4, 4)


def column(raw, x, y):
    return raw(0) + (x - 2.0), raw(1) + (y - 2.0), raw(2), raw(3)


class Near:
    def __init__(self, wide_ref, charge_ref, target_ref):
        self.wide_ref = wide_ref
        self.charge_ref = charge_ref
        self.target_ref = target_ref
        self.groups = 0
        self.charges = 0
        self.upper = lanes((ROWS, 128)) >= 64
        self.row = sublanes((ROWS, 128))

    def in_pair(self, along_z):
        return along_z + jnp.where(self.upper, 0.0, -1.0)

    def targets(self, columns):
        for ab, (x, y, z, _) in enumerate(columns):
            pieces = feature_pieces((x, y, self.in_pair(z)), -2.0)
            for j in range(ROWS):
                block = feature_block(lambda k: pieces[k][j : j + 1], *TARGET_CHOICE)
                self.target_ref[ab, j] = block.T.astype(BF16)

    def add_group(self, coords):
        for k, piece in enumerate(feature_pieces(coords, 1.0)):
            self.wide_ref[self.groups, k] = piece
        self.groups += 1
        return self.groups - 1

    def add_charge(self, charge):
        self.charge_ref[self.charges] = charge
        self.charges += 1
        return self.charges - 1

    def main(self, source):
        x, y, z, charge = source
        return self.add_group((x, y, self.in_pair(z))), self.add_charge(charge)

    def outer(self, first, second, side, keep=False):
        def merge(one, two):
            if side == 0:
                value = jnp.where(self.upper, two, lane_flip(one))
                return pltpu.roll(value, 1, 0)
            value = jnp.where(self.upper, lane_flip(two), one)
            return pltpu.roll(value, ROWS - 1, 0)

        x, y, z, charge = [merge(one, two) for one, two in zip(first, second)]
        charge = jnp.where(self.row == (0 if side == 0 else ROWS - 1), 0.0, charge)
        group = self.add_group((x, y, z + (-2.0 if side == 0 else 1.0)))
        if not keep:
            return group, self.add_charge(charge)
        low = self.add_charge(jnp.where(self.upper, 0.0, charge))
        high = self.add_charge(jnp.where(self.upper, charge, 0.0))
        return (group, low), (group, high)

    def run(self, plan, emit):
        eye = sublanes((128, 128)) == lanes((128, 128))

        def source(group, j, built):
            if group not in built:
                read = lambda k: self.wide_ref[group, k, pl.ds(j, 1), :]
                built[group] = feature_block(read, *SOURCE_CHOICE).astype(BF16)
            return built[group]

        def pairs(targets, tiles, j, own, total, built):
            block = jnp.concatenate([source(group, j, built) for group, _ in tiles], 1)
            squared = dot(targets, block)
            for position, (group, charge) in enumerate(tiles):
                inverse = lax.rsqrt(squared[:, 128 * position : 128 * position + 128])
                if group == own:
                    inverse = jnp.where(eye, 0.0, inverse)
                total = total + inverse * self.charge_ref[charge, pl.ds(j, 1), :]
            return total

        def step(j, carry):
            built = {}
            for ab, mains, below, above, own in plan:
                targets = self.target_ref[ab, j]
                total = pairs(targets, mains, j, own, jnp.zeros((128, 128), F32), built)
                lower = pairs(targets[:64], below, j, None, total[:64], built)
                higher = pairs(targets[64:], above, j, None, total[64:], built)
                total = jnp.concatenate([lower, higher], 0)
                emit(ab, j, jnp.sum(total.T, 0, keepdims=True))
            return carry

        lax.fori_loop(0, ROWS, step, 0, unroll=True)


def plan_own(near, columns):
    mains = [near.main(source) for source in columns]
    outer = [
        [near.outer(columns[2 * x], columns[2 * x + 1], side) for x in range(2)]
        for side in range(2)
    ]
    return [(ab, mains, outer[0], outer[1], mains[ab][0]) for ab in range(4)]


def plan_beside_y(near, columns):
    plan = []
    for b in range(2):
        mains = [near.main(source) for source in columns[b]]
        outer = [[near.outer(*columns[b], side)] for side in range(2)]
        plan += [(2 * a + b, mains, outer[0], outer[1], None) for a in range(2)]
    return plan


def plan_beside_x(near, columns, side_x):
    mains = [near.main(source) for source in columns]
    middle = [near.outer(columns[1], columns[2], side) for side in range(2)]
    ends = [near.outer(columns[0], columns[3], side, keep=True) for side in range(2)]
    return [
        (2 * side_x + b, mains[b : b + 3], [middle[0], ends[0][b]], [middle[1], ends[1][b]], None)
        for b in range(2)
    ]


def near_scratch(groups, charges):
    return [
        pltpu.VMEM((groups, PIECES, ROWS, 128), F32),
        pltpu.VMEM((charges, ROWS, 128), F32),
    ]


NEAR_SHAPE = (4, ROWS, 128)


def near_cost(pairs):
    return pl.CostEstimate(flops=40 * pairs, bytes_accessed=600_000, transcendentals=pairs)


ONE_ROWS = 8
LEAF_ROWS = 32
PART_ROWS = 4 * CX * CY * ROWS
OWN_ROWS = ONE_ROWS + LEAF_ROWS + PART_ROWS


def part_row(c, x, y):
    return ONE_ROWS + LEAF_ROWS + ((c * CX + x) * CY + y) * ROWS


def moments_kernel(
    offsets_hbm, charges_hbm, small_hbm, block, offsets, charges, up, basis, sums, semaphores
):
    index_y = lax.axis_index("gy")
    copies = [
        pltpu.make_async_copy(offsets_hbm, offsets, semaphores.at[0]),
        pltpu.make_async_copy(charges_hbm, charges, semaphores.at[1]),
        pltpu.make_async_copy(small_hbm.at[0:512], up, semaphores.at[2]),
    ]
    for copy in copies:
        copy.start()
    tables = basis_rows()
    segments = leaf_segments(LZ)
    copies[0].wait()
    copies[1].wait()
    for x in range(CX):
        for y in range(CY):
            for j in range(ROWS):
                span = slice(128 * j, 128 * j + 128)
                rows = [offsets[c, x, y : y + 1, span] for c in range(3)]
                charge = charges[x, y : y + 1, span]
                for c, row in enumerate(rows + [charge]):
                    place = part_row(c, x, y) + j
                    block[place : place + 1, :] = row
                tiles = basis_tile(*rows, charge, tables)
                for k in range(4):
                    pair = jnp.concatenate(tiles[2 * k : 2 * k + 2], 0)
                    high, low = halves(pair)
                    first = (x * CY + y) * 64 + 16 * k
                    basis[0, first : first + 16, span] = high
                    basis[1, first : first + 16, span] = low
    contract = (((1,), (1,)), ((), ()))
    leaf = lax.dot_general(segments, basis[0], contract, preferred_element_type=F32)
    leaf = leaf + lax.dot_general(segments, basis[1], contract, preferred_element_type=F32)
    copies[2].wait()
    sums[...] = dot_three(leaf, up[0:256], up[256:512])
    first = sums[pl.ds(0, 8, stride=2), :] + lane_flip(sums[pl.ds(1, 8, stride=2), :])
    first = jnp.where(lanes((8, 128)) < 64, first, 0.0)
    first = jnp.where(lax.rem(index_y, 2) == 1, lane_flip(first), first)
    block[0:8, :] = first
    block[8:24, :] = leaf[:, :128]
    block[24:40, :] = leaf[:, 128:]


def moments_call(offsets, charges, small):
    return pl.pallas_call(
        moments_kernel,
        out_shape=jax.ShapeDtypeStruct((OWN_ROWS, 128), F32),
        in_specs=[HBM] * 3,
        out_specs=VMEM,
        scratch_shapes=[
            pltpu.VMEM(offsets.shape, F32),
            pltpu.VMEM(charges.shape, F32),
            pltpu.VMEM((512, 128), BF16),
            pltpu.VMEM((2, 256, 1024), BF16),
            pltpu.VMEM((16, 128), F32),
            pltpu.SemaphoreType.DMA((3,)),
        ],
        compiler_params=pltpu.CompilerParams(vmem_limit_bytes=8 * MIB),
        cost_estimate=pl.CostEstimate(flops=10_000_000, bytes_accessed=300_000, transcendentals=0),
        name="moments",
    )(offsets, charges, small)


EDGE_ROWS = LEAF_ROWS + 4 * CX * ROWS


def bits_below(index, bit):
    return lax.rem(index, 1 << bit)


def bit_of(index, bit):
    return lax.rem(index // (1 << bit), 2)


def in_order(is_first, own, other):
    return jnp.concatenate([jnp.where(is_first, own, other), jnp.where(is_first, other, own)], 0)


def edge_block(block, y):
    rows = [block[ONE_ROWS : ONE_ROWS + LEAF_ROWS, :]]
    for c in range(4):
        for x in range(CX):
            rows.append(block[part_row(c, x, y) : part_row(c, x, y) + ROWS, :])
    return jnp.concatenate(rows, 0)


def group_kernel(level, last_level, own_ref, other_ref, after, out):
    index = lax.axis_index("gy")
    ones = ONE_ROWS << (level - 1)
    is_first = bit_of(index, level - 1) == 0
    if level == 1:
        out[0:ones, :] = own_ref[0:ones, :] + other_ref[0:ones, :]
        first = jnp.where(is_first, edge_block(own_ref, 0), edge_block(other_ref, 0))
        last = jnp.where(is_first, edge_block(other_ref, 1), edge_block(own_ref, 1))
    else:
        half = ones // 2
        out[0:ones, :] = in_order(is_first, own_ref[0:half, :], other_ref[0:half, :])
        own_far = own_ref[half + EDGE_ROWS : half + 2 * EDGE_ROWS, :]
        other_far = other_ref[half + EDGE_ROWS : half + 2 * EDGE_ROWS, :]
        first = jnp.where(is_first, own_far, other_far)
        last = jnp.where(is_first, other_far, own_far)
    lower = bit_of(index, level) == 0
    out[ones : ones + EDGE_ROWS, :] = jnp.where(lower, last, first)
    if not last_level:
        out[ones + EDGE_ROWS : ones + 2 * EDGE_ROWS, :] = jnp.where(lower, first, last)


def pack_call(kernel, rows, operands, name):
    return pl.pallas_call(
        kernel,
        out_shape=jax.ShapeDtypeStruct((rows, 128), F32),
        in_specs=[VMEM] * len(operands),
        out_specs=VMEM,
        compiler_params=pltpu.CompilerParams(vmem_limit_bytes=8 * MIB),
        cost_estimate=pl.CostEstimate(flops=100_000, bytes_accessed=300_000, transcendentals=0),
        name=name,
    )(*operands)


ROW_LEAF = 3 * LEAF_ROWS
ROW_PART = 4 * 4 * ROWS
ROW_ROWS = ROW_LEAF + ROW_PART


def row_part(c, y):
    return ROW_LEAF + (c * 4 + y) * ROWS


def row_kernel(levels, block, other, *refs):
    exchanged, (out, far_out) = refs[: 2 * (levels - 1)], refs[-2:]
    index = lax.axis_index("gy")
    even = lax.rem(lax.axis_index("gx"), 2) == 0
    is_first = bit_of(index, 0) == 0
    low = jnp.where(is_first, 0.0, edge_block(other, 1))
    high = jnp.where(is_first, edge_block(other, 0), 0.0)
    ones = ONE_ROWS
    for level in range(1, levels):
        own, received = exchanged[2 * level - 2 : 2 * level]
        ones = ONE_ROWS << (level - 1)
        facing = received[ones : ones + EDGE_ROWS, :]
        below = bits_below(index, level)
        upper = bit_of(index, level) == 1
        low = jnp.where(upper & (below == 0), facing, low)
        high = jnp.where(~upper & (below == (1 << level) - 1), facing, high)
        if level == levels - 1:
            out[ROW_ROWS:, :] = in_order(~upper, own[0:ones, :], received[0:ones, :])
    leaf = block[ONE_ROWS : ONE_ROWS + LEAF_ROWS, :]
    for piece, rows in enumerate((low[0:LEAF_ROWS], leaf, high[0:LEAF_ROWS])):
        out[LEAF_ROWS * piece : LEAF_ROWS * (piece + 1), :] = rows
    for c in range(4):
        columns = []
        for x in range(CX):
            row = LEAF_ROWS + (c * CX + x) * ROWS
            own = [block[part_row(c, x, y) : part_row(c, x, y) + ROWS, :] for y in range(CY)]
            columns.append([low[row : row + ROWS], *own, high[row : row + ROWS]])
        for y in range(4):
            facing, far = row_part(c, y), row_part(c, y) - ROW_LEAF
            out[facing : facing + ROWS, :] = jnp.where(even, columns[1][y], columns[0][y])
            far_out[far : far + ROWS, :] = jnp.where(even, columns[0][y], columns[1][y])


def row_call(levels, operands):
    return pl.pallas_call(
        lambda *refs: row_kernel(levels, *refs[: 2 * levels], *refs[-2:]),
        out_shape=[
            jax.ShapeDtypeStruct((rows, 128), F32)
            for rows in (ROW_ROWS + (ONE_ROWS << (levels - 1)), ROW_PART)
        ],
        in_specs=[VMEM] * len(operands),
        out_specs=[VMEM] * 2,
        compiler_params=pltpu.CompilerParams(vmem_limit_bytes=8 * MIB),
        cost_estimate=pl.CostEstimate(flops=100_000, bytes_accessed=600_000, transcendentals=0),
        name="row",
    )(*operands)


SENT_ROWS = 184


def merge_call(bit, own, other, first, rows, least, after):
    total = max(2 * rows, least)

    def kernel(own_ref, other_ref, after_ref, out):
        is_first = bit_of(lax.axis_index("gx"), bit) == 0
        span = slice(first, first + rows)
        out[0 : 2 * rows, :] = in_order(is_first, own_ref[span, :], other_ref[span, :])
        if total > 2 * rows:
            out[2 * rows :, :] = jnp.zeros((total - 2 * rows, 128), F32)

    return pack_call(kernel, total, (own, other, after), "merge")


def relay_call(received, received_far, after):
    def kernel(received_ref, far_ref, after_ref, out):
        out[0:ROW_LEAF, :] = received_ref[0:ROW_LEAF, :]
        out[ROW_LEAF:ROW_ROWS, :] = far_ref[...]

    return pack_call(kernel, ROW_ROWS, (received, received_far, after), "relay")


def own_kernel(block, targets, features, charges):
    near = Near(features, charges, targets)

    def raw(x, y):
        return lambda c: block[part_row(c, x, y) : part_row(c, x, y) + ROWS, :]

    columns = [column(raw(ab // 2, ab % 2), ab // 2 + 1, ab % 2 + 1) for ab in range(4)]
    near.targets(columns)
    return near, plan_own(near, columns)


def own_call(block, after, small, tiles):
    plans = []

    def prepare(block_ref, small, targets, features, charges, small_out, semaphore):
        copy = pltpu.make_async_copy(small, small_out, semaphore)
        copy.start()
        plans.append(own_kernel(block_ref, targets, features, charges)[1])
        copy.wait()

    def run(targets, features, charges, after_ref, tiles, out, tiles_out, semaphore):
        copy = pltpu.make_async_copy(tiles, tiles_out, semaphore)
        copy.start()

        def emit(ab, j, row):
            out[ab, pl.ds(j, 1), :] = row

        Near(features, charges, targets).run(plans[0], emit)
        copy.wait()

    prepared = pl.pallas_call(
        prepare,
        out_shape=(
            jax.ShapeDtypeStruct((4, ROWS, 128, FEATURES), BF16),
            jax.ShapeDtypeStruct((8, PIECES, ROWS, 128), F32),
            jax.ShapeDtypeStruct((8, ROWS, 128), F32),
            jax.ShapeDtypeStruct(small.shape, BF16),
        ),
        in_specs=[VMEM, HBM],
        out_specs=(VMEM,) * 4,
        scratch_shapes=[pltpu.SemaphoreType.DMA],
        compiler_params=pltpu.CompilerParams(vmem_limit_bytes=8 * MIB),
        cost_estimate=near_cost(500_000),
        name="features",
    )(block, small)
    near, tiles_near = pl.pallas_call(
        run,
        out_shape=(
            jax.ShapeDtypeStruct(NEAR_SHAPE, F32),
            jax.ShapeDtypeStruct(tiles.shape, BF16),
        ),
        in_specs=[VMEM] * 4 + [HBM],
        out_specs=(VMEM,) * 2,
        scratch_shapes=[pltpu.SemaphoreType.DMA],
        compiler_params=pltpu.CompilerParams(vmem_limit_bytes=8 * MIB),
        cost_estimate=near_cost(4_500_000),
        name="near_own",
    )(*prepared[:3], after(prepared[2]), tiles)
    return near, prepared[0], prepared[3], tiles_near


def beside_y_kernel(
    row_ref, far_ref, targets, before, flips, tiles, out, flips_out, tiles_out, wide_ref, charge_ref, semaphores
):
    copies = [
        pltpu.make_async_copy(flips, flips_out, semaphores.at[0]),
        pltpu.make_async_copy(tiles, tiles_out, semaphores.at[1]),
    ]
    for copy in copies:
        copy.start()
    even = lax.rem(lax.axis_index("gx"), 2) == 0
    near = Near(wide_ref, charge_ref, targets)

    def raw(x, y):
        def read(c):
            facing, far = row_part(c, y), row_part(c, y) - ROW_LEAF
            own = row_ref[facing : facing + ROWS, :], far_ref[far : far + ROWS, :]
            return jnp.where(even == (x == 1), *own)

        return read

    columns = [[column(raw(x, y), x + 1, y) for x in range(2)] for y in (0, 3)]
    plan = plan_beside_y(near, columns)
    out[...] = before[...]

    def emit(ab, j, row):
        out[ab, pl.ds(j, 1), :] = out[ab, pl.ds(j, 1), :] + row

    near.run(plan, emit)
    for copy in copies:
        copy.wait()


def beside_y_call(row, far, targets, before, constants):
    near_shape = jax.ShapeDtypeStruct(NEAR_SHAPE, F32)
    tables = [jax.ShapeDtypeStruct(constant.shape, BF16) for constant in constants]
    return pl.pallas_call(
        beside_y_kernel,
        out_shape=(near_shape, *tables),
        in_specs=[VMEM] * 4 + [HBM] * 2,
        out_specs=(VMEM,) * 3,
        scratch_shapes=near_scratch(8, 8) + [pltpu.SemaphoreType.DMA((2,))],
        compiler_params=pltpu.CompilerParams(vmem_limit_bytes=8 * MIB),
        cost_estimate=near_cost(2_200_000),
        name="near_y",
    )(row, far, targets, before, *constants)


def beside_x(parity, received, targets, out, wide_ref, charge_ref):
    index, count = lax.axis_index("gx"), lax.axis_size("gx")
    even = lax.rem(index, 2) == 0
    side = jnp.where(even == (parity == 0), 1, 0)
    alone = (index == 0) | (index == count - 1)
    near = Near(wide_ref, charge_ref, targets)

    def raw(y):
        def coordinate(c):
            value = received[row_part(c, y) : row_part(c, y) + ROWS, :]
            return jnp.where(alone, 0.0, value) if c == 3 and parity == 1 else value

        return coordinate

    columns = [column(raw(y), 3.0 * side.astype(F32), y) for y in range(4)]
    plan = plan_beside_x(near, columns, side)

    def emit(ab, j, row):
        out[ab, pl.ds(j, 1), :] = out[ab, pl.ds(j, 1), :] + row

    near.run(plan, emit)


def beside_x_kernel(received, targets, before, after, out, wide_ref, charge_ref):
    out[...] = before[...]
    beside_x(0, received, targets, out, wide_ref, charge_ref)


def near_call(kernel, operands, groups, charges, pairs, name):
    return pl.pallas_call(
        kernel,
        out_shape=jax.ShapeDtypeStruct(NEAR_SHAPE, F32),
        in_specs=[VMEM] * len(operands),
        out_specs=VMEM,
        scratch_shapes=near_scratch(groups, charges),
        compiler_params=pltpu.CompilerParams(vmem_limit_bytes=12 * MIB),
        cost_estimate=near_cost(pairs),
        name=name,
    )(*operands)


def store_reflected(moments, flips, flipped):
    def store(group, z, part, value):
        for half in range(2):
            place = flipped.at[group[0] + 1, group[1] + 1, z, part, half]
            place[...] = value[:, 128 * half : 128 * half + 128]

    parts = {group: halves(value) for group, value in moments.items()}
    for fx in range(2):
        for fy in range(2):
            groups = [group for group in moments if (group[0] < 0, group[1] < 0) == (fx == 1, fy == 1)]
            if not groups:
                continue
            stacked = jnp.concatenate([part for group in groups for part in parts[group]], 0)
            rows = stacked.shape[0] // (2 * len(groups))
            first = 0 if fx + fy > 0 else 1
            mixed = dot(stacked, flips[2 * fx + fy, :, 256 * first :])
            for order, group in enumerate(groups):
                for part in range(2):
                    start = rows * (2 * order + part)
                    if first == 1:
                        store(group, 0, part, parts[group][part].astype(F32))
                    for z in range(first, 2):
                        span = slice(256 * (z - first), 256 * (z - first) + 256)
                        store(group, z, part, mixed[start : start + rows, span])


def far_sums(columns, spans, flipped, flips, tiles):
    odd_row = lax.rem(sublanes((16, 256)), 2) == 1
    totals = {}
    for position, (cx, cy, cz) in enumerate(canonical_tiles()):
        entries = [
            (gx, gy, dz)
            for gx in sorted({cx, -cx})
            for gy in sorted({cy, -cy})
            for dz in sorted({cz, -cz})
            if gx in columns
        ]
        if not entries:
            continue
        pieces = [[], []]
        for gx, gy, dz in entries:
            for part in range(2):
                view = flipped.at[gx + 1, gy + 1, int(dz < 0), part]
                windows = [
                    [view[half, first + dz : first + dz + size, :] for first, size in spans]
                    for half in range(2)
                ]
                block = jnp.concatenate([jnp.concatenate(window, 0) for window in windows], 1)
                if abs(dz) == 3:
                    block = jnp.where(odd_row if dz < 0 else ~odd_row, block, 0.0)
                pieces[part].append(block.astype(BF16))
        rows = 16 * len(entries)
        part = tiles[0] if position < TILES_FIRST else tiles[1]
        tile = part.at[position % TILES_FIRST]
        both = dot(jnp.concatenate(pieces[0] + pieces[1], 0), tile[0])
        result = both[:rows] + both[rows:] + dot(jnp.concatenate(pieces[0], 0), tile[1])
        for order, (gx, gy, dz) in enumerate(entries):
            key = (int(gx < 0), int(gy < 0), int(dz < 0))
            piece = result[16 * order : 16 * order + 16]
            totals[key] = totals[key] + piece if key in totals else piece
    return totals


def unreflect(totals, flips):
    far = None
    for (fx, fy, fz), total in totals.items():
        if (fx, fy, fz) != (0, 0, 0):
            table = flips[2 * fx + fy, :, 256 * fz : 256 * fz + 256]
            both = dot(jnp.concatenate(halves(total), 0), table)
            total = both[:16] + both[16:]
        far = total if far is None else far + total
    return far


def store_leaves(row, flips, flipped):
    edge = jnp.zeros((8, 128), F32)
    groups = {}
    for gy in (-1, 0, 1):
        columns = []
        for h in range(2):
            start = LEAF_ROWS * (gy + 1) + 16 * h
            columns.append(jnp.concatenate([edge, row[start : start + 16, :], edge], 0))
        groups[0, gy] = jnp.concatenate(columns, 1)
    store_reflected(groups, flips, flipped)


LEAF_SHAPE = (3, 3, 2, 2, 2, 32, 128)
LEAF_SPANS = ((8, 16),)


def far_call(kernel, shape, operands, name):
    return pl.pallas_call(
        kernel,
        out_shape=jax.ShapeDtypeStruct(shape, F32),
        in_specs=[VMEM] * len(operands),
        out_specs=VMEM,
        compiler_params=pltpu.CompilerParams(vmem_limit_bytes=8 * MIB),
        cost_estimate=pl.CostEstimate(flops=300_000_000, bytes_accessed=600_000, transcendentals=0),
        name=name,
    )(*operands)


def own_leaves_call(row, flips, block):
    def kernel(row_ref, flips_ref, block_ref, out, basis_out):
        store_leaves(row_ref, flips_ref, out)
        tables = basis_rows()
        for x in range(CX):
            for y in range(CY):
                for j in range(ROWS):
                    places = [part_row(c, x, y) + j for c in range(3)]
                    rows = [block_ref[place : place + 1, :] for place in places]
                    for k, tile in enumerate(basis_tile(*rows, None, tables)):
                        basis_out[x * CY + y, j, 8 * k : 8 * k + 8, :] = tile

    shapes = LEAF_SHAPE, (CX * CY, ROWS, 64, 128)
    return pl.pallas_call(
        kernel,
        out_shape=[jax.ShapeDtypeStruct(shape, F32) for shape in shapes],
        in_specs=[VMEM] * 3,
        out_specs=[VMEM] * 2,
        compiler_params=pltpu.CompilerParams(vmem_limit_bytes=8 * MIB),
        cost_estimate=near_cost(100_000),
        name="own_leaves",
    )(row, flips, block)


def far_own_call(leaves, flips, tiles):
    def kernel(leaves_ref, flips_ref, tiles_ref, out):
        out[...] = unreflect(far_sums((0,), LEAF_SPANS, leaves_ref, flips_ref, (tiles_ref,)), flips_ref)

    return far_call(kernel, (LZ, 256), (leaves, flips, tiles), "far_own")


def far_side(halo, side_is_low, inside, flips, tiles, flipped):
    flip_x = jnp.where(side_is_low, 1, 0)
    edge = jnp.zeros((8, 128), F32)
    for flip_y, steps in ((0, (0, 1)), (1, (-1,))):
        stacked = []
        for gy in steps:
            columns = []
            for h in range(2):
                row = LEAF_ROWS * (gy + 1) + 16 * h
                moments = jnp.where(inside, halo[row : row + 16, :], 0.0)
                columns.append(jnp.concatenate([edge, moments, edge], 0))
            stacked += halves(jnp.concatenate(columns, 1))
        mixed = dot(jnp.concatenate(stacked, 0), flips[2 * flip_x + flip_y])
        for order, gy in enumerate(steps):
            for part, z, half in itertools.product(range(2), range(2), range(2)):
                start, lane = 32 * (2 * order + part), 256 * z + 128 * half
                flipped[2, gy + 1, z, part, half] = mixed[start : start + 32, lane : lane + 128]
    far = None
    for (_, fy, fz), total in far_sums((1,), LEAF_SPANS, flipped, flips, tiles).items():
        table = flips[2 * flip_x + fy][:, 256 * fz : 256 * fz + 256]
        both = dot(jnp.concatenate(halves(total), 0), table)
        far = both[:16] + both[16:] if far is None else far + both[:16] + both[16:]
    return far


def far_partner_call(partner, tables, after):
    def kernel(partner_ref, flips, one, two, after_ref, out, flipped):
        odd = lax.rem(lax.axis_index("gx"), 2) == 1
        out[...] = far_side(partner_ref, odd, odd | ~odd, flips, (one, two), flipped)

    return pl.pallas_call(
        kernel,
        out_shape=jax.ShapeDtypeStruct((LZ, 256), F32),
        in_specs=[VMEM] * 5,
        out_specs=VMEM,
        scratch_shapes=[pltpu.VMEM(LEAF_SHAPE, F32)],
        compiler_params=pltpu.CompilerParams(vmem_limit_bytes=8 * MIB),
        cost_estimate=pl.CostEstimate(flops=300_000_000, bytes_accessed=600_000, transcendentals=0),
        name="far_partner",
    )(partner, *tables, after)


def beyond_kernel(
    before, beyond, targets, flips, one, two, after, out, far_out, wide_ref, charge_ref, flipped
):
    out[...] = before[...]
    beside_x(1, beyond, targets, out, wide_ref, charge_ref)
    index, count = lax.axis_index("gx"), lax.axis_size("gx")
    inside = (index > 0) & (index < count - 1)
    far_out[...] = far_side(beyond, lax.rem(index, 2) == 0, inside, flips, (one, two), flipped)


def beyond_call(operands):
    return pl.pallas_call(
        beyond_kernel,
        out_shape=(jax.ShapeDtypeStruct(NEAR_SHAPE, F32), jax.ShapeDtypeStruct((LZ, 256), F32)),
        in_specs=[VMEM] * len(operands),
        out_specs=(VMEM,) * 2,
        scratch_shapes=near_scratch(8, 10) + [pltpu.VMEM(LEAF_SHAPE, F32)],
        compiler_params=pltpu.CompilerParams(vmem_limit_bytes=12 * MIB),
        cost_estimate=near_cost(2_400_000),
        name="beyond",
    )(*operands)


def upper_kernel(count_x, count_y, refs):
    own_ones, other_ones, small, flips, *tiles, _, out = refs[:8]
    refs = refs[8:]
    level_one, level_two, flipped, sums, local = refs

    index_x, index_y = lax.axis_index("gx"), lax.axis_index("gy")
    pairs_y = count_y // 2

    level_one[...] = jnp.zeros_like(level_one)
    level_two[...] = jnp.zeros_like(level_two)
    half_x = count_x // 2
    lower = index_x < half_x
    for x in range(half_x):
        for pair in range(pairs_y):
            row = 8 * (x * pairs_y + pair)
            one, two = own_ones[row : row + 8, :], other_ones[row : row + 8, :]
            level_one[x + 2, pair + 1] = jnp.where(lower, one, two)
            level_one[x + half_x + 2, pair + 1] = jnp.where(lower, two, one)
    children = jnp.concatenate(
        [
            jnp.concatenate([level_one[2 * x + 2, y + 1], level_one[2 * x + 3, y + 1]], 1)
            for x in range(half_x)
            for y in range(pairs_y)
        ],
        0,
    )
    below = half_x * pairs_y * 8
    low_lanes = lanes((4, 128)) < 64
    sums[0:below, :] = dot_three(children, small[0:256], small[256:512])
    for x in range(half_x):
        for y in range(pairs_y):
            row = (x * pairs_y + y) * 8
            even = sums[pl.ds(row, 4, stride=2), :]
            odd = sums[pl.ds(row + 1, 4, stride=2), :]
            level_two[x + 2, y + 2, 0:4] = jnp.where(low_lanes, even + lane_flip(odd), 0.0)

    def second_group(group_x, group_y):
        return jnp.concatenate(
            [
                level_two[2 * group_x + h + 2, 2 * group_y + 2]
                + lane_flip(level_two[2 * group_x + h + 2, 2 * group_y + 3])
                for h in range(2)
            ],
            1,
        )

    quarter_x, quarter_y = index_x // 4, index_y // 4
    tops = [(x, y) for x in range(count_x // 4) for y in range(count_y // 4)]
    stacked = jnp.concatenate([second_group(x, y) for x, y in tops], 0)
    if stacked.shape[0] % 16 != 0:
        stacked = jnp.concatenate([stacked, jnp.zeros((8, 256), F32)], 0)
    sums[0 : stacked.shape[0], :] = dot_three(stacked, small[0:256], small[256:512])
    top_far = jnp.zeros((16, 128), F32)
    for position, (x, y) in enumerate(tops):
        even = sums[pl.ds(8 * position, 2, stride=2), :]
        odd = sums[pl.ds(8 * position + 1, 2, stride=2), :]
        third = jnp.where(lanes((2, 128)) < 64, even + lane_flip(odd), 0.0)
        third = third[0:1] + lane_flip(third)[1:2]
        step_x, step_y = x - quarter_x + count_x // 4 - 1, y - quarter_y + count_y // 4 - 1
        row = 1536 + 256 * (step_x * (count_y // 4 * 2 - 1) + step_y)
        table = [small[pl.ds(pl.multiple_of(row + 128 * k, 128), 128), :] for k in range(2)]
        top_far = top_far + dot_three(jnp.broadcast_to(third, (16, 128)), table[0], table[1])

    edge = jnp.zeros((8, 256), F32)
    groups = {}
    for gx in (-1, 0, 1):
        for gy in (-1, 0, 1):
            steps = [2 * (index_x // 2 + gx) + h + 2 for h in range(2)]
            first_level = [level_one[step, index_y // 2 + gy + 1] for step in steps]
            second_level = second_group(quarter_x + gx, quarter_y + gy)
            blocks = [edge, jnp.concatenate(first_level, 1), edge, second_level, edge, edge]
            groups[gx, gy] = jnp.concatenate(blocks, 0)
    store_reflected(groups, flips, flipped)
    far = unreflect(far_sums((-1, 0, 1), ((8, 8), (24, 8)), flipped, flips, tiles), flips)

    def select(block, hx, hy):
        tile = jnp.where(hx == 1, block[:, 128:256], block[:, 0:128])
        return jnp.where(hy == 1, lane_flip(tile), tile)

    def refine(parent):
        keep = lanes((16, 128)) < 64
        parent = jnp.where(keep, parent, 0.0)
        high = parent.astype(BF16).astype(F32)
        low = parent - high
        left = jnp.concatenate([high + lane_flip(low), high], 1).astype(BF16)
        down = jnp.concatenate([small[512 + 256 * k : 768 + 256 * k, :] for k in range(4)], 1)
        spread = dot(left, down)
        for half in range(2):
            for h in range(2):
                span = slice(256 * half + 128 * h, 256 * half + 128 * h + 128)
                local[h, pl.ds(half, 16, stride=2), :] = spread[:, span]
        return jnp.concatenate([local[0], local[1]], 1)

    top_local = jnp.where(
        sublanes((16, 128)) == 0, top_far, jnp.where(sublanes((16, 128)) == 1, lane_flip(top_far), 0.0)
    )
    children_far = refine(top_local)
    half_index_x, half_index_y = index_x // 2, index_y // 2
    second = select(children_far[0:8], lax.rem(half_index_x, 2), lax.rem(half_index_y, 2))
    second = second + 0.25 * select(far[8:16], lax.rem(half_index_x, 2), lax.rem(half_index_y, 2))
    zeros = jnp.zeros((8, 128), F32)
    children_far = refine(jnp.concatenate([second, zeros], 0))
    first = select(children_far[0:8], lax.rem(index_x, 2), lax.rem(index_y, 2))
    first = first + 0.5 * select(far[0:8], lax.rem(index_x, 2), lax.rem(index_y, 2))
    out[...] = refine(jnp.concatenate([first, zeros], 0))[0:16]


def upper_call(count_x, count_y, operands):
    half_x, half_y = count_x // 2, count_y // 2
    scratch = [
        pltpu.VMEM((count_x + 4, half_y + 2, 8, 128), F32),
        pltpu.VMEM((half_x + 4, half_y + 4, 8, 128), F32),
        pltpu.VMEM((3, 3, 2, 2, 2, 48, 128), F32),
        pltpu.VMEM((max(16, half_x * half_y * 8), 128), F32),
        pltpu.VMEM((2, 32, 128), F32),
    ]
    return pl.pallas_call(
        lambda *refs: upper_kernel(count_x, count_y, refs),
        out_shape=jax.ShapeDtypeStruct((LZ, 256), F32),
        in_specs=[VMEM] * len(operands),
        out_specs=VMEM,
        scratch_shapes=scratch,
        compiler_params=pltpu.CompilerParams(vmem_limit_bytes=8 * MIB),
        cost_estimate=pl.CostEstimate(flops=900_000_000, bytes_accessed=600_000, transcendentals=0),
        name="upper",
    )(*operands)


def last_kernel(basis, near_rows, local, far_own, far_partner, far_beyond, out):
    leaf = local[...] + far_own[...] + far_partner[...] + far_beyond[...]

    one, two = halves(leaf)
    turned = jnp.concatenate([one.astype(F32), two.astype(F32)], 0).T.astype(BF16)
    table = leaf_segments(2 * LZ)
    for x in range(CX):
        for y in range(CY):
            column = x * CY + y
            spread = dot(turned[64 * column : 64 * column + 64], table)
            for j in range(ROWS):
                span = slice(128 * j, 128 * j + 128)
                total = None
                for k in range(8):
                    term = basis[column, j, 8 * k : 8 * k + 8, :] * spread[8 * k : 8 * k + 8, span]
                    total = term if total is None else total + term
                value = jnp.sum(total, 0, keepdims=True) + near_rows[column, j : j + 1, :]
                out[x, y : y + 1, span] = value


def last_call(operands):
    return pl.pallas_call(
        last_kernel,
        out_shape=jax.ShapeDtypeStruct((CX, CY, LZ * 64), F32),
        in_specs=[VMEM] * len(operands),
        out_specs=VMEM,
        compiler_params=pltpu.CompilerParams(vmem_limit_bytes=8 * MIB),
        name="last",
    )(*operands)


def in_hbm(value):
    return pltpu.with_memory_space_constraint(value, pltpu.HBM)


def swap_bit(value, axis, bit):
    return lax.ppermute(value, axis, [(i, i ^ (1 << bit)) for i in range(lax.axis_size(axis))])


def relay_ring(value, axis):
    count = lax.axis_size(axis)
    steps = {i: i + 2 if i % 2 == 0 else i - 2 for i in range(count)}
    steps[count - 2], steps[1] = count - 1, 0
    return lax.ppermute(value, axis, list(steps.items()))


def solution(mesh):
    count_x, count_y = mesh.shape["gx"], mesh.shape["gy"]
    levels_x, levels_y = count_x.bit_length() - 1, count_y.bit_length() - 1
    tiles = translation_tiles()
    small = small_tables(count_x // 4, count_y // 4)
    tables = small, reflection_tables(), tiles[:TILES_FIRST], tiles[TILES_FIRST:]

    def body(offsets, charges):
        small, flips, *tiles = [in_hbm(jnp.asarray(table)) for table in tables]
        block = moments_call(in_hbm(offsets), in_hbm(charges), small)
        other = swap_bit(block, "gy", 0)
        exchanged = []

        def exchange_y(after):
            pair = block, other
            for level in range(1, levels_y):
                last = level == levels_y - 1
                rows = (ONE_ROWS << (level - 1)) + EDGE_ROWS * (1 if last else 2)
                kernel = functools.partial(group_kernel, level, last)
                sent = pack_call(kernel, rows, (*pair, after), "group")
                pair = sent, swap_bit(sent, "gy", level)
                exchanged.extend(pair)
            return exchanged[0]

        near, targets, small, first_tiles = own_call(block, exchange_y, small, tiles[0])
        row, far = row_call(levels_y, (block, other, *exchanged, near))
        partner = swap_bit(row, "gx", 0)
        partner_far = swap_bit(far, "gx", 0)
        near, flips, other_tiles = beside_y_call(row, far, targets, near, (flips, tiles[1]))
        leaves, basis = own_leaves_call(row, flips, block)
        far_own = far_own_call(leaves, flips, first_tiles)
        rows = ONE_ROWS << (levels_y - 1)
        ones = merge_call(0, row, partner, ROW_ROWS, rows, SENT_ROWS, far_own)
        other_ones = swap_bit(ones, "gx", 1)
        beyond = relay_ring(relay_call(partner, partner_far, ones), "gx")
        far_tables = flips, first_tiles, other_tiles
        far_partner = far_partner_call(partner, far_tables, ones)
        near = near_call(beside_x_kernel, (partner, targets, near, far_partner), 8, 10, 1_200_000, "near_x")
        for bit in range(1, levels_x - 1):
            ones = merge_call(bit, ones, other_ones, 0, rows << bit, 0, near)
            other_ones = swap_bit(ones, "gx", bit + 1)
        near, far_beyond = beyond_call((near, beyond, targets, *far_tables, ones))
        local = upper_call(count_x, count_y, (ones, other_ones, small, *far_tables, near))
        return last_call((basis, near, local, far_own, far_partner, far_beyond))

    in_specs = (P(None, "gx", "gy", None), P("gx", "gy", None))
    out_specs = P("gx", "gy", None)
    return jax.shard_map(body, mesh=mesh, in_specs=in_specs, out_specs=out_specs, check_vma=False)
```
